512 devices in a mesh: group: 8 (over y), dev: 64 (over x, z, core).
Axes of the slice: x: 4, y: 8, z: 8, core: 2. Of those that a mesh axis runs over, the one named last changes fastest.
Arguments:
- displacement: float32 [3, 131072], P(None, ('group', 'dev')), may hold values from -6 to 6
- connectivity: int32 [8, 32768], P(None, ('group', 'dev')), may hold values from 0 to 1279, as said below
- face_nodes: int32 [512, 64, 16], P(('group', 'dev')), may hold values from 0 to 255, as said below
- strain_map: float32 [6, 24, 32768], P(None, None, ('group', 'dev')), may hold values from -1.25 to 1.25
- assignment: int32 [32768], P(('group', 'dev')), may hold values from -1 to 1023, as said below
- phases: int32 [8, 64, 3072], P('group', None, 'dev'), may hold values 0 or 1
- load_map: float32 [6, 64, 3072], P(None, None, 'dev'), may hold values from -0.013671875 to 0.013671875
- stiff_root: float32 [64, 64], replicated, may hold values from -0.75 to 0.75
- chain_map: float32 [64, 64], replicated, may hold values from -0.75 to 0.75
- bridge_map: float32 [16, 16], replicated, may hold values from -1.5 to 1.5
- elastic: float32 [6, 6], replicated, may hold values from -2.5 to 2.5
Outputs:
- stress: float32 [6, 32768], P(None, ('group', 'dev'))
- fluctuation: float32 [8, 64, 3072, 128], P('group', None, 'dev')
The draws below stay inside these ranges and needn't reach their ends.
Inputs may be any that keep to these rules, and one draw needn't show every extreme that they name: `connectivity`: an entry below 256 names an own node; 256 + p * 16 + j names slot j from partner p. Each partition has exactly 6 partners in its section, each with 1 to 16 live slots (its first partner exactly 16); only live slots are named and every live slot is named. `face_nodes`: slots that the receiver does not name hold arbitrary own nodes. `assignment`: each value 0 to 1023 appears exactly once; all others are -1. At most 8 non-negative entries lie on one partition, reached in every section. Among the Gauss points of one section at most 32 values lie in [h * 128, (h + 1) * 128) for any h, reached in every draw.
All inputs are finite; a program needn't handle non-finite values. No bound on the sum of `phases` on one device may be relied on, other than what follows from the above.
Results may differ from the reference program's by a relative error of at most 0.00022.
Values sent between devices are 32-bit elements; how exact they have to be, the bound alone decides.
No kernel may reach another device: no remote copies, remote signals or barrier semaphores. Data moves between devices by JAX's collectives and lax.ppermute only.
A program may use at most 128 MiB of HBM per device.

```python
import math
from functools import partial
import jax
import jax.numpy as jnp
from jax import lax

BLOCK = 64
IFACE = 16
BLOCKS = 48
POINTS = 128
GP_DEV = 64
NODE_DEV = 256
FACE_CAP = 16
NEIGHBOURS = 6
PLASTIC_CAP = 8
ITERS = 4
GP_TOTAL = 32768
NODES = 131072
N_GROUP = 8
N_DEV = 64
DEVICES = 512


def face_counts(key):
    key = jax.random.fold_in(key, 5)
    row_keys = jax.random.split(key, DEVICES)

    def one_row(row_key, device):
        first, second = jax.random.split(row_key)
        offsets = jax.random.permutation(first, N_DEV - 1)[:NEIGHBOURS] + 1
        peers = (device % N_DEV + offsets) % N_DEV
        amounts = jax.random.randint(second, (NEIGHBOURS,), 1, FACE_CAP + 1)
        amounts = amounts.at[0].set(FACE_CAP)
        return jnp.zeros((N_DEV,), jnp.int32).at[peers].set(amounts.astype(jnp.int32))
    return jax.vmap(one_row)(row_keys, jnp.arange(DEVICES, dtype=jnp.int32))


def draw_connectivity(key, part):
    counts = face_counts(key)
    key = jax.random.fold_in(key, 11)
    row_keys = jax.random.split(key, DEVICES)
    slots = N_DEV * FACE_CAP
    refs_count = 8 * GP_DEV

    def one_row(row_key, live_counts):
        first, second = jax.random.split(row_key)
        slot_ids = jnp.arange(slots, dtype=jnp.int32)
        live = slot_ids % FACE_CAP < live_counts[slot_ids // FACE_CAP]
        order = jnp.argsort(jnp.where(live, 0, 1), stable=True).astype(jnp.int32)
        total = jnp.sum(live.astype(jnp.int32))
        turn = jnp.arange(refs_count, dtype=jnp.int32)
        ghost = NODE_DEV + order[jnp.minimum(turn, slots - 1)]
        local = jax.random.randint(first, (refs_count,), 0, NODE_DEV)
        refs = jnp.where(turn < total, ghost, local)
        refs = jax.random.permutation(second, refs)
        return refs.reshape(8, GP_DEV)
    table = jax.vmap(one_row)(row_keys, counts)
    return jnp.transpose(table, (1, 0, 2)).reshape(8, DEVICES * GP_DEV).astype(jnp.int32)


def draw_face_nodes(key, part):
    key = jax.random.fold_in(key, 13)
    return jax.random.randint(key, (DEVICES, N_DEV, FACE_CAP), 0, NODE_DEV).astype(jnp.int32)


def draw_assignment(key, part):
    key = jax.random.fold_in(key, 17)
    key_turn, key_slots, key_place = jax.random.split(key, 3)
    base = POINTS // N_GROUP
    shares = jnp.full((N_GROUP,), base, jnp.int32).at[0].set(2 * base).at[1].set(0)
    turn = jax.random.randint(key_turn, (), 0, N_GROUP)
    grid = jnp.arange(N_GROUP, dtype=jnp.int32)
    counts = shares[(grid[:, None] - grid[None, :] + turn) % N_GROUP]
    bounds = jnp.cumsum(counts, axis=0)
    position = jnp.arange(POINTS, dtype=jnp.int32)
    section_of = jnp.sum((position[None, None, :] >= bounds[:, :, None]).astype(jnp.int32), axis=0)
    slot_perm = jax.vmap(lambda k: jax.random.permutation(k, POINTS))(jax.random.split(key_slots, N_GROUP))
    ids = grid[:, None] * POINTS + slot_perm
    order = jnp.argsort(section_of.reshape(-1), stable=True)
    ranked = ids.reshape(-1)[order].reshape(N_GROUP, POINTS)

    def one_section(section_key, section, targets):
        key_full, key_rank, key_point = jax.random.split(section_key, 3)
        full = jax.random.randint(key_full, (), 0, N_DEV)
        spots = N_DEV * PLASTIC_CAP
        spot = jnp.arange(spots, dtype=jnp.int32)
        rank_value = jax.random.permutation(key_rank, spots)
        priority = jnp.where(spot // PLASTIC_CAP == full, -1, rank_value)
        chosen = jnp.argsort(priority, stable=True)[:POINTS]
        device = chosen // PLASTIC_CAP
        within = chosen % PLASTIC_CAP
        point_perm = jax.vmap(lambda k: jax.random.permutation(k, GP_DEV))(jax.random.split(key_point, N_DEV))
        point = point_perm[device, within]
        return ((section * N_DEV + device) * GP_DEV + point, targets)
    where_to, values = jax.vmap(one_section)(jax.random.split(key_place, N_GROUP), grid, ranked)
    result = jnp.full((DEVICES * GP_DEV,), -1, jnp.int32)
    return result.at[where_to.reshape(-1).astype(jnp.int32)].set(values.reshape(-1).astype(jnp.int32))


def touch_ends(drawn, stream_key, smallest, top_value):
    index_at = [jax.random.randint(jax.random.fold_in(stream_key, axis), (), 0, length) for axis, length in enumerate(drawn.shape)]
    longest = drawn.shape.index(max(drawn.shape))
    next_to = index_at[:longest] + [(index_at[longest] + 1) % drawn.shape[longest]] + index_at[longest + 1:]
    return drawn.at[tuple(index_at)].set(smallest).at[tuple(next_to)].set(top_value)


def steps_of(key, shape, cuts, smallest, top_value):
    def one(dim, blocks):
        draws = jax.random.uniform(jax.random.fold_in(jax.random.fold_in(key, 6), dim), (blocks,), jnp.float32, smallest / len(cuts), top_value / len(cuts))
        return jnp.repeat(jnp.exp(draws), shape[dim] // blocks).reshape((-1,) + (1,) * (len(shape) - dim - 1))

    level = one(*cuts[0])
    for cut in cuts[1:]:
        level = level * one(*cut)
    return level


def normal_values(own_key, dims, spread, most, pieces=(), kind=jnp.bfloat16):
    gain = steps_of(own_key, dims, pieces, -0.22, 0.18) if pieces else 1.0
    array = jax.random.normal(own_key, dims, jnp.float32) * spread * gain
    return jnp.minimum(jnp.maximum(array, -most), most).astype(kind)


def setup_inputs(seed: int = 0) -> dict:
    key_list = jax.random.split(jax.random.key(seed), 12)
    displacement = normal_values(key_list[0], (3, NODES), 1.0, 6.0, ((1, 512),), jnp.float32)
    connectivity = draw_connectivity(jax.random.fold_in(key_list[11], 71), 0)
    face_nodes = draw_face_nodes(jax.random.fold_in(key_list[11], 71), 0)
    strain_map = normal_values(key_list[3], (6, 24, GP_TOTAL), 24 ** -0.5, 1.25, ((2, 512),), jnp.float32)
    assignment = draw_assignment(jax.random.fold_in(key_list[11], 71), 0)
    phases = touch_ends((jax.random.randint(key_list[5], (N_GROUP, BLOCK, N_DEV * BLOCKS), 0, 3) < 1).astype(jnp.int32), jax.random.fold_in(key_list[5], 1), 0, 1)
    load_map = normal_values(key_list[6], (6, BLOCK, N_DEV * BLOCKS), (BLOCK * N_DEV * BLOCKS) ** -0.5, 0.013671875, ((2, 64),), jnp.float32)
    stiff_root = normal_values(key_list[7], (BLOCK, BLOCK), BLOCK ** -0.5, 0.75, (), jnp.float32)
    chain_map = normal_values(key_list[8], (BLOCK, BLOCK), BLOCK ** -0.5, 0.75, (), jnp.float32)
    bridge_map = normal_values(key_list[9], (IFACE, IFACE), IFACE ** -0.5, 1.5, (), jnp.float32)
    elastic = normal_values(key_list[10], (6, 6), 6 ** -0.5, 2.5, (), jnp.float32)
    return dict(displacement=displacement, connectivity=connectivity, face_nodes=face_nodes, strain_map=strain_map, assignment=assignment, phases=phases, load_map=load_map, stiff_root=stiff_root, chain_map=chain_map, bridge_map=bridge_map, elastic=elastic)


ridge = 0.5

def operate(field, weights, stiff_root, chain_map, bridge_map):
    hp = lax.Precision.HIGHEST
    lifted = jnp.einsum('ij,jdks->idks', stiff_root, field, precision=hp)
    core = jnp.einsum('ji,jdks->idks', stiff_root, weights[..., None] * lifted, precision=hp)
    edge = field - jnp.einsum('ij,jdks->idks', chain_map, jnp.roll(field, -1, axis=2), precision=hp)
    behind = jnp.einsum('ji,jdks->idks', chain_map, edge, precision=hp)
    result = ridge * field + core + edge - jnp.roll(behind, 1, axis=2)
    top = BLOCK - IFACE
    face = field[top:] - jnp.einsum('ij,jdks->idks', bridge_map, jnp.roll(field[:IFACE], -1, axis=1), precision=hp)
    below = jnp.roll(field[top:], 1, axis=1) - jnp.einsum('ij,jdks->idks', bridge_map, field[:IFACE], precision=hp)
    pull = jnp.einsum('ji,jdks->idks', bridge_map, below, precision=hp)
    return jnp.concatenate([result[:IFACE] - pull, result[IFACE:top], result[top:] + face], axis=0)

def krylov(rhs, apply_fn):
    solution = jnp.zeros_like(rhs)
    residual = rhs
    direction = rhs
    norm_now = lax.optimization_barrier(jnp.sum(residual * residual, axis=(0, 1, 2)))
    for step in range(ITERS):
        image = apply_fn(direction)
        alpha = norm_now / lax.optimization_barrier(jnp.sum(direction * image, axis=(0, 1, 2)))
        solution = solution + alpha[None, None, None, :] * direction
        residual = residual - alpha[None, None, None, :] * image
        if step + 1 < ITERS:
            norm_next = lax.optimization_barrier(jnp.sum(residual * residual, axis=(0, 1, 2)))
            direction = residual + (norm_next / norm_now)[None, None, None, :] * direction
            norm_now = norm_next
    return solution

def reference(displacement, connectivity, face_nodes, strain_map, assignment, phases, load_map, stiff_root, chain_map, bridge_map, elastic):
    hp = lax.Precision.HIGHEST
    owners = jnp.arange(DEVICES, dtype=jnp.int32)
    flat_index = owners[:, None, None] * NODE_DEV + face_nodes
    sent = displacement[:, flat_index].reshape(3, N_GROUP, N_DEV, N_DEV, FACE_CAP)
    ghost = jnp.transpose(sent, (0, 1, 3, 2, 4)).reshape(3, DEVICES, N_DEV * FACE_CAP)
    local = displacement.reshape(3, DEVICES, NODE_DEV)
    table = jnp.concatenate([local, ghost], axis=2)
    width = NODE_DEV + N_DEV * FACE_CAP
    refs = connectivity.reshape(8, DEVICES, GP_DEV) + (owners * width)[None, :, None]
    nodal = table.reshape(3, DEVICES * width)[:, refs]
    nodal = jnp.transpose(nodal, (1, 0, 2, 3)).reshape(24, GP_TOTAL)
    strain = lax.optimization_barrier(jnp.sum(strain_map * nodal[None], axis=1))
    plastic = assignment >= 0
    slots = jnp.where(plastic, assignment, N_GROUP * POINTS).astype(jnp.int32)
    point_strain = jnp.zeros((6, N_GROUP * POINTS + 1), jnp.float32).at[:, slots].set(strain)
    point_strain = point_strain[:, :N_GROUP * POINTS].reshape(6, N_GROUP, POINTS)
    load_four = load_map.reshape(6, BLOCK, N_DEV, BLOCKS)
    scale_out = math.sqrt(BLOCK * N_DEV * BLOCKS)

    def solve_group(inputs):
        labels, group_strain = inputs
        weights = (1.0 + 2.0 * labels.astype(jnp.float32)).reshape(BLOCK, N_DEV, BLOCKS)
        rhs = jnp.einsum('cidk,cs->idks', load_four, group_strain, precision=hp)
        apply_fn = partial(operate, weights=weights, stiff_root=stiff_root, chain_map=chain_map, bridge_map=bridge_map)
        solution = krylov(rhs, apply_fn)
        group_stress = jnp.dot(elastic, group_strain, precision=hp) + jnp.einsum('cidk,idks->cs', load_four, solution, precision=hp)
        return (group_stress, scale_out * solution.reshape(BLOCK, N_DEV * BLOCKS, POINTS))
    point_stress, fluctuation = lax.map(solve_group, (phases, jnp.transpose(point_strain, (1, 0, 2))))
    flat_stress = jnp.transpose(point_stress, (1, 0, 2)).reshape(6, N_GROUP * POINTS)
    rve_stress = flat_stress[:, jnp.where(plastic, assignment, 0).astype(jnp.int32)]
    stress = jnp.where(plastic[None], rve_stress, jnp.dot(elastic, strain, precision=hp))
    return (stress, fluctuation)
```

```python
import math

import jax
import jax.numpy as jnp
from jax import lax
from jax.experimental import pallas as pl
from jax.experimental.pallas import tpu as pltpu
from jax.sharding import PartitionSpec as P

BLOCK = 64
IFACE = 16
BLOCKS = 48
POINTS = 128
PLASTIC_CAP = 8
HALF = BLOCKS // 2
ROWS = HALF * 8
LANES = 128

ridge = 0.5
F32 = jnp.float32
BF16 = jnp.bfloat16
HIGHEST = lax.Precision.HIGHEST


def iota(shape, dim):
    return lax.broadcasted_iota(jnp.int32, shape, dim)


def dot(a, b):
    return jnp.dot(a, b, precision=HIGHEST, preferred_element_type=F32)


def dot_nt(a, b):
    return lax.dot_general(
        a, b, (((1,), (1,)), ((), ())), precision=HIGHEST, preferred_element_type=F32
    )


def dot_tn(a, b):
    return lax.dot_general(
        a, b, (((0,), (0,)), ((), ())), precision=HIGHEST, preferred_element_type=F32
    )


def bdot(a, b):
    return jnp.dot(a, b, preferred_element_type=F32)


def bdot_nt(a, b):
    return lax.dot_general(a, b, (((1,), (1,)), ((), ())), preferred_element_type=F32)


def split2(x):
    high = x.astype(BF16)
    return high, (x - high.astype(F32)).astype(BF16)


def split3(x):
    high = x.astype(BF16).astype(F32)
    rest = x - high
    middle = rest.astype(BF16).astype(F32)
    return high, middle, rest - middle


def spread_rows(values):
    n = values.shape[1]
    rows = []
    for part in split3(values):
        for c in range(3):
            rows.append(jnp.broadcast_to(part[c : c + 1], (16, n)))
        rows.append(jnp.zeros((16, n), F32))
    return jnp.concatenate(rows, axis=0)


def pack_kernel(load_ref, phase_ref, out_ref, even):
    for c in range(8):
        if c < 6:
            value = load_ref[c]
        elif c == 6:
            value = 1.0 + 2.0 * phase_ref[0].astype(F32)
        else:
            out_ref[pl.ds(c, HALF, stride=8), :] = jnp.zeros((HALF, LANES), F32)
            continue
        padded = jnp.concatenate([value, jnp.zeros((BLOCK, LANES - BLOCKS), F32)], axis=1)
        turned = jnp.transpose(jnp.concatenate([padded, padded], axis=0))
        even[...] = turned
        first = even[pl.ds(0, HALF, stride=2), :]
        second = even[pl.ds(1, HALF, stride=2), :]
        out_ref[pl.ds(c, HALF, stride=8), :] = jnp.where(
            iota((HALF, LANES), 1) < BLOCK, first, second
        )


def face_kernel(disp_ref, face_ref, out_ref):
    devs = face_ref.shape[1]
    nodes = disp_ref.shape[1]
    faces = face_ref[0]
    spread = spread_rows(disp_ref[...])
    spread = jnp.concatenate([spread, jnp.zeros((64, nodes), F32)], axis=0).astype(BF16)
    place = iota((devs, nodes), 1)
    hot = jnp.concatenate(
        [jnp.where(faces[:, j : j + 1] == place, 1.0, 0.0) for j in range(16)], axis=0
    ).astype(BF16)
    found = bdot_nt(hot, spread)
    lane = iota((devs, 256), 1) % 16
    total = jnp.zeros((devs, 256), F32)
    for j in range(16):
        total = total + jnp.where(lane == j, found[j * devs : (j + 1) * devs], 0.0)
    near = total[:, :LANES]
    out_ref[:, 0, :] = (near + pltpu.roll(near, 64, 1)) + total[:, LANES:]


def weight_kernel(root_ref, chain_ref, bridge_ref, w1h, w1l, wbh, wbl, w2h, w2l, basis_ref):
    root, chain, bridge = root_ref[...], chain_ref[...], bridge_ref[...]

    zero = jnp.zeros((BLOCK, BLOCK), F32)

    def straight(m):
        return jnp.concatenate(
            [jnp.concatenate([m, zero], axis=1), jnp.concatenate([zero, m], axis=1)], axis=0
        )

    def crossed(m):
        return jnp.concatenate(
            [jnp.concatenate([zero, m], axis=1), jnp.concatenate([m, zero], axis=1)], axis=0
        )

    gap = BLOCK - IFACE
    wide = jnp.concatenate([bridge, jnp.zeros((IFACE, gap), F32)], axis=1)
    upper = jnp.concatenate([jnp.zeros((gap, BLOCK), F32), wide], axis=0)
    eye = jnp.where(iota((BLOCK, BLOCK), 0) == iota((BLOCK, BLOCK), 1), 1.0, 0.0)
    root_t = dot_nt(eye, root)
    chain_t = dot_nt(eye, chain)
    lower = dot_nt(eye, upper)
    first = jnp.concatenate([straight(root_t), crossed(chain_t)], axis=1)
    w1h[...], w1l[...] = split2(first)
    wbh[...], wbl[...] = split2(straight(lower))
    second = jnp.concatenate([straight(root), -crossed(chain), -straight(upper)], axis=0)
    w2h[...], w2l[...] = split2(second)

    size = 2 * BLOCK
    diagonal = iota((size, size), 0) == iota((size, size), 1)
    edge = jnp.where(diagonal, 1.0, 0.0) - crossed(chain)
    face = straight(jnp.where(iota((BLOCK, BLOCK), 0) >= gap, eye, 0.0) - upper)
    model = 2.0 * dot_tn(straight(root), straight(root)) + dot_tn(edge, edge) + dot_tn(face, face)
    model = model + jnp.where(diagonal, ridge, 0.0)

    def inner(p, q):
        return jnp.sum(jnp.sum(p * q, axis=1, keepdims=True), axis=0, keepdims=True)

    now = jnp.where(diagonal, size**-0.5, 0.0)
    past, image = None, size**-0.5 * model
    centres, steps = [], []
    for n in range(3):
        if n:
            image = dot(model, now)
        centre = inner(now, image)
        rest = image - centre * now
        if n:
            rest = rest - steps[-1] * past
        step = jnp.maximum(jnp.sqrt(inner(rest, rest)), 0.01 * centres[0] if n else 0.01 * centre)
        centres.append(centre)
        steps.append(step)
        past, now = now, rest / step
    row = iota((8, LANES), 0)
    table = jnp.zeros((8, LANES), F32)
    for n, value in enumerate(centres + steps):
        table = jnp.where(row == n, value, table)
    basis_ref[...] = table


def krylov_kernel(
    own_ref, m1_ref, m2_ref, p1_ref, p2_ref, w1h, w1l, wbh, wbl, w2h, w2l, basis_ref, u_ref, gram_ref
):
    centre = [basis_ref[n : n + 1, :] for n in range(3)]
    step = [basis_ref[n + 3 : n + 4, :] for n in range(3)]
    inverse = [1.0 / v for v in step]
    lane = iota((ROWS, LANES), 1)
    early = lane < BLOCK
    top = (lane % BLOCK) >= BLOCK - IFACE

    def weights_of(x):
        w = x.reshape(HALF, 8, LANES)[:, 6:7, :]
        return jnp.broadcast_to(w, (HALF, 8, LANES)).reshape(ROWS, LANES)

    def stage(x, high, low):
        xh, xl = split2(x)
        return bdot(xh, high) + (bdot(xl, high) + bdot(xh, low))

    def up(x):
        return jnp.concatenate([x[8:], x[:8]], axis=0)

    def down(x):
        return jnp.concatenate([x[ROWS - 8 :], x[: ROWS - 8]], axis=0)

    def halves(x, w):
        both = stage(x, w1h[...], w1l[...])
        lifted = both[:, :LANES]
        mixed = both[:, LANES:]
        edge = x - jnp.where(early, mixed, up(mixed))
        return lifted, w * lifted, edge

    def bridged(x):
        return stage(x, wbh[...], wbl[...])

    def face(x, following):
        return jnp.where(top, x, 0.0) - following

    def apply(x, w, f, f_before):
        _, weighted, edge = halves(x, w)
        shifted = jnp.where(early, edge, down(edge))
        left = jnp.concatenate([weighted, shifted, f_before], axis=1)
        return ridge * x + edge + f + stage(left, w2h[...], w2l[...])

    x0 = [m1_ref[...], own_ref[...], p1_ref[...], p2_ref[...]]
    w = [weights_of(x) for x in x0]
    zero = jnp.zeros((ROWS, LANES), F32)

    b0 = [bridged(x) for x in x0]
    f0 = [face(m2_ref[...], b0[0])] + [face(x0[p], b0[p + 1]) for p in range(3)] + [zero]
    x1 = []
    for p in range(4):
        image = apply(x0[p], w[p], f0[p + 1], f0[p])
        x1.append(inverse[0] * (image - centre[0] * x0[p]))

    b1 = [None] + [bridged(x1[p]) for p in range(1, 4)]
    f1 = [zero] + [face(x1[p], b1[p + 1]) for p in range(3)]
    x2 = []
    for p in range(3):
        image = apply(x1[p], w[p], f1[p + 1], f1[p])
        x2.append(inverse[1] * (image - centre[1] * x1[p] - step[0] * x0[p]))

    b2 = [None] + [bridged(x2[p]) for p in range(1, 3)]
    f2 = [face(x2[p], b2[p + 1]) for p in range(2)] + [zero]
    x3 = [None]
    for p in range(1, 3):
        image = apply(x2[p], w[p], f2[p], f2[p - 1])
        x3.append(inverse[2] * (image - centre[2] * x2[p] - step[1] * x1[p]))

    lifted, weighted, edge = halves(x3[1], w[1])
    f3 = face(x3[1], bridged(x3[2]))

    basis = [x0[1], x1[1], x2[1], x3[1]]
    for n in range(4):
        u_ref[n] = basis[n]

    def long(x):
        return jnp.concatenate([x[8 * k : 8 * k + 8] for k in range(HALF)], axis=1)

    tall = jnp.concatenate([long(x) for x in basis + [lifted, weighted, edge, f3]], axis=0)
    high = tall.astype(BF16).astype(F32)
    both = jnp.concatenate([high, tall - high], axis=0).astype(BF16)
    product = bdot_nt(both, both)
    product = product[:64] + product[64:]
    product = product + pltpu.roll(product, 64, 1)

    def pair(a, b, to):
        return pltpu.roll(product[8 * a : 8 * a + 8], (8 * (to - b)) % LANES, 1)

    at = iota((8, LANES), 1) // 8
    energy = 0.5 * pair(3, 3, 7) + (pair(4, 5, 7) + pair(6, 6, 7) + pair(7, 7, 7))
    moments = jnp.where(at < 4, product[:8], 0.0)
    moments = jnp.where(at == 4, pair(2, 2, 4), moments)
    moments = jnp.where(at == 5, pair(2, 3, 5), moments)
    moments = jnp.where(at == 6, pair(3, 3, 6), moments)
    moments = jnp.where(at == 7, energy, moments)
    for t in range(3):
        gram_ref[:, t * LANES : (t + 1) * LANES] = moments[2 * t : 2 * t + 1] + pltpu.roll(
            moments[2 * t + 1 : 2 * t + 2], 64, 1
        )


def turn_kernel(u_ref, out_ref, wide):
    for k in range(HALF):
        rows = jnp.concatenate([u_ref[n, 8 * k : 8 * k + 8, :] for n in range(4)], axis=0)
        high = rows.astype(BF16).astype(F32)
        stack = jnp.concatenate([high, rows - high, high, jnp.zeros_like(high)], axis=0)
        turned = jnp.transpose(stack)
        wide[pl.ds(2 * k, BLOCK, stride=BLOCKS), :] = turned[:BLOCK]
        wide[pl.ds(2 * k + 1, BLOCK, stride=BLOCKS), :] = turned[BLOCK:]
    out_ref[...] = wide[...].astype(BF16)


def strain_kernel(
    disp_ref, arrived_ref, conn_ref, map_ref, assign_ref, gram_ref, send_ref, strain_ref
):
    devs = arrived_ref.shape[0]
    nodes = disp_ref.shape[1]
    points = conn_ref.shape[1]
    conn = conn_ref[...]
    index = jnp.concatenate([conn[a : a + 1] for a in range(8)], axis=1)
    refs = 8 * points
    own = jnp.where(iota((nodes, refs), 0) == index, 1.0, 0.0).astype(BF16)
    partner = (index - nodes) >> 4
    other = jnp.where(iota((devs, refs), 0) == partner, 1.0, 0.0).astype(BF16)
    ghost = jnp.transpose(arrived_ref[:, 0, :])[:64]
    ghost = jnp.concatenate(split3(ghost), axis=0).astype(BF16)
    table = spread_rows(disp_ref[...]).astype(BF16)
    found = bdot(table, own) + bdot(ghost, other)
    found = (found[:64] + found[64:128]) + found[128:]
    found = jnp.where(iota((64, refs), 0) % 16 == index % 16, found, 0.0)
    sums = [jnp.sum(found[16 * c : 16 * c + 16], axis=0, keepdims=True) for c in range(3)]
    nodal = jnp.concatenate(
        [sums[c][:, a * points : (a + 1) * points] for a in range(8) for c in range(3)], axis=0
    )
    strain = jnp.concatenate(
        [jnp.sum(map_ref[c] * nodal, axis=0, keepdims=True) for c in range(6)], axis=0
    )
    strain_ref[...] = jnp.concatenate([strain, jnp.zeros((2, points), F32)], axis=0)

    assign = assign_ref[...]
    plastic = assign >= 0
    flags = jnp.where(plastic, 1.0, 0.0)
    before = jnp.where(iota((points, points), 0) < iota((points, points), 1), 1.0, 0.0)
    rank = bdot(jnp.broadcast_to(flags, (8, points)).astype(BF16), before.astype(BF16))
    pick = jnp.where(plastic & (rank == iota((8, points), 0).astype(F32)), 1.0, 0.0)
    values = jnp.concatenate(
        [
            strain,
            (assign + 1).astype(F32),
            jnp.zeros((LANES - 7, points), F32),
        ],
        axis=0,
    )
    chosen = dot_nt(pick, values)
    line = chosen[0:1]
    for slot in range(1, PLASTIC_CAP):
        line = line + pltpu.roll(chosen[slot : slot + 1], 8 * slot, 1)
    line = jnp.concatenate([gram_ref[...], line], axis=1)
    send_ref[:, 0, :] = jnp.broadcast_to(line, (devs, 4 * LANES))


def section_kernel(arrived_ref, send_ref, own_ref):
    devs = arrived_ref.shape[0]
    groups = send_ref.shape[0]
    arrived = arrived_ref[:, 0, :]
    total = jnp.sum(arrived[:, : 3 * LANES], axis=0, keepdims=True)
    low = iota((1, LANES), 1) < 64
    rows = []
    for t in range(3):
        tile = total[:, t * LANES : (t + 1) * LANES]
        rows.append(jnp.where(low, tile, 0.0))
        rows.append(jnp.where(low, pltpu.roll(tile, 64, 1), 0.0))
    rows.append(jnp.zeros((2, LANES), F32))
    moments = jnp.concatenate(rows, axis=0)
    own_ref[...] = moments

    cand = arrived[:, 3 * LANES :]
    entry = iota((LANES, 4 * LANES), 1)
    copies = jnp.where(
        iota((LANES, 4 * LANES), 0) == (entry // 64) * 8 + entry % 8, 1.0, 0.0
    )
    tiled = dot(cand, copies)
    spot = iota((devs, LANES), 1)
    column = iota((devs, 64), 1)
    left, right = [], []
    for slot in range(PLASTIC_CAP):
        target = cand[:, 8 * slot + 6 : 8 * slot + 7].astype(jnp.int32) - 1
        right.append(jnp.where((target & (POINTS - 1)) == spot, 1.0, 0.0))
        keep = ((target >> 7) == column // 8) & (column % 8 < 6)
        left.append(jnp.where(keep, tiled[:, 64 * slot : 64 * slot + 64], 0.0))
    dense = dot_tn(jnp.concatenate(left, axis=0), jnp.concatenate(right, axis=0))
    for h in range(groups):
        send_ref[h, 0:8, :] = dense[8 * h : 8 * h + 8]
        send_ref[h, 8:16, :] = moments


def coefficients(m, centre, step):
    m00, m01, m02, m03, m22, m23, m33, energy = m
    m11 = m00 + (step[1] * m02 + (centre[1] - centre[0]) * m01) / step[0]
    m12 = (step[2] * m03 + (centre[2] - centre[0]) * m02 + step[1] * m01) / step[0]
    m13 = (step[1] * (m22 - m11) + (centre[1] - centre[2]) * m12 + step[0] * m02) / step[2]
    products = [
        [m00, m01, m02, m03],
        [m01, m11, m12, m13],
        [m02, m12, m22, m23],
        [m03, m13, m23, m33],
    ]

    def gram(a, b):
        return products[a][b]

    def image(a, b):
        a, b = max(a, b), min(a, b)
        if b == 3:
            return energy
        value = step[b] * products[a][b + 1] + centre[b] * products[a][b]
        return value + step[b - 1] * products[a][b - 1] if b else value

    def inner(p, form):
        total = None
        for a in range(len(p)):
            for b in range(a, len(p)):
                term = p[a] * p[b] * form(a, b)
                if a != b:
                    term = 2.0 * term
                total = term if total is None else total + term
        return total

    def times(p):
        out = [jnp.zeros_like(p[0]) for _ in range(len(p) + 1)]
        for b, v in enumerate(p):
            out[b + 1] = out[b + 1] + step[b] * v
            out[b] = out[b] + centre[b] * v
            if b:
                out[b - 1] = out[b - 1] + step[b - 1] * v
        return out

    one = jnp.ones_like(m00)
    answer = []
    residual = [one]
    direction = [one]
    norm = m00
    for turn in range(4):
        alpha = norm / inner(direction, image)
        answer = answer + [jnp.zeros_like(one)]
        answer = [x + alpha * p for x, p in zip(answer, direction)]
        if turn < 3:
            stepped = times(direction)
            residual = residual + [jnp.zeros_like(one)]
            residual = [r - alpha * v for r, v in zip(residual, stepped)]
            later = inner(residual, gram)
            beta = later / norm
            direction = direction + [jnp.zeros_like(one)]
            direction = [r + beta * p for r, p in zip(residual, direction)]
            norm = later
    return answer


def final_kernel(
    scale, arrived_ref, own_ref, strain_ref, assign_ref, elastic_ref, basis_ref, u_ref, stress_ref, out_ref
):
    groups = arrived_ref.shape[0]
    points = strain_ref.shape[1]
    centre = [basis_ref[n : n + 1, :] for n in range(3)]
    step = [basis_ref[n + 3 : n + 4, :] for n in range(3)]
    field = arrived_ref[0, 0:8, :]
    for h in range(1, groups):
        field = field + arrived_ref[h, 0:8, :]
    diagonal = (iota((64, LANES), 0) // 8) == (iota((64, LANES), 1) // 8)

    def tall(x):
        return jnp.concatenate([x] * 8, axis=0)

    def opened(moments):
        return jnp.where(diagonal, tall(moments), 0.0)[:, :64]

    strain = strain_ref[...]
    padded = jnp.concatenate([strain, jnp.zeros((8, LANES - points), F32)], axis=1)
    assign = jnp.concatenate(
        [assign_ref[...], jnp.full((1, LANES - points), -1, jnp.int32)], axis=1
    )
    forces = dot(opened(own_ref[...]), tall(field))
    every = jnp.concatenate([opened(arrived_ref[h, 8:16, :]) for h in range(groups)], axis=0)
    products = dot(every, tall(padded))
    group_of = assign >> 7
    local = jnp.zeros((64, LANES), F32)
    for h in range(groups):
        local = local + jnp.where(group_of == h, products[64 * h : 64 * h + 64], 0.0)

    m = []
    for n in range(8):
        first = jnp.sum(forces[8 * n : 8 * n + 8] * field, axis=0, keepdims=True)
        second = jnp.sum(local[8 * n : 8 * n + 8] * padded, axis=0, keepdims=True)
        m.append(jnp.concatenate([first, second], axis=0))
    answer = coefficients(m, centre, step)

    extra = jnp.zeros((8, LANES), F32)
    for n in range(4):
        extra = extra + answer[n][1:2] * local[8 * n : 8 * n + 8]
    elastic_stress = dot(elastic_ref[...], strain[:6])
    plastic = assign_ref[...] >= 0
    stress_ref[...] = elastic_stress + jnp.where(plastic, extra[:6, :points], 0.0)

    right = jnp.concatenate([(scale * answer[n][0:1]) * field for n in range(4)], axis=0)
    high = right.astype(BF16).astype(F32)
    right = jnp.concatenate([high, high, right - high, jnp.zeros_like(high)], axis=0).astype(BF16)
    for part in range(6):
        rows = slice(512 * part, 512 * part + 512)
        out_ref[rows, :] = bdot(u_ref[rows, :], right)


def call(kernel, outs, *args, scratch=()):
    vmem = pl.BlockSpec(memory_space=pltpu.VMEM)
    many = isinstance(outs, list)
    return pl.pallas_call(
        kernel,
        out_shape=outs,
        in_specs=[vmem] * len(args),
        out_specs=[vmem] * len(outs) if many else vmem,
        scratch_shapes=list(scratch),
        compiler_params=pltpu.CompilerParams(vmem_limit_bytes=32 * 1024 * 1024),
    )(*args)


def arr(*shape, dtype=F32):
    return jax.ShapeDtypeStruct(shape, dtype)


def shifted(x, by):
    devices = lax.axis_size("dev")
    return lax.ppermute(x, "dev", [(i, (i + by) % devices) for i in range(devices)])


def exchange(x, axis):
    return lax.all_to_all(x, axis, split_axis=0, concat_axis=0, tiled=True)


def local(
    displacement,
    connectivity,
    face_nodes,
    strain_map,
    assignment,
    phases,
    load_map,
    stiff_root,
    chain_map,
    bridge_map,
    elastic,
):
    groups = lax.axis_size("group")
    devs = lax.axis_size("dev")
    points = connectivity.shape[1]
    assign = assignment.reshape(1, -1)

    packed = call(
        pack_kernel,
        arr(ROWS, LANES),
        load_map,
        phases,
        scratch=[pltpu.VMEM((LANES, LANES), F32)],
    )
    near = [shifted(packed, 1), shifted(packed, 2), shifted(packed, -1), shifted(packed, -2)]
    faces = call(face_kernel, arr(devs, 1, LANES), displacement, face_nodes)
    arrived = exchange(faces, "dev")

    *weights, terms = call(
        weight_kernel,
        [
            arr(LANES, 2 * LANES, dtype=BF16),
            arr(LANES, 2 * LANES, dtype=BF16),
            arr(LANES, LANES, dtype=BF16),
            arr(LANES, LANES, dtype=BF16),
            arr(3 * LANES, LANES, dtype=BF16),
            arr(3 * LANES, LANES, dtype=BF16),
            arr(8, LANES),
        ],
        stiff_root,
        chain_map,
        bridge_map,
    )
    vectors, gram = call(
        krylov_kernel,
        [arr(4, ROWS, LANES), arr(1, 3 * LANES)],
        packed,
        *near,
        *weights,
        terms,
    )
    send, strain = call(
        strain_kernel,
        [arr(devs, 1, 4 * LANES), arr(8, points)],
        displacement,
        arrived,
        connectivity,
        strain_map,
        assign,
        gram,
    )
    section = exchange(send, "dev")
    turned = call(
        turn_kernel,
        arr(BLOCK * BLOCKS, LANES, dtype=BF16),
        vectors,
        scratch=[pltpu.VMEM((BLOCK * BLOCKS, LANES), F32)],
    )
    across, own = call(section_kernel, [arr(groups, 16, LANES), arr(8, LANES)], section)
    gathered = exchange(across, "group")
    scale = math.sqrt(BLOCK * devs * BLOCKS)
    stress, fluctuation = call(
        lambda *refs: final_kernel(scale, *refs),
        [arr(6, points), arr(BLOCK * BLOCKS, POINTS)],
        gathered,
        own,
        strain,
        assign,
        elastic,
        terms,
        turned,
    )
    return stress, fluctuation.reshape(1, BLOCK, BLOCKS, POINTS)


def solution(mesh):
    in_specs = (
        P(None, ("group", "dev")),
        P(None, ("group", "dev")),
        P(("group", "dev"), None, None),
        P(None, None, ("group", "dev")),
        P(("group", "dev")),
        P("group", None, "dev"),
        P(None, None, "dev"),
        P(),
        P(),
        P(),
        P(),
    )
    out_specs = (P(None, ("group", "dev")), P("group", None, "dev", None))
    return jax.shard_map(local, mesh=mesh, in_specs=in_specs, out_specs=out_specs, check_vma=False)
```

```python
import math

import jax
import jax.numpy as jnp
from jax import lax
from jax.experimental import pallas as pl
from jax.experimental.pallas import tpu as pltpu
from jax.sharding import PartitionSpec as P

BLOCK = 64
IFACE = 16
BLOCKS = 48
POINTS = 128
PLASTIC_CAP = 8
NODES = 256
HALF = BLOCKS // 2
ROWS = HALF * 8
LANES = 128

ridge = 0.5
F32 = jnp.float32
BF16 = jnp.bfloat16
HIGHEST = lax.Precision.HIGHEST


def iota(shape, dim):
    return lax.broadcasted_iota(jnp.int32, shape, dim)


def dot(a, b):
    return jnp.dot(a, b, precision=HIGHEST, preferred_element_type=F32)


def dot_nt(a, b):
    return lax.dot_general(
        a, b, (((1,), (1,)), ((), ())), precision=HIGHEST, preferred_element_type=F32
    )


def dot_tn(a, b):
    return lax.dot_general(
        a, b, (((0,), (0,)), ((), ())), precision=HIGHEST, preferred_element_type=F32
    )


def bdot(a, b):
    return jnp.dot(a, b, preferred_element_type=F32)


def bdot_nt(a, b):
    return lax.dot_general(a, b, (((1,), (1,)), ((), ())), preferred_element_type=F32)


def split2(x):
    high = x.astype(BF16)
    return high, (x - high.astype(F32)).astype(BF16)


def split3(x):
    high = x.astype(BF16).astype(F32)
    rest = x - high
    middle = rest.astype(BF16).astype(F32)
    return high, middle, rest - middle


def spread_rows(values):
    n = values.shape[1]
    rows = []
    for part in split3(values):
        for c in range(3):
            rows.append(jnp.broadcast_to(part[c : c + 1], (16, n)))
        rows.append(jnp.zeros((16, n), F32))
    return jnp.concatenate(rows, axis=0)


def stacked(ref, m):
    high, low = split2(m)
    rows = m.shape[0]
    ref[:rows] = high
    ref[rows : 2 * rows] = high
    ref[2 * rows :] = low


def rough(a, b):
    return bdot(a.astype(BF16), b.astype(BF16))


def pack(load, phase, out_ref):
    for c in range(6):
        out_ref[pl.ds(c, HALF, stride=8), :] = jnp.concatenate(
            [load[pl.ds(c, 1), pl.ds(par, HALF, stride=2), :][0] for par in range(2)], axis=1
        )
    labels = [phase[pl.ds(0, 1), pl.ds(par, HALF, stride=2), :][0] for par in range(2)]
    weights = 1.0 + 2.0 * jnp.concatenate(labels, axis=1).astype(F32)
    out_ref[pl.ds(6, HALF, stride=8), :] = weights
    out_ref[pl.ds(7, HALF, stride=8), :] = jnp.zeros((HALF, LANES), F32)


def faces(disp, listed, out_ref):
    devs = listed.shape[2]
    nodes = disp.shape[1]
    names = jnp.concatenate([listed[0].astype(F32), jnp.zeros((16, LANES - devs), F32)], axis=1)
    names = jnp.concatenate([names, jnp.zeros((LANES - 16, LANES), F32)], axis=0)
    names = jnp.transpose(names)[:devs]
    spread = spread_rows(disp[...])
    spread = jnp.concatenate([spread, jnp.zeros((64, nodes), F32)], axis=0).astype(BF16)
    place = iota((devs, nodes), 1).astype(F32)
    hot = jnp.concatenate(
        [jnp.where(names[:, j : j + 1] == place, 1.0, 0.0) for j in range(16)], axis=0
    ).astype(BF16)
    found = bdot_nt(hot, spread)
    lane = iota((devs, 256), 1) % 16
    total = jnp.zeros((devs, 256), F32)
    for j in range(16):
        total = total + jnp.where(lane == j, found[j * devs : (j + 1) * devs], 0.0)
    near = total[:, :LANES]
    out_ref[:, 0, :] = (near + pltpu.roll(near, 64, 1)) + total[:, LANES:]


def fetch(sources, targets, sems):
    copies = [
        pltpu.make_async_copy(a, b, sems.at[n]) for n, (a, b) in enumerate(zip(sources, targets))
    ]
    for copy in copies:
        copy.start()
    for copy in copies:
        copy.wait()


def own_nodes(disp, conn):
    nodes, points = disp.shape[1], conn.shape[1]
    index = side_by_side(conn[...])
    hot = jnp.where(iota((nodes, 8 * points), 0) == index, 1.0, 0.0).astype(BF16)
    parts = jnp.concatenate(split3(disp[...]) + (jnp.zeros((7, nodes), F32),), axis=0)
    found = bdot(parts.astype(BF16), hot)
    return by_node((found[0:3] + found[3:6]) + found[6:9], points)


def side_by_side(rows):
    return jnp.concatenate([rows[a : a + 1] for a in range(rows.shape[0])], axis=1)


def by_node(sums, points):
    return jnp.concatenate(
        [sums[:, a * points : (a + 1) * points] for a in range(8)],
        axis=0,
    )


def first_kernel(*refs):
    face_ref, pack_ref, carry_ref, disp, listed, load, phase, conn, maps, assign, sems = refs[7:]
    fetch(refs[:7], [disp, listed, load, phase, conn, maps, assign], sems)
    faces(disp, listed, face_ref)
    pack(load, phase, pack_ref)
    points = conn.shape[1]
    blank = jnp.zeros((7, points), F32)
    for c in range(6):
        carry_ref[24 * c : 24 * c + 24, :points] = maps[c]
    carry_ref[144:152, :points] = conn[...].astype(F32)
    carry_ref[152:160, :points] = jnp.concatenate([assign[...].astype(F32), blank], axis=0)
    carry_ref[160:184, :points] = own_nodes(disp, conn)
    carry_ref[:, points:] = jnp.zeros((184, LANES - points), F32)


def tables(root_ref, chain_ref, bridge_ref, w1, wb, w2, basis_ref):
    root, chain, bridge = root_ref[...], chain_ref[...], bridge_ref[...]
    zero = jnp.zeros((BLOCK, BLOCK), F32)

    def straight(m):
        return jnp.concatenate(
            [jnp.concatenate([m, zero], axis=1), jnp.concatenate([zero, m], axis=1)], axis=0
        )

    def crossed(m):
        return jnp.concatenate(
            [jnp.concatenate([zero, m], axis=1), jnp.concatenate([m, zero], axis=1)], axis=0
        )

    gap = BLOCK - IFACE
    wide = jnp.concatenate([bridge, jnp.zeros((IFACE, gap), F32)], axis=1)
    upper = jnp.concatenate([jnp.zeros((gap, BLOCK), F32), wide], axis=0)
    roots, chains, bridges = straight(root), crossed(chain), straight(upper)
    stacked(w1, jnp.concatenate([jnp.transpose(roots), jnp.transpose(chains)], axis=1))
    stacked(wb, jnp.transpose(bridges))
    stacked(w2, jnp.concatenate([roots, -chains, -bridges], axis=0))

    size = 2 * BLOCK
    diagonal = iota((size, size), 0) == iota((size, size), 1)
    edge = jnp.where(diagonal, 1.0, 0.0) - chains
    face = jnp.where(diagonal & (iota((size, size), 0) % BLOCK >= gap), 1.0, 0.0) - bridges
    tall = jnp.concatenate([2.0**0.5 * roots, edge, face], axis=0)
    model = rough(jnp.transpose(tall), tall)
    model = model + jnp.where(diagonal, ridge, 0.0)

    def inner(p, q):
        return jnp.sum(jnp.sum(p * q, axis=1, keepdims=True), axis=0, keepdims=True)

    now = jnp.where(diagonal, size**-0.5, 0.0)
    past, image = None, size**-0.5 * model
    centres, steps = [], []
    for n in range(3):
        if n:
            image = rough(model, now)
        centre = inner(now, image)
        rest = image - centre * now
        if n:
            rest = rest - steps[-1] * past
        step = jnp.maximum(jnp.sqrt(inner(rest, rest)), 0.01 * centres[0] if n else 0.01 * centre)
        centres.append(centre)
        steps.append(step)
        past, now = now, rest / step
    row = iota((8, LANES), 0)
    table = jnp.zeros((8, LANES), F32)
    for n, value in enumerate(centres + steps):
        table = jnp.where(row == n, value, table)
    basis_ref[...] = table


def krylov_kernel(
    own_ref, m1_ref, m2_ref, p1_ref, p2_ref, w1, wb, w2, basis_ref, u_ref, gram_ref
):
    centre = [basis_ref[n : n + 1, :] for n in range(3)]
    step = [basis_ref[n + 3 : n + 4, :] for n in range(3)]
    inverse = [1.0 / v for v in step]

    def lanes(x):
        return iota(x.shape, 1)

    def weights_of(x):
        w = x.reshape(HALF, 8, LANES)[:, 6:7, :]
        return jnp.broadcast_to(w, (HALF, 8, LANES)).reshape(ROWS, LANES)

    def stage(x, w):
        high, low = split2(x)
        return bdot(jnp.concatenate([high, low, high], axis=1), w[...])

    def blocks(x):
        return [x[n : n + ROWS] for n in range(0, x.shape[0], ROWS)]

    def up(x):
        parts = [p for v in blocks(x) for p in (v[8:], v[:8])]
        return jnp.concatenate(parts, axis=0)

    def down(x):
        parts = [p for v in blocks(x) for p in (v[ROWS - 8 :], v[: ROWS - 8])]
        return jnp.concatenate(parts, axis=0)

    def halves(x, w):
        both = stage(x, w1)
        lifted = both[:, :LANES]
        mixed = both[:, LANES:]
        edge = x - jnp.where(lanes(x) < BLOCK, mixed, up(mixed))
        return lifted, w * lifted, edge

    def face(x, following):
        return jnp.where(lanes(x) % BLOCK >= BLOCK - IFACE, x, 0.0) - following

    def apply(x, w, f, f_before):
        _, weighted, edge = halves(x, w)
        shifted = jnp.where(lanes(x) < BLOCK, edge, down(edge))
        left = jnp.concatenate([weighted, shifted, f_before], axis=1)
        return ridge * x + edge + f + stage(left, w2)

    zero = jnp.zeros((ROWS, LANES), F32)
    near = [m1_ref[...], own_ref[...], p1_ref[...], p2_ref[...]]
    w = jnp.concatenate([weights_of(x) for x in near], axis=0)

    x0 = jnp.concatenate(near, axis=0)
    known = jnp.concatenate([m2_ref[...], x0[: 3 * ROWS]], axis=0)
    f = jnp.concatenate([face(known, stage(x0, wb)), zero], axis=0)
    image = apply(x0, w, f[ROWS:], f[: 4 * ROWS])
    x1 = inverse[0] * (image - centre[0] * x0)

    f = jnp.concatenate([zero, face(x1[: 3 * ROWS], stage(x1[ROWS:], wb))], axis=0)
    now, past = x1[: 3 * ROWS], x0[: 3 * ROWS]
    image = apply(now, w[: 3 * ROWS], f[ROWS:], f[: 3 * ROWS])
    x2 = inverse[1] * (image - centre[1] * now - step[0] * past)

    f = jnp.concatenate([face(x2[: 2 * ROWS], stage(x2[ROWS:], wb)), zero], axis=0)
    now, past = x2[ROWS:], x1[ROWS : 3 * ROWS]
    image = apply(now, w[ROWS : 3 * ROWS], f[ROWS:], f[: 2 * ROWS])
    x3 = inverse[2] * (image - centre[2] * now - step[1] * past)

    own = x3[:ROWS]
    lifted, weighted, edge = halves(own, w[ROWS : 2 * ROWS])
    f3 = face(own, stage(x3[ROWS:], wb))

    basis = [near[1], x1[ROWS : 2 * ROWS], x2[ROWS : 2 * ROWS], own]
    for n in range(4):
        u_ref[n] = basis[n]

    def long(x):
        return jnp.concatenate([x[8 * k : 8 * k + 8] for k in range(HALF)], axis=1)

    tall = jnp.concatenate([long(x) for x in basis + [lifted, weighted, edge, f3]], axis=0)
    high = tall.astype(BF16).astype(F32)
    both = jnp.concatenate([high, tall - high], axis=0).astype(BF16)
    product = bdot_nt(both, both)
    product = product[:64] + product[64:]
    product = product + pltpu.roll(product, 64, 1)

    def pair(a, b, to):
        return pltpu.roll(product[8 * a : 8 * a + 8], (8 * (to - b)) % LANES, 1)

    at = iota((8, LANES), 1) // 8
    energy = 0.5 * pair(3, 3, 7) + (pair(4, 5, 7) + pair(6, 6, 7) + pair(7, 7, 7))
    moments = jnp.where(at < 4, product[:8], 0.0)
    moments = jnp.where(at == 4, pair(2, 2, 4), moments)
    moments = jnp.where(at == 5, pair(2, 3, 5), moments)
    moments = jnp.where(at == 6, pair(3, 3, 6), moments)
    moments = jnp.where(at == 7, energy, moments)
    for t in range(3):
        gram_ref[:, t * LANES : (t + 1) * LANES] = moments[2 * t : 2 * t + 1] + pltpu.roll(
            moments[2 * t + 1 : 2 * t + 2], 64, 1
        )


def turn_kernel(u_ref, out_ref, wide):
    for k in range(HALF):
        rows = jnp.concatenate([u_ref[n, 8 * k : 8 * k + 8, :] for n in range(4)], axis=0)
        high = rows.astype(BF16).astype(F32)
        stack = jnp.concatenate([high, rows - high, high, jnp.zeros_like(high)], axis=0)
        turned = jnp.transpose(stack)
        wide[pl.ds(2 * k, BLOCK, stride=BLOCKS), :] = turned[:BLOCK]
        wide[pl.ds(2 * k + 1, BLOCK, stride=BLOCKS), :] = turned[BLOCK:]
    out_ref[...] = wide[...].astype(BF16)


def strain_kernel(carry_ref, arrived_ref, gram_ref, send_ref, strain_ref):
    devs = arrived_ref.shape[0]
    copies = send_ref.shape[0]
    points = strain_ref.shape[1]
    index = side_by_side(carry_ref[144:152, :points].astype(jnp.int32))
    refs = 8 * points
    partner = (index - NODES) >> 4
    other = jnp.where(iota((devs, refs), 0) == partner, 1.0, 0.0).astype(BF16)
    ghost = jnp.transpose(arrived_ref[:, 0, :])[:64]
    ghost = jnp.concatenate(split3(ghost), axis=0).astype(BF16)
    found = bdot(ghost, other)
    found = (found[:64] + found[64:128]) + found[128:]
    found = jnp.where(iota((64, refs), 0) % 16 == index % 16, found, 0.0)
    sums = [jnp.sum(found[16 * c : 16 * c + 16], axis=0, keepdims=True) for c in range(3)]
    nodal = by_node(jnp.concatenate(sums, axis=0), points) + carry_ref[160:184, :points]
    strain = jnp.concatenate(
        [
            jnp.sum(carry_ref[24 * c : 24 * c + 24, :points] * nodal, axis=0, keepdims=True)
            for c in range(6)
        ],
        axis=0,
    )
    strain_ref[...] = jnp.concatenate([strain, jnp.zeros((2, points), F32)], axis=0)

    assign = carry_ref[152:153, :points]
    plastic = assign >= 0.0
    flags = jnp.where(plastic, 1.0, 0.0)
    before = jnp.where(iota((points, points), 0) < iota((points, points), 1), 1.0, 0.0)
    rank = bdot(jnp.broadcast_to(flags, (8, points)).astype(BF16), before.astype(BF16))
    pick = jnp.where(plastic & (rank == iota((8, points), 0).astype(F32)), 1.0, 0.0)
    values = jnp.concatenate(
        [
            strain,
            assign + 1.0,
            jnp.zeros((LANES - 7, points), F32),
        ],
        axis=0,
    )
    chosen = dot_nt(pick, values)
    line = chosen[0:1]
    for slot in range(1, PLASTIC_CAP):
        line = line + pltpu.roll(chosen[slot : slot + 1], 8 * slot, 1)
    line = jnp.concatenate([gram_ref[...], line], axis=1)
    send_ref[:, 0, :] = jnp.broadcast_to(line, (copies, 4 * LANES))


def section_kernel(arrived_ref, send_ref):
    devs = arrived_ref.shape[0]
    groups = send_ref.shape[0] // 2
    total = jnp.sum(arrived_ref[:, 0, : 3 * LANES], axis=0, keepdims=True)
    cand = arrived_ref[:, 0, 3 * LANES :]
    turned = jnp.transpose(jnp.concatenate([cand] * (LANES // devs), axis=0))
    line = jnp.concatenate([turned[8 * n : 8 * n + 8, :devs] for n in range(PLASTIC_CAP)], axis=1)
    width = PLASTIC_CAP * devs
    target = line[6:7].astype(jnp.int32) - 1
    row = iota((64, width), 0)
    keep = ((target >> 7) == row // 8) & (row % 8 < 6)
    left = [
        jnp.where(keep, jnp.concatenate([part] * 8, axis=0), 0.0).astype(BF16)
        for part in split3(line)
    ]
    hot = jnp.where(iota((POINTS, width), 0) == (target & (POINTS - 1)), 1.0, 0.0).astype(BF16)
    dense = bdot_nt(jnp.concatenate(left, axis=0), hot)
    dense = (dense[:64] + dense[64:128]) + dense[128:]
    for h in range(groups):
        for core in range(2):
            for c in range(6):
                lanes = slice(c * LANES, (c + 1) * LANES)
                send_ref[2 * h + core, :, lanes] = dense[8 * h + c : 8 * h + c + 1]
            send_ref[2 * h + core, :, 6 * LANES :] = total


def coefficients(m, centre, step):
    m00, m01, m02, m03, m22, m23, m33, energy = m
    m11 = m00 + (step[1] * m02 + (centre[1] - centre[0]) * m01) / step[0]
    m12 = (step[2] * m03 + (centre[2] - centre[0]) * m02 + step[1] * m01) / step[0]
    m13 = (step[1] * (m22 - m11) + (centre[1] - centre[2]) * m12 + step[0] * m02) / step[2]
    products = [
        [m00, m01, m02, m03],
        [m01, m11, m12, m13],
        [m02, m12, m22, m23],
        [m03, m13, m23, m33],
    ]

    def gram(a, b):
        return products[a][b]

    def image(a, b):
        a, b = max(a, b), min(a, b)
        if b == 3:
            return energy
        value = step[b] * products[a][b + 1] + centre[b] * products[a][b]
        return value + step[b - 1] * products[a][b - 1] if b else value

    def inner(p, form):
        total = None
        for a in range(len(p)):
            for b in range(a, len(p)):
                term = p[a] * p[b] * form(a, b)
                if a != b:
                    term = 2.0 * term
                total = term if total is None else total + term
        return total

    def times(p):
        out = [jnp.zeros_like(p[0]) for _ in range(len(p) + 1)]
        for b, v in enumerate(p):
            out[b + 1] = out[b + 1] + step[b] * v
            out[b] = out[b] + centre[b] * v
            if b:
                out[b - 1] = out[b - 1] + step[b - 1] * v
        return out

    one = jnp.ones_like(m00)
    answer = []
    residual = [one]
    direction = [one]
    norm = m00
    for turn in range(4):
        alpha = norm / inner(direction, image)
        answer = answer + [jnp.zeros_like(one)]
        answer = [x + alpha * p for x, p in zip(answer, direction)]
        if turn < 3:
            stepped = times(direction)
            residual = residual + [jnp.zeros_like(one)]
            residual = [r - alpha * v for r, v in zip(residual, stepped)]
            later = inner(residual, gram)
            beta = later / norm
            direction = direction + [jnp.zeros_like(one)]
            direction = [r + beta * p for r, p in zip(residual, direction)]
            norm = later
    return answer


def final_kernel(
    scale,
    arrived_ref,
    strain_ref,
    assign_ref,
    elastic_ref,
    basis_ref,
    u_ref,
    stress_ref,
    out_hbm,
    out_ref,
    sems,
):
    groups = arrived_ref.shape[0] // 2
    points = strain_ref.shape[1]
    mine = lax.axis_index("group")
    centre = [basis_ref[n : n + 1, :] for n in range(3)]
    step = [basis_ref[n + 3 : n + 4, :] for n in range(3)]
    both = jnp.sum(arrived_ref[:, 0, : 6 * LANES], axis=0, keepdims=True)
    field = [both[:, c * LANES : (c + 1) * LANES] for c in range(6)]
    field = jnp.concatenate(field + [jnp.zeros((2, LANES), F32)], axis=0)

    def unfold(lines):
        tiles = []
        for t in range(3):
            tile = lines[:, t * LANES : (t + 1) * LANES]
            low = iota(tile.shape, 1) < 64
            tiles.append(jnp.where(low, tile, 0.0))
            tiles.append(jnp.where(low, pltpu.roll(tile, 64, 1), 0.0))
        blank = jnp.zeros((2, LANES), F32)
        return [
            jnp.concatenate([v[h : h + 1] for v in tiles] + [blank], axis=0)
            for h in range(lines.shape[0])
        ]

    lane = iota((8, LANES), 1)
    diagonal = (iota((64, LANES), 0) // 8) == (iota((64, LANES), 1) % 64) // 8

    def tall(x):
        return jnp.concatenate([x] * 8, axis=0)

    def opened(moments):
        high, middle, low = split3(moments + pltpu.roll(moments, 64, 1))
        first = jnp.where(diagonal, tall(jnp.where(lane < 64, high, middle)), 0.0).astype(BF16)
        second = jnp.where(diagonal, tall(jnp.where(lane < 64, high, low)), 0.0).astype(BF16)
        return jnp.concatenate([first, first, second], axis=1)

    def meeting(x):
        high, middle, low = (tall(part) for part in split3(x))
        parts = [high, high, middle, middle, low, high]
        return jnp.concatenate(parts, axis=0).astype(BF16)

    strain = strain_ref[...]
    padded = jnp.concatenate([strain, jnp.zeros((8, LANES - points), F32)], axis=1)
    assign = jnp.concatenate(
        [assign_ref[...], jnp.full((1, LANES - points), -1, jnp.int32)], axis=1
    )
    halves = arrived_ref[:, 0, 6 * LANES :]
    whole = [halves[2 * h : 2 * h + 1] + halves[2 * h + 1 : 2 * h + 2] for h in range(groups)]
    every = unfold(jnp.concatenate(whole, axis=0))
    own = jnp.zeros((8, LANES), F32)
    for h in range(groups):
        own = own + jnp.where(mine == h, every[h], 0.0)
    forces = bdot(opened(own), meeting(field))
    every = jnp.concatenate([opened(v) for v in every], axis=0)
    products = bdot(every, meeting(padded))
    group_of = assign >> 7
    local = jnp.zeros((64, LANES), F32)
    for h in range(groups):
        local = local + jnp.where(group_of == h, products[64 * h : 64 * h + 64], 0.0)

    m = []
    for n in range(8):
        first = jnp.sum(forces[8 * n : 8 * n + 8] * field, axis=0, keepdims=True)
        second = jnp.sum(local[8 * n : 8 * n + 8] * padded, axis=0, keepdims=True)
        m.append(jnp.concatenate([first, second], axis=0))
    answer = coefficients(m, centre, step)

    extra = jnp.zeros((8, LANES), F32)
    for n in range(4):
        extra = extra + answer[n][1:2] * local[8 * n : 8 * n + 8]
    elastic_stress = dot(elastic_ref[...], strain[:6])
    plastic = assign_ref[...] >= 0
    stress_ref[...] = elastic_stress + jnp.where(plastic, extra[:6, :points], 0.0)

    right = jnp.concatenate([(scale * answer[n][0:1]) * field for n in range(4)], axis=0)
    high = right.astype(BF16).astype(F32)
    right = jnp.concatenate([high, high, right - high, jnp.zeros_like(high)], axis=0).astype(BF16)
    copies = []
    for part in range(6):
        rows = pl.ds(512 * part, 512)
        out_ref[rows, :] = bdot(u_ref[rows, :], right)
        copy = pltpu.make_async_copy(out_ref.at[rows], out_hbm.at[rows], sems.at[part])
        copy.start()
        copies.append(copy)
    for copy in copies:
        copy.wait()


def call(kernel, outs, *args, scratch=(), own_copies=0, last_out=None):
    vmem = pl.BlockSpec(memory_space=pltpu.VMEM)
    many = isinstance(outs, list)
    out_specs = [vmem] * len(outs) if many else vmem
    if last_out:
        out_specs[-1] = pl.BlockSpec(memory_space=last_out)
    scratch = list(scratch)
    if own_copies:
        scratch += [pltpu.VMEM(x.shape, x.dtype) for x in args[:own_copies]]
        scratch += [pltpu.SemaphoreType.DMA((own_copies,))]
    spaces = [pl.BlockSpec(memory_space=pltpu.HBM)] * own_copies + [vmem] * len(args)
    limit = 60 if own_copies else 32
    return pl.pallas_call(
        kernel,
        out_shape=outs,
        in_specs=spaces[: len(args)],
        out_specs=out_specs,
        scratch_shapes=scratch,
        compiler_params=pltpu.CompilerParams(vmem_limit_bytes=limit * 1024 * 1024),
    )(*args)


def arr(*shape, dtype=F32):
    return jax.ShapeDtypeStruct(shape, dtype)


def shifted(x, by):
    devices = lax.axis_size("dev")
    return lax.ppermute(x, "dev", [(i, (i + by) % devices) for i in range(devices)])


def exchange(x, axis, members=None):
    return lax.all_to_all(
        x, axis, split_axis=0, concat_axis=0, tiled=True, axis_index_groups=members
    )


def local(
    displacement,
    connectivity,
    face_nodes,
    strain_map,
    assignment,
    phases,
    load_map,
    stiff_root,
    chain_map,
    bridge_map,
    elastic,
):
    groups = lax.axis_size("group")
    devs = lax.axis_size("dev")
    points = connectivity.shape[1]
    assign = assignment.reshape(1, -1)

    listed = jnp.transpose(face_nodes, (0, 2, 1))
    load = jnp.transpose(load_map, (0, 2, 1))
    labels = jnp.transpose(phases, (0, 2, 1))
    sources = [displacement, listed, load, labels, connectivity, strain_map, assign]
    outgoing, packed, carry = call(
        first_kernel,
        [arr(devs, 1, LANES), arr(ROWS, LANES), arr(184, LANES)],
        *sources,
        own_copies=len(sources),
    )
    *weights, terms = call(
        tables,
        [
            arr(3 * LANES, 2 * LANES, dtype=BF16),
            arr(3 * LANES, LANES, dtype=BF16),
            arr(9 * LANES, LANES, dtype=BF16),
            arr(8, LANES),
        ],
        stiff_root,
        chain_map,
        bridge_map,
    )
    arrived = exchange(outgoing, "dev")
    near = [shifted(packed, 1), shifted(packed, 2), shifted(packed, -1), shifted(packed, -2)]
    vectors, gram = call(
        krylov_kernel,
        [arr(4, ROWS, LANES), arr(1, 3 * LANES)],
        packed,
        *near,
        *weights,
        terms,
    )
    send, strain = call(
        strain_kernel,
        [arr(devs // 2, 1, 4 * LANES), arr(8, points)],
        carry,
        arrived,
        gram,
    )
    same_core = [list(range(core, devs, 2)) for core in range(2)]
    same_chip = [
        [g * devs + chip + core for g in range(groups) for core in range(2)]
        for chip in range(0, devs, 2)
    ]
    section = exchange(send, "dev", same_core)
    turned = call(
        turn_kernel,
        arr(BLOCK * BLOCKS, LANES, dtype=BF16),
        vectors,
        scratch=[pltpu.VMEM((BLOCK * BLOCKS, LANES), F32)],
    )
    across = call(section_kernel, arr(2 * groups, 1, 9 * LANES), section)
    gathered = exchange(across, ("group", "dev"), same_chip)
    scale = math.sqrt(BLOCK * devs * BLOCKS)
    stress, fluctuation = call(
        lambda *refs: final_kernel(scale, *refs),
        [arr(6, points), arr(BLOCK * BLOCKS, POINTS)],
        gathered,
        strain,
        assign,
        elastic,
        terms,
        turned,
        scratch=[
            pltpu.VMEM((BLOCK * BLOCKS, POINTS), F32),
            pltpu.SemaphoreType.DMA((6,)),
        ],
        last_out=pl.ANY,
    )
    return stress, fluctuation.reshape(1, BLOCK, BLOCKS, POINTS)


def solution(mesh):
    in_specs = (
        P(None, ("group", "dev")),
        P(None, ("group", "dev")),
        P(("group", "dev"), None, None),
        P(None, None, ("group", "dev")),
        P(("group", "dev")),
        P("group", None, "dev"),
        P(None, None, "dev"),
        P(),
        P(),
        P(),
        P(),
    )
    out_specs = (P(None, ("group", "dev")), P("group", None, "dev", None))
    return jax.shard_map(local, mesh=mesh, in_specs=in_specs, out_specs=out_specs, check_vma=False)
```

```python
import math

import jax
import jax.numpy as jnp
from jax import lax
from jax.experimental import pallas as pl
from jax.experimental.pallas import tpu as pltpu
from jax.sharding import PartitionSpec as P

BLOCK = 64
IFACE = 16
BLOCKS = 48
POINTS = 128
PLASTIC_CAP = 8
NODES = 256
HALF = BLOCKS // 2
ROWS = HALF * 8
LANES = 128

ridge = 0.5
F32 = jnp.float32
BF16 = jnp.bfloat16
HIGHEST = lax.Precision.HIGHEST


def iota(shape, dim):
    return lax.broadcasted_iota(jnp.int32, shape, dim)


def dot(a, b):
    return jnp.dot(a, b, precision=HIGHEST, preferred_element_type=F32)


def dot_nt(a, b):
    return lax.dot_general(
        a, b, (((1,), (1,)), ((), ())), precision=HIGHEST, preferred_element_type=F32
    )


def dot_tn(a, b):
    return lax.dot_general(
        a, b, (((0,), (0,)), ((), ())), precision=HIGHEST, preferred_element_type=F32
    )


def bdot(a, b):
    return jnp.dot(a, b, preferred_element_type=F32)


def bdot_nt(a, b):
    return lax.dot_general(a, b, (((1,), (1,)), ((), ())), preferred_element_type=F32)


def split2(x):
    high = x.astype(BF16)
    return high, (x - high.astype(F32)).astype(BF16)


def split3(x):
    high = x.astype(BF16).astype(F32)
    rest = x - high
    middle = rest.astype(BF16).astype(F32)
    return high, middle, rest - middle


def spread_rows(values):
    n = values.shape[1]
    rows = []
    for part in split3(values):
        for c in range(3):
            rows.append(jnp.broadcast_to(part[c : c + 1], (16, n)))
        rows.append(jnp.zeros((16, n), F32))
    return jnp.concatenate(rows, axis=0)


def stacked(ref, m):
    high, low = split2(m)
    rows = m.shape[0]
    ref[:rows] = high
    ref[rows : 2 * rows] = high
    ref[2 * rows :] = low


def rough(a, b):
    return bdot(a.astype(BF16), b.astype(BF16))


def pack(load, phase, out_ref):
    for c in range(6):
        out_ref[pl.ds(c, HALF, stride=8), :] = jnp.concatenate(
            [load[pl.ds(c, 1), pl.ds(par, HALF, stride=2), :][0] for par in range(2)], axis=1
        )
    labels = [phase[pl.ds(0, 1), pl.ds(par, HALF, stride=2), :][0] for par in range(2)]
    weights = 1.0 + 2.0 * jnp.concatenate(labels, axis=1).astype(F32)
    out_ref[pl.ds(6, HALF, stride=8), :] = weights
    out_ref[pl.ds(7, HALF, stride=8), :] = jnp.zeros((HALF, LANES), F32)


def faces(disp, listed, out_ref):
    devs = listed.shape[2]
    nodes = disp.shape[1]
    names = jnp.concatenate([listed[0].astype(F32), jnp.zeros((16, LANES - devs), F32)], axis=1)
    names = jnp.concatenate([names, jnp.zeros((LANES - 16, LANES), F32)], axis=0)
    names = jnp.transpose(names)[:devs]
    spread = spread_rows(disp[...])
    spread = jnp.concatenate([spread, jnp.zeros((64, nodes), F32)], axis=0).astype(BF16)
    place = iota((devs, nodes), 1).astype(F32)
    hot = jnp.concatenate(
        [jnp.where(names[:, j : j + 1] == place, 1.0, 0.0) for j in range(16)], axis=0
    ).astype(BF16)
    found = bdot_nt(hot, spread)
    lane = iota((devs, 256), 1) % 16
    total = jnp.zeros((devs, 256), F32)
    for j in range(16):
        total = total + jnp.where(lane == j, found[j * devs : (j + 1) * devs], 0.0)
    near = total[:, :LANES]
    out_ref[:, 0, :] = (near + pltpu.roll(near, 64, 1)) + total[:, LANES:]


def fetch(sources, targets, sems):
    copies = [
        pltpu.make_async_copy(a, b, sems.at[n]) for n, (a, b) in enumerate(zip(sources, targets))
    ]
    for copy in copies:
        copy.start()
    for copy in copies:
        copy.wait()


def own_nodes(disp, conn):
    nodes, points = disp.shape[1], conn.shape[1]
    index = side_by_side(conn[...])
    hot = jnp.where(iota((nodes, 8 * points), 0) == index, 1.0, 0.0).astype(BF16)
    parts = jnp.concatenate(split3(disp[...]) + (jnp.zeros((7, nodes), F32),), axis=0)
    found = bdot(parts.astype(BF16), hot)
    return by_node((found[0:3] + found[3:6]) + found[6:9], points)


def side_by_side(rows):
    return jnp.concatenate([rows[a : a + 1] for a in range(rows.shape[0])], axis=1)


def by_node(sums, points):
    return jnp.concatenate(
        [sums[:, a * points : (a + 1) * points] for a in range(8)],
        axis=0,
    )


def first_kernel(*refs):
    face_ref, pack_ref, rest_ref, *held, sems = refs[10:]
    fetch(refs[:10], held, sems)
    disp, listed, load, phase, conn, maps, assign, root, chain, bridge = held
    faces(disp, listed, face_ref)
    pack(load, phase, pack_ref)
    points = conn.shape[1]
    blank = jnp.zeros((7, points), F32)
    for c in range(6):
        rest_ref[24 * c : 24 * c + 24, :points] = maps[c]
    rest_ref[144:152, :points] = conn[...].astype(F32)
    rest_ref[152:160, :points] = jnp.concatenate([assign[...].astype(F32), blank], axis=0)
    rest_ref[160:184, :points] = own_nodes(disp, conn)
    rest_ref[:184, points:] = jnp.zeros((184, LANES - points), F32)
    rest_ref[184:248, :] = jnp.concatenate([root[...], chain[...]], axis=1)
    wide = jnp.concatenate([bridge[...], jnp.zeros((IFACE, LANES - IFACE), F32)], axis=1)
    rest_ref[248:264, :] = wide
    rest_ref[264:, :] = pack_ref[...]


def tables(rest_ref, w1, wb, w2, basis_ref):
    root, chain = rest_ref[184:248, :BLOCK], rest_ref[184:248, BLOCK:]
    bridge = rest_ref[248:264, :IFACE]
    zero = jnp.zeros((BLOCK, BLOCK), F32)

    def straight(m):
        return jnp.concatenate(
            [jnp.concatenate([m, zero], axis=1), jnp.concatenate([zero, m], axis=1)], axis=0
        )

    def crossed(m):
        return jnp.concatenate(
            [jnp.concatenate([zero, m], axis=1), jnp.concatenate([m, zero], axis=1)], axis=0
        )

    gap = BLOCK - IFACE
    wide = jnp.concatenate([bridge, jnp.zeros((IFACE, gap), F32)], axis=1)
    upper = jnp.concatenate([jnp.zeros((gap, BLOCK), F32), wide], axis=0)
    roots, chains, bridges = straight(root), crossed(chain), straight(upper)
    stacked(w1, jnp.concatenate([jnp.transpose(roots), jnp.transpose(chains)], axis=1))
    stacked(wb, jnp.transpose(bridges))
    stacked(w2, jnp.concatenate([roots, -chains, -bridges], axis=0))

    size = 2 * BLOCK
    diagonal = iota((size, size), 0) == iota((size, size), 1)
    edge = jnp.where(diagonal, 1.0, 0.0) - chains
    face = jnp.where(diagonal & (iota((size, size), 0) % BLOCK >= gap), 1.0, 0.0) - bridges
    tall = jnp.concatenate([2.0**0.5 * roots, edge, face], axis=0)
    model = rough(jnp.transpose(tall), tall)
    model = model + jnp.where(diagonal, ridge, 0.0)

    def inner(p, q):
        return jnp.sum(jnp.sum(p * q, axis=1, keepdims=True), axis=0, keepdims=True)

    now = jnp.where(diagonal, size**-0.5, 0.0)
    past, image = None, size**-0.5 * model
    centres, steps = [], []
    for n in range(3):
        if n:
            image = rough(model, now)
        centre = inner(now, image)
        rest = image - centre * now
        if n:
            rest = rest - steps[-1] * past
        step = jnp.maximum(jnp.sqrt(inner(rest, rest)), 0.01 * centres[0] if n else 0.01 * centre)
        centres.append(centre)
        steps.append(step)
        past, now = now, rest / step
    row = iota((8, LANES), 0)
    table = jnp.zeros((8, LANES), F32)
    for n, value in enumerate(centres + steps):
        table = jnp.where(row == n, value, table)
    basis_ref[...] = table


def krylov_kernel(
    rest_ref, m1_ref, m2_ref, p1_ref, p2_ref, w1, wb, w2, basis_ref, cand_ref, u_ref, send_ref
):
    centre = [basis_ref[n : n + 1, :] for n in range(3)]
    step = [basis_ref[n + 3 : n + 4, :] for n in range(3)]
    inverse = [1.0 / v for v in step]

    def lanes(x):
        return iota(x.shape, 1)

    def weights_of(x):
        w = x.reshape(HALF, 8, LANES)[:, 6:7, :]
        return jnp.broadcast_to(w, (HALF, 8, LANES)).reshape(ROWS, LANES)

    def stage(x, w):
        high, low = split2(x)
        return bdot(jnp.concatenate([high, low, high], axis=1), w[...])

    def blocks(x):
        return [x[n : n + ROWS] for n in range(0, x.shape[0], ROWS)]

    def up(x):
        parts = [p for v in blocks(x) for p in (v[8:], v[:8])]
        return jnp.concatenate(parts, axis=0)

    def down(x):
        parts = [p for v in blocks(x) for p in (v[ROWS - 8 :], v[: ROWS - 8])]
        return jnp.concatenate(parts, axis=0)

    def halves(x, w):
        both = stage(x, w1)
        lifted = both[:, :LANES]
        mixed = both[:, LANES:]
        edge = x - jnp.where(lanes(x) < BLOCK, mixed, up(mixed))
        return lifted, w * lifted, edge

    def face(x, following):
        return jnp.where(lanes(x) % BLOCK >= BLOCK - IFACE, x, 0.0) - following

    def apply(x, w, f, f_before):
        _, weighted, edge = halves(x, w)
        shifted = jnp.where(lanes(x) < BLOCK, edge, down(edge))
        left = jnp.concatenate([weighted, shifted, f_before], axis=1)
        return ridge * x + edge + f + stage(left, w2)

    zero = jnp.zeros((ROWS, LANES), F32)
    near = [m1_ref[...], rest_ref[264:, :], p1_ref[...], p2_ref[...]]
    w = jnp.concatenate([weights_of(x) for x in near], axis=0)

    x0 = jnp.concatenate(near, axis=0)
    known = jnp.concatenate([m2_ref[...], x0[: 3 * ROWS]], axis=0)
    f = jnp.concatenate([face(known, stage(x0, wb)), zero], axis=0)
    image = apply(x0, w, f[ROWS:], f[: 4 * ROWS])
    x1 = inverse[0] * (image - centre[0] * x0)

    f = jnp.concatenate([zero, face(x1[: 3 * ROWS], stage(x1[ROWS:], wb))], axis=0)
    now, past = x1[: 3 * ROWS], x0[: 3 * ROWS]
    image = apply(now, w[: 3 * ROWS], f[ROWS:], f[: 3 * ROWS])
    x2 = inverse[1] * (image - centre[1] * now - step[0] * past)

    f = jnp.concatenate([face(x2[: 2 * ROWS], stage(x2[ROWS:], wb)), zero], axis=0)
    now, past = x2[ROWS:], x1[ROWS : 3 * ROWS]
    image = apply(now, w[ROWS : 3 * ROWS], f[ROWS:], f[: 2 * ROWS])
    x3 = inverse[2] * (image - centre[2] * now - step[1] * past)

    own = x3[:ROWS]
    lifted, weighted, edge = halves(own, w[ROWS : 2 * ROWS])
    f3 = face(own, stage(x3[ROWS:], wb))

    basis = [near[1], x1[ROWS : 2 * ROWS], x2[ROWS : 2 * ROWS], own]
    for n in range(4):
        u_ref[n] = basis[n]

    def long(x):
        return jnp.concatenate([x[8 * k : 8 * k + 8] for k in range(HALF)], axis=1)

    tall = jnp.concatenate([long(x) for x in basis + [lifted, weighted, edge, f3]], axis=0)
    high = tall.astype(BF16).astype(F32)
    both = jnp.concatenate([high, tall - high], axis=0).astype(BF16)
    product = bdot_nt(both, both)
    product = product[:64] + product[64:]
    product = product + pltpu.roll(product, 64, 1)

    def pair(a, b, to):
        return pltpu.roll(product[8 * a : 8 * a + 8], (8 * (to - b)) % LANES, 1)

    at = iota((8, LANES), 1) // 8
    energy = 0.5 * pair(3, 3, 7) + (pair(4, 5, 7) + pair(6, 6, 7) + pair(7, 7, 7))
    moments = jnp.where(at < 4, product[:8], 0.0)
    moments = jnp.where(at == 4, pair(2, 2, 4), moments)
    moments = jnp.where(at == 5, pair(2, 3, 5), moments)
    moments = jnp.where(at == 6, pair(3, 3, 6), moments)
    moments = jnp.where(at == 7, energy, moments)
    line = [
        moments[2 * t : 2 * t + 1] + pltpu.roll(moments[2 * t + 1 : 2 * t + 2], 64, 1)
        for t in range(3)
    ]
    line = jnp.concatenate(line + [cand_ref[...]], axis=1)
    send_ref[:, 0, :] = jnp.broadcast_to(line, (send_ref.shape[0], 4 * LANES))


def turn_kernel(u_ref, out_ref, wide):
    for k in range(HALF):
        rows = jnp.concatenate([u_ref[n, 8 * k : 8 * k + 8, :] for n in range(4)], axis=0)
        high = rows.astype(BF16).astype(F32)
        stack = jnp.concatenate([high, rows - high, high, jnp.zeros_like(high)], axis=0)
        turned = jnp.transpose(stack)
        wide[pl.ds(2 * k, BLOCK, stride=BLOCKS), :] = turned[:BLOCK]
        wide[pl.ds(2 * k + 1, BLOCK, stride=BLOCKS), :] = turned[BLOCK:]
    out_ref[...] = wide[...].astype(BF16)


def strain_kernel(rest_ref, arrived_ref, cand_ref, strain_ref):
    devs = arrived_ref.shape[0]
    points = strain_ref.shape[1]
    index = side_by_side(rest_ref[144:152, :points].astype(jnp.int32))
    refs = 8 * points
    partner = (index - NODES) >> 4
    other = jnp.where(iota((devs, refs), 0) == partner, 1.0, 0.0).astype(BF16)
    ghost = jnp.transpose(arrived_ref[:, 0, :])[:64]
    ghost = jnp.concatenate(split3(ghost), axis=0).astype(BF16)
    found = bdot(ghost, other)
    found = (found[:64] + found[64:128]) + found[128:]
    found = jnp.where(iota((64, refs), 0) % 16 == index % 16, found, 0.0)
    sums = [jnp.sum(found[16 * c : 16 * c + 16], axis=0, keepdims=True) for c in range(3)]
    nodal = by_node(jnp.concatenate(sums, axis=0), points) + rest_ref[160:184, :points]
    strain = jnp.concatenate(
        [
            jnp.sum(rest_ref[24 * c : 24 * c + 24, :points] * nodal, axis=0, keepdims=True)
            for c in range(6)
        ],
        axis=0,
    )
    strain_ref[...] = jnp.concatenate([strain, jnp.zeros((2, points), F32)], axis=0)

    assign = rest_ref[152:153, :points]
    plastic = assign >= 0.0
    flags = jnp.where(plastic, 1.0, 0.0)
    before = jnp.where(iota((points, points), 0) < iota((points, points), 1), 1.0, 0.0)
    rank = bdot(jnp.broadcast_to(flags, (8, points)).astype(BF16), before.astype(BF16))
    pick = jnp.where(plastic & (rank == iota((8, points), 0).astype(F32)), 1.0, 0.0)
    values = jnp.concatenate(
        [
            strain,
            assign + 1.0,
            jnp.zeros((LANES - 7, points), F32),
        ],
        axis=0,
    )
    chosen = dot_nt(pick, values)
    line = chosen[0:1]
    for slot in range(1, PLASTIC_CAP):
        line = line + pltpu.roll(chosen[slot : slot + 1], 8 * slot, 1)
    cand_ref[...] = line


def section_kernel(arrived_ref, send_ref):
    devs = arrived_ref.shape[0]
    groups = send_ref.shape[0] // 2
    total = jnp.sum(arrived_ref[:, 0, : 3 * LANES], axis=0, keepdims=True)
    cand = arrived_ref[:, 0, 3 * LANES :]
    turned = jnp.transpose(jnp.concatenate([cand] * (LANES // devs), axis=0))
    line = jnp.concatenate([turned[8 * n : 8 * n + 8, :devs] for n in range(PLASTIC_CAP)], axis=1)
    width = PLASTIC_CAP * devs
    target = line[6:7].astype(jnp.int32) - 1
    row = iota((64, width), 0)
    keep = ((target >> 7) == row // 8) & (row % 8 < 6)
    left = [
        jnp.where(keep, jnp.concatenate([part] * 8, axis=0), 0.0).astype(BF16)
        for part in split3(line)
    ]
    hot = jnp.where(iota((POINTS, width), 0) == (target & (POINTS - 1)), 1.0, 0.0).astype(BF16)
    dense = bdot_nt(jnp.concatenate(left, axis=0), hot)
    dense = (dense[:64] + dense[64:128]) + dense[128:]
    for h in range(groups):
        for core in range(2):
            for c in range(6):
                lanes = slice(c * LANES, (c + 1) * LANES)
                send_ref[2 * h + core, :, lanes] = dense[8 * h + c : 8 * h + c + 1]
            send_ref[2 * h + core, :, 6 * LANES :] = total


def coefficients(m, centre, step):
    m00, m01, m02, m03, m22, m23, m33, energy = m
    m11 = m00 + (step[1] * m02 + (centre[1] - centre[0]) * m01) / step[0]
    m12 = (step[2] * m03 + (centre[2] - centre[0]) * m02 + step[1] * m01) / step[0]
    m13 = (step[1] * (m22 - m11) + (centre[1] - centre[2]) * m12 + step[0] * m02) / step[2]
    products = [
        [m00, m01, m02, m03],
        [m01, m11, m12, m13],
        [m02, m12, m22, m23],
        [m03, m13, m23, m33],
    ]

    def gram(a, b):
        return products[a][b]

    def image(a, b):
        a, b = max(a, b), min(a, b)
        if b == 3:
            return energy
        value = step[b] * products[a][b + 1] + centre[b] * products[a][b]
        return value + step[b - 1] * products[a][b - 1] if b else value

    def inner(p, form):
        total = None
        for a in range(len(p)):
            for b in range(a, len(p)):
                term = p[a] * p[b] * form(a, b)
                if a != b:
                    term = 2.0 * term
                total = term if total is None else total + term
        return total

    def times(p):
        out = [jnp.zeros_like(p[0]) for _ in range(len(p) + 1)]
        for b, v in enumerate(p):
            out[b + 1] = out[b + 1] + step[b] * v
            out[b] = out[b] + centre[b] * v
            if b:
                out[b - 1] = out[b - 1] + step[b - 1] * v
        return out

    one = jnp.ones_like(m00)
    answer = []
    residual = [one]
    direction = [one]
    norm = m00
    for turn in range(4):
        alpha = norm / inner(direction, image)
        answer = answer + [jnp.zeros_like(one)]
        answer = [x + alpha * p for x, p in zip(answer, direction)]
        if turn < 3:
            stepped = times(direction)
            residual = residual + [jnp.zeros_like(one)]
            residual = [r - alpha * v for r, v in zip(residual, stepped)]
            later = inner(residual, gram)
            beta = later / norm
            direction = direction + [jnp.zeros_like(one)]
            direction = [r + beta * p for r, p in zip(residual, direction)]
            norm = later
    return answer


def final_kernel(
    scale,
    arrived_ref,
    strain_ref,
    assign_ref,
    elastic_ref,
    basis_ref,
    u_ref,
    stress_ref,
    out_ref,
):
    groups = arrived_ref.shape[0] // 2
    points = strain_ref.shape[1]
    mine = lax.axis_index("group")
    centre = [basis_ref[n : n + 1, :] for n in range(3)]
    step = [basis_ref[n + 3 : n + 4, :] for n in range(3)]
    both = jnp.sum(arrived_ref[:, 0, : 6 * LANES], axis=0, keepdims=True)
    field = [both[:, c * LANES : (c + 1) * LANES] for c in range(6)]
    field = jnp.concatenate(field + [jnp.zeros((2, LANES), F32)], axis=0)

    def unfold(lines):
        tiles = []
        for t in range(3):
            tile = lines[:, t * LANES : (t + 1) * LANES]
            low = iota(tile.shape, 1) < 64
            tiles.append(jnp.where(low, tile, 0.0))
            tiles.append(jnp.where(low, pltpu.roll(tile, 64, 1), 0.0))
        blank = jnp.zeros((2, LANES), F32)
        return [
            jnp.concatenate([v[h : h + 1] for v in tiles] + [blank], axis=0)
            for h in range(lines.shape[0])
        ]

    lane = iota((8, LANES), 1)
    diagonal = (iota((64, LANES), 0) // 8) == (iota((64, LANES), 1) % 64) // 8

    def tall(x):
        return jnp.concatenate([x] * 8, axis=0)

    def opened(moments):
        high, middle, low = split3(moments + pltpu.roll(moments, 64, 1))
        first = jnp.where(diagonal, tall(jnp.where(lane < 64, high, middle)), 0.0).astype(BF16)
        second = jnp.where(diagonal, tall(jnp.where(lane < 64, high, low)), 0.0).astype(BF16)
        return jnp.concatenate([first, first, second], axis=1)

    def meeting(x):
        high, middle, low = (tall(part) for part in split3(x))
        parts = [high, high, middle, middle, low, high]
        return jnp.concatenate(parts, axis=0).astype(BF16)

    strain = strain_ref[...]
    padded = jnp.concatenate([strain, jnp.zeros((8, LANES - points), F32)], axis=1)
    assign = jnp.concatenate(
        [assign_ref[...], jnp.full((1, LANES - points), -1, jnp.int32)], axis=1
    )
    halves = arrived_ref[:, 0, 6 * LANES :]
    whole = [halves[2 * h : 2 * h + 1] + halves[2 * h + 1 : 2 * h + 2] for h in range(groups)]
    every = unfold(jnp.concatenate(whole, axis=0))
    own = jnp.zeros((8, LANES), F32)
    for h in range(groups):
        own = own + jnp.where(mine == h, every[h], 0.0)
    forces = bdot(opened(own), meeting(field))
    every = jnp.concatenate([opened(v) for v in every], axis=0)
    products = bdot(every, meeting(padded))
    group_of = assign >> 7
    local = jnp.zeros((64, LANES), F32)
    for h in range(groups):
        local = local + jnp.where(group_of == h, products[64 * h : 64 * h + 64], 0.0)

    m = []
    for n in range(8):
        first = jnp.sum(forces[8 * n : 8 * n + 8] * field, axis=0, keepdims=True)
        second = jnp.sum(local[8 * n : 8 * n + 8] * padded, axis=0, keepdims=True)
        m.append(jnp.concatenate([first, second], axis=0))
    answer = coefficients(m, centre, step)

    extra = jnp.zeros((8, LANES), F32)
    for n in range(4):
        extra = extra + answer[n][1:2] * local[8 * n : 8 * n + 8]
    elastic_stress = dot(elastic_ref[...], strain[:6])
    plastic = assign_ref[...] >= 0
    stress_ref[...] = elastic_stress + jnp.where(plastic, extra[:6, :points], 0.0)

    right = jnp.concatenate([(scale * answer[n][0:1]) * field for n in range(4)], axis=0)
    high = right.astype(BF16).astype(F32)
    right = jnp.concatenate([high, high, right - high, jnp.zeros_like(high)], axis=0).astype(BF16)
    for part in range(6):
        rows = slice(512 * part, 512 * part + 512)
        out_ref[rows, :] = bdot(u_ref[rows, :], right)


def call(kernel, outs, *args, scratch=(), own_copies=0):
    vmem = pl.BlockSpec(memory_space=pltpu.VMEM)
    many = isinstance(outs, list)
    out_specs = [vmem] * len(outs) if many else vmem
    scratch = list(scratch)
    if own_copies:
        scratch += [pltpu.VMEM(x.shape, x.dtype) for x in args[:own_copies]]
        scratch += [pltpu.SemaphoreType.DMA((own_copies,))]
    spaces = [pl.BlockSpec(memory_space=pltpu.HBM)] * own_copies + [vmem] * len(args)
    limit = 60 if own_copies else 32
    return pl.pallas_call(
        kernel,
        out_shape=outs,
        in_specs=spaces[: len(args)],
        out_specs=out_specs,
        scratch_shapes=scratch,
        compiler_params=pltpu.CompilerParams(vmem_limit_bytes=limit * 1024 * 1024),
    )(*args)


def arr(*shape, dtype=F32):
    return jax.ShapeDtypeStruct(shape, dtype)


def shifted(x, by):
    devices = lax.axis_size("dev")
    return lax.ppermute(x, "dev", [(i, (i + by) % devices) for i in range(devices)])


def exchange(x, axis, members=None):
    return lax.all_to_all(
        x, axis, split_axis=0, concat_axis=0, tiled=True, axis_index_groups=members
    )


def local(
    displacement,
    connectivity,
    face_nodes,
    strain_map,
    assignment,
    phases,
    load_map,
    stiff_root,
    chain_map,
    bridge_map,
    elastic,
):
    groups = lax.axis_size("group")
    devs = lax.axis_size("dev")
    points = connectivity.shape[1]
    assign = assignment.reshape(1, -1)

    listed = jnp.transpose(face_nodes, (0, 2, 1))
    load = jnp.transpose(load_map, (0, 2, 1))
    labels = jnp.transpose(phases, (0, 2, 1))
    sources = [displacement, listed, load, labels, connectivity, strain_map, assign]
    sources += [stiff_root, chain_map, bridge_map]
    outgoing, packed, rest = call(
        first_kernel,
        [arr(devs, 1, LANES), arr(ROWS, LANES), arr(264 + ROWS, LANES)],
        *sources,
        own_copies=len(sources),
    )
    arrived = exchange(outgoing, "dev")
    near = [shifted(packed, 1), shifted(packed, 2), shifted(packed, -1), shifted(packed, -2)]
    *weights, terms = call(
        tables,
        [
            arr(3 * LANES, 2 * LANES, dtype=BF16),
            arr(3 * LANES, LANES, dtype=BF16),
            arr(9 * LANES, LANES, dtype=BF16),
            arr(8, LANES),
        ],
        rest,
    )
    cand, strain = call(strain_kernel, [arr(1, LANES), arr(8, points)], rest, arrived)
    vectors, send = call(
        krylov_kernel,
        [arr(4, ROWS, LANES), arr(devs // 2, 1, 4 * LANES)],
        rest,
        *near,
        *weights,
        terms,
        cand,
    )
    same_core = [list(range(core, devs, 2)) for core in range(2)]
    same_chip = [
        [g * devs + chip + core for g in range(groups) for core in range(2)]
        for chip in range(0, devs, 2)
    ]
    section = exchange(send, "dev", same_core)
    turned = call(
        turn_kernel,
        arr(BLOCK * BLOCKS, LANES, dtype=BF16),
        vectors,
        scratch=[pltpu.VMEM((BLOCK * BLOCKS, LANES), F32)],
    )
    across = call(section_kernel, arr(2 * groups, 1, 9 * LANES), section)
    gathered = exchange(across, ("group", "dev"), same_chip)
    scale = math.sqrt(BLOCK * devs * BLOCKS)
    stress, fluctuation = call(
        lambda *refs: final_kernel(scale, *refs),
        [arr(6, points), arr(BLOCK * BLOCKS, POINTS)],
        gathered,
        strain,
        assign,
        elastic,
        terms,
        turned,
    )
    return stress, fluctuation.reshape(1, BLOCK, BLOCKS, POINTS)


def solution(mesh):
    in_specs = (
        P(None, ("group", "dev")),
        P(None, ("group", "dev")),
        P(("group", "dev"), None, None),
        P(None, None, ("group", "dev")),
        P(("group", "dev")),
        P("group", None, "dev"),
        P(None, None, "dev"),
        P(),
        P(),
        P(),
        P(),
    )
    out_specs = (P(None, ("group", "dev")), P("group", None, "dev", None))
    return jax.shard_map(local, mesh=mesh, in_specs=in_specs, out_specs=out_specs, check_vma=False)
```

```python
import math

import jax
import jax.numpy as jnp
from jax import lax
from jax.experimental import pallas as pl
from jax.experimental.pallas import tpu as pltpu
from jax.sharding import PartitionSpec as P

BLOCK = 64
IFACE = 16
BLOCKS = 48
POINTS = 128
PLASTIC_CAP = 8
NODES = 256
HALF = BLOCKS // 2
ROWS = HALF * 8
LANES = 128

ridge = 0.5
F32 = jnp.float32
BF16 = jnp.bfloat16
HIGHEST = lax.Precision.HIGHEST


def iota(shape, dim):
    return lax.broadcasted_iota(jnp.int32, shape, dim)


def dot(a, b):
    return jnp.dot(a, b, precision=HIGHEST, preferred_element_type=F32)


def dot_nt(a, b):
    return lax.dot_general(
        a, b, (((1,), (1,)), ((), ())), precision=HIGHEST, preferred_element_type=F32
    )


def dot_tn(a, b):
    return lax.dot_general(
        a, b, (((0,), (0,)), ((), ())), precision=HIGHEST, preferred_element_type=F32
    )


def bdot(a, b):
    return jnp.dot(a, b, preferred_element_type=F32)


def bdot_nt(a, b):
    return lax.dot_general(a, b, (((1,), (1,)), ((), ())), preferred_element_type=F32)


def split2(x):
    high = x.astype(BF16)
    return high, (x - high.astype(F32)).astype(BF16)


def split3(x):
    high = x.astype(BF16).astype(F32)
    rest = x - high
    middle = rest.astype(BF16).astype(F32)
    return high, middle, rest - middle


def spread_rows(values):
    n = values.shape[1]
    rows = []
    for part in split3(values):
        for c in range(3):
            rows.append(jnp.broadcast_to(part[c : c + 1], (16, n)))
        rows.append(jnp.zeros((16, n), F32))
    return jnp.concatenate(rows, axis=0)


def stacked(ref, m):
    high, low = split2(m)
    rows = m.shape[0]
    ref[:rows] = high
    ref[rows : 2 * rows] = high
    ref[2 * rows :] = low


def rough(a, b):
    return bdot(a.astype(BF16), b.astype(BF16))


def pack(load, phase, out_ref):
    for c in range(6):
        out_ref[pl.ds(c, HALF, stride=8), :] = jnp.concatenate(
            [load[pl.ds(c, 1), pl.ds(par, HALF, stride=2), :][0] for par in range(2)], axis=1
        )
    labels = [phase[pl.ds(0, 1), pl.ds(par, HALF, stride=2), :][0] for par in range(2)]
    weights = 1.0 + 2.0 * jnp.concatenate(labels, axis=1).astype(F32)
    out_ref[pl.ds(6, HALF, stride=8), :] = weights
    out_ref[pl.ds(7, HALF, stride=8), :] = jnp.zeros((HALF, LANES), F32)


def faces(disp, listed, out_ref):
    devs = listed.shape[2]
    nodes = disp.shape[1]
    names = jnp.concatenate([listed[0].astype(F32), jnp.zeros((16, LANES - devs), F32)], axis=1)
    names = jnp.concatenate([names, jnp.zeros((LANES - 16, LANES), F32)], axis=0)
    names = jnp.transpose(names)[:devs]
    spread = spread_rows(disp[...])
    spread = jnp.concatenate([spread, jnp.zeros((64, nodes), F32)], axis=0).astype(BF16)
    place = iota((devs, nodes), 1).astype(F32)
    hot = jnp.concatenate(
        [jnp.where(names[:, j : j + 1] == place, 1.0, 0.0) for j in range(16)], axis=0
    ).astype(BF16)
    found = bdot_nt(hot, spread)
    lane = iota((devs, 256), 1) % 16
    total = jnp.zeros((devs, 256), F32)
    for j in range(16):
        total = total + jnp.where(lane == j, found[j * devs : (j + 1) * devs], 0.0)
    near = total[:, :LANES]
    out_ref[:, 0, :] = (near + pltpu.roll(near, 64, 1)) + total[:, LANES:]


def fetch(sources, targets, sems):
    copies = [
        pltpu.make_async_copy(a, b, sems.at[n]) for n, (a, b) in enumerate(zip(sources, targets))
    ]
    for copy in copies:
        copy.start()
    for copy in copies:
        copy.wait()


def own_nodes(disp, conn):
    nodes, points = disp.shape[1], conn.shape[1]
    index = side_by_side(conn[...])
    hot = jnp.where(iota((nodes, 8 * points), 0) == index, 1.0, 0.0).astype(BF16)
    parts = jnp.concatenate(split3(disp[...]) + (jnp.zeros((7, nodes), F32),), axis=0)
    found = bdot(parts.astype(BF16), hot)
    return by_node((found[0:3] + found[3:6]) + found[6:9], points)


def side_by_side(rows):
    return jnp.concatenate([rows[a : a + 1] for a in range(rows.shape[0])], axis=1)


def by_node(sums, points):
    return jnp.concatenate(
        [sums[:, a * points : (a + 1) * points] for a in range(8)],
        axis=0,
    )


def first_kernel(*refs):
    face_ref, pack_ref, rest_ref, *held, sems = refs[10:]
    fetch(refs[:10], held, sems)
    disp, listed, load, phase, conn, maps, assign, root, chain, bridge = held
    faces(disp, listed, face_ref)
    pack(load, phase, pack_ref)
    points = conn.shape[1]
    blank = jnp.zeros((7, points), F32)
    for c in range(6):
        rest_ref[24 * c : 24 * c + 24, :points] = maps[c]
    rest_ref[144:152, :points] = conn[...].astype(F32)
    rest_ref[152:160, :points] = jnp.concatenate([assign[...].astype(F32), blank], axis=0)
    rest_ref[160:184, :points] = own_nodes(disp, conn)
    rest_ref[:184, points:] = jnp.zeros((184, LANES - points), F32)
    rest_ref[184:248, :] = jnp.concatenate([root[...], chain[...]], axis=1)
    wide = jnp.concatenate([bridge[...], jnp.zeros((IFACE, LANES - IFACE), F32)], axis=1)
    rest_ref[248:264, :] = wide
    rest_ref[264:, :] = pack_ref[...]


def tables(rest_ref, w1, wb, w2, basis_ref, strain_part, own_part):
    strain_part[...] = rest_ref[:184]
    own_part[...] = rest_ref[264:]
    root, chain = rest_ref[184:248, :BLOCK], rest_ref[184:248, BLOCK:]
    bridge = rest_ref[248:264, :IFACE]
    zero = jnp.zeros((BLOCK, BLOCK), F32)

    def straight(m):
        return jnp.concatenate(
            [jnp.concatenate([m, zero], axis=1), jnp.concatenate([zero, m], axis=1)], axis=0
        )

    def crossed(m):
        return jnp.concatenate(
            [jnp.concatenate([zero, m], axis=1), jnp.concatenate([m, zero], axis=1)], axis=0
        )

    gap = BLOCK - IFACE
    wide = jnp.concatenate([bridge, jnp.zeros((IFACE, gap), F32)], axis=1)
    upper = jnp.concatenate([jnp.zeros((gap, BLOCK), F32), wide], axis=0)
    roots, chains, bridges = straight(root), crossed(chain), straight(upper)
    stacked(w1, jnp.concatenate([jnp.transpose(roots), jnp.transpose(chains)], axis=1))
    stacked(wb, jnp.transpose(bridges))
    stacked(w2, jnp.concatenate([roots, -chains, -bridges], axis=0))

    size = 2 * BLOCK
    diagonal = iota((size, size), 0) == iota((size, size), 1)
    edge = jnp.where(diagonal, 1.0, 0.0) - chains
    face = jnp.where(diagonal & (iota((size, size), 0) % BLOCK >= gap), 1.0, 0.0) - bridges
    tall = jnp.concatenate([2.0**0.5 * roots, edge, face], axis=0)
    model = rough(jnp.transpose(tall), tall)
    model = model + jnp.where(diagonal, ridge, 0.0)

    def inner(p, q):
        return jnp.sum(jnp.sum(p * q, axis=1, keepdims=True), axis=0, keepdims=True)

    now = jnp.where(diagonal, size**-0.5, 0.0)
    past, image = None, size**-0.5 * model
    centres, steps = [], []
    for n in range(3):
        if n:
            image = rough(model, now)
        centre = inner(now, image)
        rest = image - centre * now
        if n:
            rest = rest - steps[-1] * past
        step = jnp.maximum(jnp.sqrt(inner(rest, rest)), 0.01 * centres[0] if n else 0.01 * centre)
        centres.append(centre)
        steps.append(step)
        past, now = now, rest / step
    row = iota((8, LANES), 0)
    table = jnp.zeros((8, LANES), F32)
    for n, value in enumerate(centres + steps):
        table = jnp.where(row == n, value, table)
    basis_ref[...] = table


def krylov_kernel(
    own_ref, m1_ref, m2_ref, p1_ref, p2_ref, w1, wb, w2, basis_ref, cand_ref, u_ref, send_ref
):
    centre = [basis_ref[n : n + 1, :] for n in range(3)]
    step = [basis_ref[n + 3 : n + 4, :] for n in range(3)]
    inverse = [1.0 / v for v in step]

    def lanes(x):
        return iota(x.shape, 1)

    def weights_of(x):
        w = x.reshape(HALF, 8, LANES)[:, 6:7, :]
        return jnp.broadcast_to(w, (HALF, 8, LANES)).reshape(ROWS, LANES)

    def parts(x):
        high, low = split2(x)
        return jnp.concatenate([high, low, high], axis=1)

    def stage(x, w):
        return bdot(parts(x), w[...])

    def blocks(x):
        return [x[n : n + ROWS] for n in range(0, x.shape[0], ROWS)]

    def up(x):
        parts = [p for v in blocks(x) for p in (v[8:], v[:8])]
        return jnp.concatenate(parts, axis=0)

    def down(x):
        parts = [p for v in blocks(x) for p in (v[ROWS - 8 :], v[: ROWS - 8])]
        return jnp.concatenate(parts, axis=0)

    def halves(x, w, split):
        both = bdot(split, w1[...])
        lifted = both[:, :LANES]
        mixed = both[:, LANES:]
        edge = x - jnp.where(lanes(x) < BLOCK, mixed, up(mixed))
        return lifted, w * lifted, edge

    def face(x, following):
        return jnp.where(lanes(x) % BLOCK >= BLOCK - IFACE, x, 0.0) - following

    def apply(x, w, split, f, f_before):
        _, weighted, edge = halves(x, w, split)
        shifted = jnp.where(lanes(x) < BLOCK, edge, down(edge))
        left = jnp.concatenate([weighted, shifted, f_before], axis=1)
        return ridge * x + edge + f + stage(left, w2)

    zero = jnp.zeros((ROWS, LANES), F32)
    near = [m1_ref[...], own_ref[...], p1_ref[...], p2_ref[...]]
    w = jnp.concatenate([weights_of(x) for x in near], axis=0)

    x0 = jnp.concatenate(near, axis=0)
    known = jnp.concatenate([m2_ref[...], x0[: 3 * ROWS]], axis=0)
    split = parts(x0)
    f = jnp.concatenate([face(known, bdot(split, wb[...])), zero], axis=0)
    image = apply(x0, w, split, f[ROWS:], f[: 4 * ROWS])
    x1 = inverse[0] * (image - centre[0] * x0)

    split = parts(x1)
    f = jnp.concatenate([zero, face(x1[: 3 * ROWS], bdot(split[ROWS:], wb[...]))], axis=0)
    now, past = x1[: 3 * ROWS], x0[: 3 * ROWS]
    image = apply(now, w[: 3 * ROWS], split[: 3 * ROWS], f[ROWS:], f[: 3 * ROWS])
    x2 = inverse[1] * (image - centre[1] * now - step[0] * past)

    split = parts(x2[ROWS:])
    f = jnp.concatenate([face(x2[: 2 * ROWS], bdot(split, wb[...])), zero], axis=0)
    now, past = x2[ROWS:], x1[ROWS : 3 * ROWS]
    image = apply(now, w[ROWS : 3 * ROWS], split, f[ROWS:], f[: 2 * ROWS])
    x3 = inverse[2] * (image - centre[2] * now - step[1] * past)

    own = x3[:ROWS]
    lifted, weighted, edge = halves(own, w[ROWS : 2 * ROWS], parts(own))
    f3 = face(own, stage(x3[ROWS:], wb))

    basis = [near[1], x1[ROWS : 2 * ROWS], x2[ROWS : 2 * ROWS], own]
    for n in range(4):
        u_ref[n] = basis[n]

    def long(x):
        return jnp.concatenate([x[8 * k : 8 * k + 8] for k in range(HALF)], axis=1)

    tall = jnp.concatenate([long(x) for x in basis + [lifted, weighted, edge, f3]], axis=0)
    high = tall.astype(BF16).astype(F32)
    both = jnp.concatenate([high, tall - high], axis=0).astype(BF16)
    product = bdot_nt(both, both)
    product = product[:64] + product[64:]
    product = product + pltpu.roll(product, 64, 1)

    def pair(a, b, to):
        return pltpu.roll(product[8 * a : 8 * a + 8], (8 * (to - b)) % LANES, 1)

    at = iota((8, LANES), 1) // 8
    energy = 0.5 * pair(3, 3, 7) + (pair(4, 5, 7) + pair(6, 6, 7) + pair(7, 7, 7))
    moments = jnp.where(at < 4, product[:8], 0.0)
    moments = jnp.where(at == 4, pair(2, 2, 4), moments)
    moments = jnp.where(at == 5, pair(2, 3, 5), moments)
    moments = jnp.where(at == 6, pair(3, 3, 6), moments)
    moments = jnp.where(at == 7, energy, moments)
    line = [
        moments[2 * t : 2 * t + 1] + pltpu.roll(moments[2 * t + 1 : 2 * t + 2], 64, 1)
        for t in range(3)
    ]
    line = jnp.concatenate(line + [cand_ref[...]], axis=1)
    send_ref[:, 0, :] = jnp.broadcast_to(line, (send_ref.shape[0], 4 * LANES))


def turn_kernel(u_ref, out_ref, wide):
    for k in range(HALF):
        rows = jnp.concatenate([u_ref[n, 8 * k : 8 * k + 8, :] for n in range(4)], axis=0)
        high = rows.astype(BF16).astype(F32)
        stack = jnp.concatenate([high, rows - high, high, jnp.zeros_like(high)], axis=0)
        turned = jnp.transpose(stack)
        wide[pl.ds(2 * k, BLOCK, stride=BLOCKS), :] = turned[:BLOCK]
        wide[pl.ds(2 * k + 1, BLOCK, stride=BLOCKS), :] = turned[BLOCK:]
    out_ref[...] = wide[...].astype(BF16)


def strain_kernel(rest_ref, arrived_ref, cand_ref, strain_ref):
    devs = arrived_ref.shape[0]
    points = strain_ref.shape[1]
    index = side_by_side(rest_ref[144:152, :points].astype(jnp.int32))
    refs = 8 * points
    partner = (index - NODES) >> 4
    other = jnp.where(iota((devs, refs), 0) == partner, 1.0, 0.0).astype(BF16)
    ghost = jnp.transpose(arrived_ref[:, 0, :])[:64]
    ghost = jnp.concatenate(split3(ghost), axis=0).astype(BF16)
    found = bdot(ghost, other)
    found = (found[:64] + found[64:128]) + found[128:]
    found = jnp.where(iota((64, refs), 0) % 16 == index % 16, found, 0.0)
    sums = [jnp.sum(found[16 * c : 16 * c + 16], axis=0, keepdims=True) for c in range(3)]
    nodal = by_node(jnp.concatenate(sums, axis=0), points) + rest_ref[160:184, :points]
    strain = jnp.concatenate(
        [
            jnp.sum(rest_ref[24 * c : 24 * c + 24, :points] * nodal, axis=0, keepdims=True)
            for c in range(6)
        ],
        axis=0,
    )
    strain_ref[...] = jnp.concatenate([strain, jnp.zeros((2, points), F32)], axis=0)

    assign = rest_ref[152:153, :points]
    plastic = assign >= 0.0
    flags = jnp.where(plastic, 1.0, 0.0)
    before = jnp.where(iota((points, points), 0) < iota((points, points), 1), 1.0, 0.0)
    rank = bdot(jnp.broadcast_to(flags, (8, points)).astype(BF16), before.astype(BF16))
    pick = jnp.where(plastic & (rank == iota((8, points), 0).astype(F32)), 1.0, 0.0)
    values = jnp.concatenate(
        [
            strain,
            assign + 1.0,
            jnp.zeros((LANES - 7, points), F32),
        ],
        axis=0,
    )
    chosen = dot_nt(pick, values)
    line = chosen[0:1]
    for slot in range(1, PLASTIC_CAP):
        line = line + pltpu.roll(chosen[slot : slot + 1], 8 * slot, 1)
    cand_ref[...] = line


def section_kernel(arrived_ref, send_ref):
    devs = arrived_ref.shape[0]
    groups = send_ref.shape[0] // 2
    total = jnp.sum(arrived_ref[:, 0, : 3 * LANES], axis=0, keepdims=True)
    cand = arrived_ref[:, 0, 3 * LANES :]
    turned = jnp.transpose(jnp.concatenate([cand] * (LANES // devs), axis=0))
    line = jnp.concatenate([turned[8 * n : 8 * n + 8, :devs] for n in range(PLASTIC_CAP)], axis=1)
    width = PLASTIC_CAP * devs
    target = line[6:7].astype(jnp.int32) - 1
    row = iota((64, width), 0)
    keep = ((target >> 7) == row // 8) & (row % 8 < 6)
    left = [
        jnp.where(keep, jnp.concatenate([part] * 8, axis=0), 0.0).astype(BF16)
        for part in split3(line)
    ]
    hot = jnp.where(iota((POINTS, width), 0) == (target & (POINTS - 1)), 1.0, 0.0).astype(BF16)
    dense = bdot_nt(jnp.concatenate(left, axis=0), hot)
    dense = (dense[:64] + dense[64:128]) + dense[128:]
    for h in range(groups):
        for core in range(2):
            for c in range(6):
                lanes = slice(c * LANES, (c + 1) * LANES)
                send_ref[2 * h + core, :, lanes] = dense[8 * h + c : 8 * h + c + 1]
            send_ref[2 * h + core, :, 6 * LANES :] = total


def coefficients(m, centre, step):
    m00, m01, m02, m03, m22, m23, m33, energy = m
    m11 = m00 + (step[1] * m02 + (centre[1] - centre[0]) * m01) / step[0]
    m12 = (step[2] * m03 + (centre[2] - centre[0]) * m02 + step[1] * m01) / step[0]
    m13 = (step[1] * (m22 - m11) + (centre[1] - centre[2]) * m12 + step[0] * m02) / step[2]
    products = [
        [m00, m01, m02, m03],
        [m01, m11, m12, m13],
        [m02, m12, m22, m23],
        [m03, m13, m23, m33],
    ]

    def gram(a, b):
        return products[a][b]

    def image(a, b):
        a, b = max(a, b), min(a, b)
        if b == 3:
            return energy
        value = step[b] * products[a][b + 1] + centre[b] * products[a][b]
        return value + step[b - 1] * products[a][b - 1] if b else value

    def inner(p, form):
        total = None
        for a in range(len(p)):
            for b in range(a, len(p)):
                term = p[a] * p[b] * form(a, b)
                if a != b:
                    term = 2.0 * term
                total = term if total is None else total + term
        return total

    def times(p):
        out = [jnp.zeros_like(p[0]) for _ in range(len(p) + 1)]
        for b, v in enumerate(p):
            out[b + 1] = out[b + 1] + step[b] * v
            out[b] = out[b] + centre[b] * v
            if b:
                out[b - 1] = out[b - 1] + step[b - 1] * v
        return out

    one = jnp.ones_like(m00)
    answer = []
    residual = [one]
    direction = [one]
    norm = m00
    for turn in range(4):
        alpha = norm / inner(direction, image)
        answer = answer + [jnp.zeros_like(one)]
        answer = [x + alpha * p for x, p in zip(answer, direction)]
        if turn < 3:
            stepped = times(direction)
            residual = residual + [jnp.zeros_like(one)]
            residual = [r - alpha * v for r, v in zip(residual, stepped)]
            later = inner(residual, gram)
            beta = later / norm
            direction = direction + [jnp.zeros_like(one)]
            direction = [r + beta * p for r, p in zip(residual, direction)]
            norm = later
    return answer


def final_kernel(
    scale,
    arrived_ref,
    strain_ref,
    assign_ref,
    elastic_ref,
    basis_ref,
    u_ref,
    stress_ref,
    out_ref,
):
    groups = arrived_ref.shape[0] // 2
    points = strain_ref.shape[1]
    mine = lax.axis_index("group")
    centre = [basis_ref[n : n + 1, :] for n in range(3)]
    step = [basis_ref[n + 3 : n + 4, :] for n in range(3)]
    both = jnp.sum(arrived_ref[:, 0, : 6 * LANES], axis=0, keepdims=True)
    field = [both[:, c * LANES : (c + 1) * LANES] for c in range(6)]
    field = jnp.concatenate(field + [jnp.zeros((2, LANES), F32)], axis=0)

    def unfold(lines):
        tiles = []
        for t in range(3):
            tile = lines[:, t * LANES : (t + 1) * LANES]
            low = iota(tile.shape, 1) < 64
            tiles.append(jnp.where(low, tile, 0.0))
            tiles.append(jnp.where(low, pltpu.roll(tile, 64, 1), 0.0))
        blank = jnp.zeros((2, LANES), F32)
        return [
            jnp.concatenate([v[h : h + 1] for v in tiles] + [blank], axis=0)
            for h in range(lines.shape[0])
        ]

    lane = iota((8, LANES), 1)
    diagonal = (iota((64, LANES), 0) // 8) == (iota((64, LANES), 1) % 64) // 8

    def tall(x):
        return jnp.concatenate([x] * 8, axis=0)

    def opened(moments):
        high, middle, low = split3(moments + pltpu.roll(moments, 64, 1))
        first = jnp.where(diagonal, tall(jnp.where(lane < 64, high, middle)), 0.0).astype(BF16)
        second = jnp.where(diagonal, tall(jnp.where(lane < 64, high, low)), 0.0).astype(BF16)
        return jnp.concatenate([first, first, second], axis=1)

    def meeting(x):
        high, middle, low = (tall(part) for part in split3(x))
        parts = [high, high, middle, middle, low, high]
        return jnp.concatenate(parts, axis=0).astype(BF16)

    strain = strain_ref[...]
    padded = jnp.concatenate([strain, jnp.zeros((8, LANES - points), F32)], axis=1)
    assign = jnp.concatenate(
        [assign_ref[...], jnp.full((1, LANES - points), -1, jnp.int32)], axis=1
    )
    halves = arrived_ref[:, 0, 6 * LANES :]
    whole = [halves[2 * h : 2 * h + 1] + halves[2 * h + 1 : 2 * h + 2] for h in range(groups)]
    every = unfold(jnp.concatenate(whole, axis=0))
    own = jnp.zeros((8, LANES), F32)
    for h in range(groups):
        own = own + jnp.where(mine == h, every[h], 0.0)
    forces = bdot(opened(own), meeting(field))
    every = jnp.concatenate([opened(v) for v in every], axis=0)
    products = bdot(every, meeting(padded))
    group_of = assign >> 7
    local = jnp.zeros((64, LANES), F32)
    for h in range(groups):
        local = local + jnp.where(group_of == h, products[64 * h : 64 * h + 64], 0.0)

    m = []
    for n in range(8):
        first = jnp.sum(forces[8 * n : 8 * n + 8] * field, axis=0, keepdims=True)
        second = jnp.sum(local[8 * n : 8 * n + 8] * padded, axis=0, keepdims=True)
        m.append(jnp.concatenate([first, second], axis=0))
    answer = coefficients(m, centre, step)

    extra = jnp.zeros((8, LANES), F32)
    for n in range(4):
        extra = extra + answer[n][1:2] * local[8 * n : 8 * n + 8]
    elastic_stress = dot(elastic_ref[...], strain[:6])
    plastic = assign_ref[...] >= 0
    stress_ref[...] = elastic_stress + jnp.where(plastic, extra[:6, :points], 0.0)

    right = jnp.concatenate([(scale * answer[n][0:1]) * field for n in range(4)], axis=0)
    high = right.astype(BF16).astype(F32)
    right = jnp.concatenate([high, high, right - high, jnp.zeros_like(high)], axis=0).astype(BF16)
    for part in range(6):
        rows = slice(512 * part, 512 * part + 512)
        out_ref[rows, :] = bdot(u_ref[rows, :], right)


def call(kernel, outs, *args, scratch=(), own_copies=0, cost=None):
    vmem = pl.BlockSpec(memory_space=pltpu.VMEM)
    many = isinstance(outs, list)
    out_specs = [vmem] * len(outs) if many else vmem
    scratch = list(scratch)
    if own_copies:
        scratch += [pltpu.VMEM(x.shape, x.dtype) for x in args[:own_copies]]
        scratch += [pltpu.SemaphoreType.DMA((own_copies,))]
    spaces = [pl.BlockSpec(memory_space=pltpu.HBM)] * own_copies + [vmem] * len(args)
    limit = 60 if own_copies else 32
    return pl.pallas_call(
        kernel,
        out_shape=outs,
        in_specs=spaces[: len(args)],
        out_specs=out_specs,
        scratch_shapes=scratch,
        cost_estimate=cost,
        compiler_params=pltpu.CompilerParams(vmem_limit_bytes=limit * 1024 * 1024),
    )(*args)


def arr(*shape, dtype=F32):
    return jax.ShapeDtypeStruct(shape, dtype)


def shifted(x, by):
    devices = lax.axis_size("dev")
    return lax.ppermute(x, "dev", [(i, (i + by) % devices) for i in range(devices)])


def exchange(x, axis, members=None):
    return lax.all_to_all(
        x, axis, split_axis=0, concat_axis=0, tiled=True, axis_index_groups=members
    )


def local(
    displacement,
    connectivity,
    face_nodes,
    strain_map,
    assignment,
    phases,
    load_map,
    stiff_root,
    chain_map,
    bridge_map,
    elastic,
):
    groups = lax.axis_size("group")
    devs = lax.axis_size("dev")
    points = connectivity.shape[1]
    assign = assignment.reshape(1, -1)

    listed = jnp.transpose(face_nodes, (0, 2, 1))
    load = jnp.transpose(load_map, (0, 2, 1))
    labels = jnp.transpose(phases, (0, 2, 1))
    sources = [displacement, listed, load, labels, connectivity, strain_map, assign]
    sources += [stiff_root, chain_map, bridge_map]
    outgoing, packed, rest = call(
        first_kernel,
        [arr(devs, 1, LANES), arr(ROWS, LANES), arr(264 + ROWS, LANES)],
        *sources,
        own_copies=len(sources),
    )
    arrived = exchange(outgoing, "dev")
    near = [shifted(packed, 1), shifted(packed, 2), shifted(packed, -1), shifted(packed, -2)]
    *weights, terms, strain_part, own_part = call(
        tables,
        [
            arr(3 * LANES, 2 * LANES, dtype=BF16),
            arr(3 * LANES, LANES, dtype=BF16),
            arr(9 * LANES, LANES, dtype=BF16),
            arr(8, LANES),
            arr(184, LANES),
            arr(ROWS, LANES),
        ],
        rest,
    )
    cand, strain = call(
        strain_kernel,
        [arr(1, LANES), arr(8, points)],
        strain_part,
        arrived,
        cost=pl.CostEstimate(flops=2 * 10**10, bytes_accessed=0, transcendentals=0),
    )
    vectors, send = call(
        krylov_kernel,
        [arr(4, ROWS, LANES), arr(devs // 2, 1, 4 * LANES)],
        own_part,
        *near,
        *weights,
        terms,
        cand,
    )
    same_core = [list(range(core, devs, 2)) for core in range(2)]
    same_chip = [
        [g * devs + chip + core for g in range(groups) for core in range(2)]
        for chip in range(0, devs, 2)
    ]
    section = exchange(send, "dev", same_core)
    turned = call(
        turn_kernel,
        arr(BLOCK * BLOCKS, LANES, dtype=BF16),
        vectors,
        scratch=[pltpu.VMEM((BLOCK * BLOCKS, LANES), F32)],
    )
    across = call(section_kernel, arr(2 * groups, 1, 9 * LANES), section)
    gathered = exchange(across, ("group", "dev"), same_chip)
    scale = math.sqrt(BLOCK * devs * BLOCKS)
    stress, fluctuation = call(
        lambda *refs: final_kernel(scale, *refs),
        [arr(6, points), arr(BLOCK * BLOCKS, POINTS)],
        gathered,
        strain,
        assign,
        elastic,
        terms,
        turned,
    )
    return stress, fluctuation.reshape(1, BLOCK, BLOCKS, POINTS)


def solution(mesh):
    in_specs = (
        P(None, ("group", "dev")),
        P(None, ("group", "dev")),
        P(("group", "dev"), None, None),
        P(None, None, ("group", "dev")),
        P(("group", "dev")),
        P("group", None, "dev"),
        P(None, None, "dev"),
        P(),
        P(),
        P(),
        P(),
    )
    out_specs = (P(None, ("group", "dev")), P("group", None, "dev", None))
    return jax.shard_map(local, mesh=mesh, in_specs=in_specs, out_specs=out_specs, check_vma=False)
```

```python
import math

import jax
import jax.numpy as jnp
from jax import lax
from jax.experimental import pallas as pl
from jax.experimental.pallas import tpu as pltpu
from jax.sharding import PartitionSpec as P

BLOCK = 64
IFACE = 16
BLOCKS = 48
POINTS = 128
PLASTIC_CAP = 8
NODES = 256
HALF = BLOCKS // 2
ROWS = HALF * 8
LANES = 128

ridge = 0.5
F32 = jnp.float32
BF16 = jnp.bfloat16
HIGHEST = lax.Precision.HIGHEST


def iota(shape, dim):
    return lax.broadcasted_iota(jnp.int32, shape, dim)


def dot(a, b):
    return jnp.dot(a, b, precision=HIGHEST, preferred_element_type=F32)


def dot_nt(a, b):
    return lax.dot_general(
        a, b, (((1,), (1,)), ((), ())), precision=HIGHEST, preferred_element_type=F32
    )


def dot_tn(a, b):
    return lax.dot_general(
        a, b, (((0,), (0,)), ((), ())), precision=HIGHEST, preferred_element_type=F32
    )


def bdot(a, b):
    return jnp.dot(a, b, preferred_element_type=F32)


def bdot_nt(a, b):
    return lax.dot_general(a, b, (((1,), (1,)), ((), ())), preferred_element_type=F32)


def split2(x):
    high = x.astype(BF16)
    return high, (x - high.astype(F32)).astype(BF16)


def split3(x):
    high = x.astype(BF16).astype(F32)
    rest = x - high
    middle = rest.astype(BF16).astype(F32)
    return high, middle, rest - middle


def spread_rows(values):
    n = values.shape[1]
    rows = []
    for part in split3(values):
        for c in range(3):
            rows.append(jnp.broadcast_to(part[c : c + 1], (16, n)))
        rows.append(jnp.zeros((16, n), F32))
    return jnp.concatenate(rows, axis=0)


def stacked(ref, m):
    high, low = split2(m)
    rows = m.shape[0]
    ref[:rows] = high
    ref[rows : 2 * rows] = high
    ref[2 * rows :] = low


def rough(a, b):
    return bdot(a.astype(BF16), b.astype(BF16))


def pack(load, phase, out_ref):
    for c in range(6):
        out_ref[pl.ds(c, HALF, stride=8), :] = jnp.concatenate(
            [load[pl.ds(c, 1), pl.ds(par, HALF, stride=2), :][0] for par in range(2)], axis=1
        )
    labels = [phase[pl.ds(0, 1), pl.ds(par, HALF, stride=2), :][0] for par in range(2)]
    weights = 1.0 + 2.0 * jnp.concatenate(labels, axis=1).astype(F32)
    out_ref[pl.ds(6, HALF, stride=8), :] = weights
    out_ref[pl.ds(7, HALF, stride=8), :] = jnp.zeros((HALF, LANES), F32)


def faces(disp, listed, out_ref):
    devs = listed.shape[2]
    nodes = disp.shape[1]
    names = jnp.concatenate([listed[0].astype(F32), jnp.zeros((16, LANES - devs), F32)], axis=1)
    names = jnp.concatenate([names, jnp.zeros((LANES - 16, LANES), F32)], axis=0)
    names = jnp.transpose(names)[:devs]
    spread = spread_rows(disp[...])
    spread = jnp.concatenate([spread, jnp.zeros((64, nodes), F32)], axis=0).astype(BF16)
    place = iota((devs, nodes), 1).astype(F32)
    hot = jnp.concatenate(
        [jnp.where(names[:, j : j + 1] == place, 1.0, 0.0) for j in range(16)], axis=0
    ).astype(BF16)
    found = bdot_nt(hot, spread)
    lane = iota((devs, 256), 1) % 16
    total = jnp.zeros((devs, 256), F32)
    for j in range(16):
        total = total + jnp.where(lane == j, found[j * devs : (j + 1) * devs], 0.0)
    near = total[:, :LANES]
    out_ref[:, 0, :] = (near + pltpu.roll(near, 64, 1)) + total[:, LANES:]


def fetch(sources, targets, sems):
    copies = [
        pltpu.make_async_copy(a, b, sems.at[n]) for n, (a, b) in enumerate(zip(sources, targets))
    ]
    for copy in copies:
        copy.start()
    for copy in copies:
        copy.wait()


QUARTER = ROWS // 4


def edge_rows(x):
    lane = iota((QUARTER, LANES), 1) // IFACE
    out = jnp.zeros((QUARTER, LANES), F32)
    for q in range(4):
        rows = x[QUARTER * q : QUARTER * (q + 1)]
        out = jnp.where(lane == 2 * q, pltpu.roll(rows, (32 * q - 48) % LANES, 1), out)
        out = jnp.where(lane == 2 * q + 1, pltpu.roll(rows, (32 * q - 96) % LANES, 1), out)
    return out


def spread_edge(x):
    lane = iota((QUARTER, LANES), 1) // IFACE
    out = []
    for q in range(4):
        first = pltpu.roll(x, (48 - 32 * q) % LANES, 1)
        second = pltpu.roll(x, (96 - 32 * q) % LANES, 1)
        out.append(jnp.where(lane == 3, first, jnp.where(lane == 7, second, 0.0)))
    return jnp.concatenate(out, axis=0)


def own_nodes(disp, conn):
    nodes, points = disp.shape[1], conn.shape[1]
    index = side_by_side(conn[...])
    hot = jnp.where(iota((nodes, 8 * points), 0) == index, 1.0, 0.0).astype(BF16)
    parts = jnp.concatenate(split3(disp[...]) + (jnp.zeros((7, nodes), F32),), axis=0)
    found = bdot(parts.astype(BF16), hot)
    return by_node((found[0:3] + found[3:6]) + found[6:9], points)


def side_by_side(rows):
    return jnp.concatenate([rows[a : a + 1] for a in range(rows.shape[0])], axis=1)


def by_node(sums, points):
    return jnp.concatenate(
        [sums[:, a * points : (a + 1) * points] for a in range(8)],
        axis=0,
    )


def first_kernel(*refs):
    face_ref, pack_ref, edge_ref, rest_ref, *held, sems = refs[10:]
    fetch(refs[:10], held, sems)
    disp, listed, load, phase, conn, maps, assign, root, chain, bridge = held
    faces(disp, listed, face_ref)
    pack(load, phase, pack_ref)
    edge_ref[...] = edge_rows(pack_ref[...])
    points = conn.shape[1]
    blank = jnp.zeros((7, points), F32)
    for c in range(6):
        rest_ref[24 * c : 24 * c + 24, :points] = maps[c]
    rest_ref[144:152, :points] = conn[...].astype(F32)
    rest_ref[152:160, :points] = jnp.concatenate([assign[...].astype(F32), blank], axis=0)
    rest_ref[160:184, :points] = own_nodes(disp, conn)
    rest_ref[:184, points:] = jnp.zeros((184, LANES - points), F32)
    rest_ref[184:248, :] = jnp.concatenate([root[...], chain[...]], axis=1)
    wide = jnp.concatenate([bridge[...], jnp.zeros((IFACE, LANES - IFACE), F32)], axis=1)
    rest_ref[248:264, :] = wide
    rest_ref[264:, :] = pack_ref[...]


def tables(rest_ref, w1, wb, w2, basis_ref, strain_part, own_part):
    strain_part[...] = rest_ref[:184]
    own_part[...] = rest_ref[264:]
    root, chain = rest_ref[184:248, :BLOCK], rest_ref[184:248, BLOCK:]
    bridge = rest_ref[248:264, :IFACE]
    zero = jnp.zeros((BLOCK, BLOCK), F32)

    def straight(m):
        return jnp.concatenate(
            [jnp.concatenate([m, zero], axis=1), jnp.concatenate([zero, m], axis=1)], axis=0
        )

    def crossed(m):
        return jnp.concatenate(
            [jnp.concatenate([zero, m], axis=1), jnp.concatenate([m, zero], axis=1)], axis=0
        )

    gap = BLOCK - IFACE
    wide = jnp.concatenate([bridge, jnp.zeros((IFACE, gap), F32)], axis=1)
    upper = jnp.concatenate([jnp.zeros((gap, BLOCK), F32), wide], axis=0)
    roots, chains, bridges = straight(root), crossed(chain), straight(upper)
    stacked(w1, jnp.concatenate([jnp.transpose(roots), jnp.transpose(chains)], axis=1))
    stacked(wb, jnp.transpose(bridges))
    stacked(w2, jnp.concatenate([roots, -chains, -bridges], axis=0))

    size = 2 * BLOCK
    diagonal = iota((size, size), 0) == iota((size, size), 1)
    edge = jnp.where(diagonal, 1.0, 0.0) - chains
    face = jnp.where(diagonal & (iota((size, size), 0) % BLOCK >= gap), 1.0, 0.0) - bridges
    tall = jnp.concatenate([2.0**0.5 * roots, edge, face], axis=0)
    model = rough(jnp.transpose(tall), tall)
    model = model + jnp.where(diagonal, ridge, 0.0)

    def inner(p, q):
        return jnp.sum(jnp.sum(p * q, axis=1, keepdims=True), axis=0, keepdims=True)

    now = jnp.where(diagonal, size**-0.5, 0.0)
    past, image = None, size**-0.5 * model
    centres, steps = [], []
    for n in range(3):
        if n:
            image = rough(model, now)
        centre = inner(now, image)
        rest = image - centre * now
        if n:
            rest = rest - steps[-1] * past
        step = jnp.maximum(jnp.sqrt(inner(rest, rest)), 0.01 * centres[0] if n else 0.01 * centre)
        centres.append(centre)
        steps.append(step)
        past, now = now, rest / step
    row = iota((8, LANES), 0)
    table = jnp.zeros((8, LANES), F32)
    for n, value in enumerate(centres + steps):
        table = jnp.where(row == n, value, table)
    basis_ref[...] = table


def krylov_kernel(
    own_ref, m1_ref, m2_ref, p1_ref, p2_ref, w1, wb, w2, basis_ref, cand_ref, u_ref, send_ref
):
    centre = [basis_ref[n : n + 1, :] for n in range(3)]
    step = [basis_ref[n + 3 : n + 4, :] for n in range(3)]
    inverse = [1.0 / v for v in step]

    def lanes(x):
        return iota(x.shape, 1)

    def weights_of(x):
        w = x.reshape(HALF, 8, LANES)[:, 6:7, :]
        return jnp.broadcast_to(w, (HALF, 8, LANES)).reshape(ROWS, LANES)

    def parts(x):
        high, low = split2(x)
        return jnp.concatenate([high, low, high], axis=1)

    def stage(x, w):
        return bdot(parts(x), w[...])

    def blocks(x):
        return [x[n : n + ROWS] for n in range(0, x.shape[0], ROWS)]

    def up(x):
        parts = [p for v in blocks(x) for p in (v[8:], v[:8])]
        return jnp.concatenate(parts, axis=0)

    def down(x):
        parts = [p for v in blocks(x) for p in (v[ROWS - 8 :], v[: ROWS - 8])]
        return jnp.concatenate(parts, axis=0)

    def halves(x, w, split):
        both = bdot(split, w1[...])
        lifted = both[:, :LANES]
        mixed = both[:, LANES:]
        edge = x - jnp.where(lanes(x) < BLOCK, mixed, up(mixed))
        return lifted, w * lifted, edge

    def face(x, following):
        return jnp.where(lanes(x) % BLOCK >= BLOCK - IFACE, x, 0.0) - following

    def apply(x, w, split, f, f_before):
        _, weighted, edge = halves(x, w, split)
        shifted = jnp.where(lanes(x) < BLOCK, edge, down(edge))
        left = jnp.concatenate([weighted, shifted, f_before], axis=1)
        return ridge * x + edge + f + stage(left, w2)

    zero = jnp.zeros((ROWS, LANES), F32)
    near = [m1_ref[...], own_ref[...], p1_ref[...], p2_ref[...]]
    w = jnp.concatenate([weights_of(x) for x in near], axis=0)

    x0 = jnp.concatenate(near, axis=0)
    known = jnp.concatenate([spread_edge(m2_ref[...]), x0[: 3 * ROWS]], axis=0)
    split = parts(x0)
    f = jnp.concatenate([face(known, bdot(split, wb[...])), zero], axis=0)
    image = apply(x0, w, split, f[ROWS:], f[: 4 * ROWS])
    x1 = inverse[0] * (image - centre[0] * x0)

    split = parts(x1)
    f = jnp.concatenate([zero, face(x1[: 3 * ROWS], bdot(split[ROWS:], wb[...]))], axis=0)
    now, past = x1[: 3 * ROWS], x0[: 3 * ROWS]
    image = apply(now, w[: 3 * ROWS], split[: 3 * ROWS], f[ROWS:], f[: 3 * ROWS])
    x2 = inverse[1] * (image - centre[1] * now - step[0] * past)

    split = parts(x2[ROWS:])
    f = jnp.concatenate([face(x2[: 2 * ROWS], bdot(split, wb[...])), zero], axis=0)
    now, past = x2[ROWS:], x1[ROWS : 3 * ROWS]
    image = apply(now, w[ROWS : 3 * ROWS], split, f[ROWS:], f[: 2 * ROWS])
    x3 = inverse[2] * (image - centre[2] * now - step[1] * past)

    own = x3[:ROWS]
    lifted, weighted, edge = halves(own, w[ROWS : 2 * ROWS], parts(own))
    f3 = face(own, stage(x3[ROWS:], wb))

    basis = [near[1], x1[ROWS : 2 * ROWS], x2[ROWS : 2 * ROWS], own]
    for n in range(4):
        u_ref[n] = basis[n]

    def long(x):
        return jnp.concatenate([x[8 * k : 8 * k + 8] for k in range(HALF)], axis=1)

    tall = jnp.concatenate([long(x) for x in basis + [lifted, weighted, edge, f3]], axis=0)
    high = tall.astype(BF16).astype(F32)
    both = jnp.concatenate([high, tall - high], axis=0).astype(BF16)
    product = bdot_nt(both, both)
    product = product[:64] + product[64:]
    product = product + pltpu.roll(product, 64, 1)

    def pair(a, b, to):
        return pltpu.roll(product[8 * a : 8 * a + 8], (8 * (to - b)) % LANES, 1)

    at = iota((8, LANES), 1) // 8
    energy = 0.5 * pair(3, 3, 7) + (pair(4, 5, 7) + pair(6, 6, 7) + pair(7, 7, 7))
    moments = jnp.where(at < 4, product[:8], 0.0)
    moments = jnp.where(at == 4, pair(2, 2, 4), moments)
    moments = jnp.where(at == 5, pair(2, 3, 5), moments)
    moments = jnp.where(at == 6, pair(3, 3, 6), moments)
    moments = jnp.where(at == 7, energy, moments)
    line = [
        moments[2 * t : 2 * t + 1] + pltpu.roll(moments[2 * t + 1 : 2 * t + 2], 64, 1)
        for t in range(3)
    ]
    line = jnp.concatenate(line + [cand_ref[...]], axis=1)
    send_ref[:, 0, :] = jnp.broadcast_to(line, (send_ref.shape[0], 4 * LANES))


def turn_kernel(u_ref, out_ref, wide):
    for k in range(HALF):
        rows = jnp.concatenate([u_ref[n, 8 * k : 8 * k + 8, :] for n in range(4)], axis=0)
        high = rows.astype(BF16).astype(F32)
        stack = jnp.concatenate([high, rows - high, high, jnp.zeros_like(high)], axis=0)
        turned = jnp.transpose(stack)
        wide[pl.ds(2 * k, BLOCK, stride=BLOCKS), :] = turned[:BLOCK]
        wide[pl.ds(2 * k + 1, BLOCK, stride=BLOCKS), :] = turned[BLOCK:]
    out_ref[...] = wide[...].astype(BF16)


def strain_kernel(rest_ref, arrived_ref, cand_ref, strain_ref):
    devs = arrived_ref.shape[0]
    points = strain_ref.shape[1]
    index = side_by_side(rest_ref[144:152, :points].astype(jnp.int32))
    refs = 8 * points
    partner = (index - NODES) >> 4
    other = jnp.where(iota((devs, refs), 0) == partner, 1.0, 0.0).astype(BF16)
    ghost = jnp.transpose(arrived_ref[:, 0, :])[:64]
    ghost = jnp.concatenate(split3(ghost), axis=0).astype(BF16)
    found = bdot(ghost, other)
    found = (found[:64] + found[64:128]) + found[128:]
    found = jnp.where(iota((64, refs), 0) % 16 == index % 16, found, 0.0)
    sums = [jnp.sum(found[16 * c : 16 * c + 16], axis=0, keepdims=True) for c in range(3)]
    nodal = by_node(jnp.concatenate(sums, axis=0), points) + rest_ref[160:184, :points]
    strain = jnp.concatenate(
        [
            jnp.sum(rest_ref[24 * c : 24 * c + 24, :points] * nodal, axis=0, keepdims=True)
            for c in range(6)
        ],
        axis=0,
    )
    strain_ref[...] = jnp.concatenate([strain, jnp.zeros((2, points), F32)], axis=0)

    assign = rest_ref[152:153, :points]
    plastic = assign >= 0.0
    flags = jnp.where(plastic, 1.0, 0.0)
    before = jnp.where(iota((points, points), 0) < iota((points, points), 1), 1.0, 0.0)
    rank = bdot(jnp.broadcast_to(flags, (8, points)).astype(BF16), before.astype(BF16))
    pick = jnp.where(plastic & (rank == iota((8, points), 0).astype(F32)), 1.0, 0.0)
    values = jnp.concatenate(
        [
            strain,
            assign + 1.0,
            jnp.zeros((LANES - 7, points), F32),
        ],
        axis=0,
    )
    chosen = dot_nt(pick, values)
    line = chosen[0:1]
    for slot in range(1, PLASTIC_CAP):
        line = line + pltpu.roll(chosen[slot : slot + 1], 8 * slot, 1)
    cand_ref[...] = line


def section_kernel(arrived_ref, send_ref):
    devs = arrived_ref.shape[0]
    groups = send_ref.shape[0] // 2
    total = jnp.sum(arrived_ref[:, 0, : 3 * LANES], axis=0, keepdims=True)
    cand = arrived_ref[:, 0, 3 * LANES :]
    turned = jnp.transpose(jnp.concatenate([cand] * (LANES // devs), axis=0))
    line = jnp.concatenate([turned[8 * n : 8 * n + 8, :devs] for n in range(PLASTIC_CAP)], axis=1)
    width = PLASTIC_CAP * devs
    target = line[6:7].astype(jnp.int32) - 1
    row = iota((64, width), 0)
    keep = ((target >> 7) == row // 8) & (row % 8 < 6)
    left = [
        jnp.where(keep, jnp.concatenate([part] * 8, axis=0), 0.0).astype(BF16)
        for part in split3(line)
    ]
    hot = jnp.where(iota((POINTS, width), 0) == (target & (POINTS - 1)), 1.0, 0.0).astype(BF16)
    dense = bdot_nt(jnp.concatenate(left, axis=0), hot)
    dense = (dense[:64] + dense[64:128]) + dense[128:]
    for h in range(groups):
        for core in range(2):
            for c in range(6):
                lanes = slice(c * LANES, (c + 1) * LANES)
                send_ref[2 * h + core, :, lanes] = dense[8 * h + c : 8 * h + c + 1]
            send_ref[2 * h + core, :, 6 * LANES :] = total


def coefficients(m, centre, step):
    m00, m01, m02, m03, m22, m23, m33, energy = m
    m11 = m00 + (step[1] * m02 + (centre[1] - centre[0]) * m01) / step[0]
    m12 = (step[2] * m03 + (centre[2] - centre[0]) * m02 + step[1] * m01) / step[0]
    m13 = (step[1] * (m22 - m11) + (centre[1] - centre[2]) * m12 + step[0] * m02) / step[2]
    products = [
        [m00, m01, m02, m03],
        [m01, m11, m12, m13],
        [m02, m12, m22, m23],
        [m03, m13, m23, m33],
    ]

    def gram(a, b):
        return products[a][b]

    def image(a, b):
        a, b = max(a, b), min(a, b)
        if b == 3:
            return energy
        value = step[b] * products[a][b + 1] + centre[b] * products[a][b]
        return value + step[b - 1] * products[a][b - 1] if b else value

    def inner(p, form):
        total = None
        for a in range(len(p)):
            for b in range(a, len(p)):
                term = p[a] * p[b] * form(a, b)
                if a != b:
                    term = 2.0 * term
                total = term if total is None else total + term
        return total

    def times(p):
        out = [jnp.zeros_like(p[0]) for _ in range(len(p) + 1)]
        for b, v in enumerate(p):
            out[b + 1] = out[b + 1] + step[b] * v
            out[b] = out[b] + centre[b] * v
            if b:
                out[b - 1] = out[b - 1] + step[b - 1] * v
        return out

    one = jnp.ones_like(m00)
    answer = []
    residual = [one]
    direction = [one]
    norm = m00
    for turn in range(4):
        alpha = norm / inner(direction, image)
        answer = answer + [jnp.zeros_like(one)]
        answer = [x + alpha * p for x, p in zip(answer, direction)]
        if turn < 3:
            stepped = times(direction)
            residual = residual + [jnp.zeros_like(one)]
            residual = [r - alpha * v for r, v in zip(residual, stepped)]
            later = inner(residual, gram)
            beta = later / norm
            direction = direction + [jnp.zeros_like(one)]
            direction = [r + beta * p for r, p in zip(residual, direction)]
            norm = later
    return answer


def final_kernel(
    scale,
    arrived_ref,
    strain_ref,
    assign_ref,
    elastic_ref,
    basis_ref,
    u_ref,
    stress_ref,
    out_ref,
):
    groups = arrived_ref.shape[0] // 2
    points = strain_ref.shape[1]
    mine = lax.axis_index("group")
    centre = [basis_ref[n : n + 1, :] for n in range(3)]
    step = [basis_ref[n + 3 : n + 4, :] for n in range(3)]
    both = jnp.sum(arrived_ref[:, 0, : 6 * LANES], axis=0, keepdims=True)
    field = [both[:, c * LANES : (c + 1) * LANES] for c in range(6)]
    field = jnp.concatenate(field + [jnp.zeros((2, LANES), F32)], axis=0)

    def unfold(lines):
        tiles = []
        for t in range(3):
            tile = lines[:, t * LANES : (t + 1) * LANES]
            low = iota(tile.shape, 1) < 64
            tiles.append(jnp.where(low, tile, 0.0))
            tiles.append(jnp.where(low, pltpu.roll(tile, 64, 1), 0.0))
        blank = jnp.zeros((2, LANES), F32)
        return [
            jnp.concatenate([v[h : h + 1] for v in tiles] + [blank], axis=0)
            for h in range(lines.shape[0])
        ]

    lane = iota((8, LANES), 1)
    diagonal = (iota((64, LANES), 0) // 8) == (iota((64, LANES), 1) % 64) // 8

    def tall(x):
        return jnp.concatenate([x] * 8, axis=0)

    def opened(moments):
        high, middle, low = split3(moments + pltpu.roll(moments, 64, 1))
        first = jnp.where(diagonal, tall(jnp.where(lane < 64, high, middle)), 0.0).astype(BF16)
        second = jnp.where(diagonal, tall(jnp.where(lane < 64, high, low)), 0.0).astype(BF16)
        return jnp.concatenate([first, first, second], axis=1)

    def meeting(x):
        high, middle, low = (tall(part) for part in split3(x))
        parts = [high, high, middle, middle, low, high]
        return jnp.concatenate(parts, axis=0).astype(BF16)

    strain = strain_ref[...]
    padded = jnp.concatenate([strain, jnp.zeros((8, LANES - points), F32)], axis=1)
    assign = jnp.concatenate(
        [assign_ref[...], jnp.full((1, LANES - points), -1, jnp.int32)], axis=1
    )
    halves = arrived_ref[:, 0, 6 * LANES :]
    whole = [halves[2 * h : 2 * h + 1] + halves[2 * h + 1 : 2 * h + 2] for h in range(groups)]
    every = unfold(jnp.concatenate(whole, axis=0))
    own = jnp.zeros((8, LANES), F32)
    for h in range(groups):
        own = own + jnp.where(mine == h, every[h], 0.0)
    forces = bdot(opened(own), meeting(field))
    every = jnp.concatenate([opened(v) for v in every], axis=0)
    products = bdot(every, meeting(padded))
    group_of = assign >> 7
    local = jnp.zeros((64, LANES), F32)
    for h in range(groups):
        local = local + jnp.where(group_of == h, products[64 * h : 64 * h + 64], 0.0)

    m = []
    for n in range(8):
        first = jnp.sum(forces[8 * n : 8 * n + 8] * field, axis=0, keepdims=True)
        second = jnp.sum(local[8 * n : 8 * n + 8] * padded, axis=0, keepdims=True)
        m.append(jnp.concatenate([first, second], axis=0))
    answer = coefficients(m, centre, step)

    extra = jnp.zeros((8, LANES), F32)
    for n in range(4):
        extra = extra + answer[n][1:2] * local[8 * n : 8 * n + 8]
    elastic_stress = dot(elastic_ref[...], strain[:6])
    plastic = assign_ref[...] >= 0
    stress_ref[...] = elastic_stress + jnp.where(plastic, extra[:6, :points], 0.0)

    right = jnp.concatenate([(scale * answer[n][0:1]) * field for n in range(4)], axis=0)
    high = right.astype(BF16).astype(F32)
    right = jnp.concatenate([high, high, right - high, jnp.zeros_like(high)], axis=0).astype(BF16)
    for part in range(6):
        rows = slice(512 * part, 512 * part + 512)
        out_ref[rows, :] = bdot(u_ref[rows, :], right)


def call(kernel, outs, *args, scratch=(), own_copies=0, cost=None):
    vmem = pl.BlockSpec(memory_space=pltpu.VMEM)
    many = isinstance(outs, list)
    out_specs = [vmem] * len(outs) if many else vmem
    scratch = list(scratch)
    if own_copies:
        scratch += [pltpu.VMEM(x.shape, x.dtype) for x in args[:own_copies]]
        scratch += [pltpu.SemaphoreType.DMA((own_copies,))]
    spaces = [pl.BlockSpec(memory_space=pltpu.HBM)] * own_copies + [vmem] * len(args)
    limit = 60 if own_copies else 32
    return pl.pallas_call(
        kernel,
        out_shape=outs,
        in_specs=spaces[: len(args)],
        out_specs=out_specs,
        scratch_shapes=scratch,
        cost_estimate=cost,
        compiler_params=pltpu.CompilerParams(vmem_limit_bytes=limit * 1024 * 1024),
    )(*args)


def arr(*shape, dtype=F32):
    return jax.ShapeDtypeStruct(shape, dtype)


def shifted(x, by):
    devices = lax.axis_size("dev")
    return lax.ppermute(x, "dev", [(i, (i + by) % devices) for i in range(devices)])


def exchange(x, axis, members=None):
    return lax.all_to_all(
        x, axis, split_axis=0, concat_axis=0, tiled=True, axis_index_groups=members
    )


def local(
    displacement,
    connectivity,
    face_nodes,
    strain_map,
    assignment,
    phases,
    load_map,
    stiff_root,
    chain_map,
    bridge_map,
    elastic,
):
    groups = lax.axis_size("group")
    devs = lax.axis_size("dev")
    points = connectivity.shape[1]
    assign = assignment.reshape(1, -1)

    listed = jnp.transpose(face_nodes, (0, 2, 1))
    load = jnp.transpose(load_map, (0, 2, 1))
    labels = jnp.transpose(phases, (0, 2, 1))
    sources = [displacement, listed, load, labels, connectivity, strain_map, assign]
    sources += [stiff_root, chain_map, bridge_map]
    outgoing, packed, edge, rest = call(
        first_kernel,
        [arr(devs, 1, LANES), arr(ROWS, LANES), arr(QUARTER, LANES), arr(264 + ROWS, LANES)],
        *sources,
        own_copies=len(sources),
    )
    arrived = exchange(outgoing, "dev")
    near = [shifted(packed, 1), shifted(edge, 2), shifted(packed, -1), shifted(packed, -2)]
    *weights, terms, strain_part, own_part = call(
        tables,
        [
            arr(3 * LANES, 2 * LANES, dtype=BF16),
            arr(3 * LANES, LANES, dtype=BF16),
            arr(9 * LANES, LANES, dtype=BF16),
            arr(8, LANES),
            arr(184, LANES),
            arr(ROWS, LANES),
        ],
        rest,
    )
    cand, strain = call(
        strain_kernel,
        [arr(1, LANES), arr(8, points)],
        strain_part,
        arrived,
        cost=pl.CostEstimate(flops=2 * 10**10, bytes_accessed=0, transcendentals=0),
    )
    vectors, send = call(
        krylov_kernel,
        [arr(4, ROWS, LANES), arr(devs // 2, 1, 4 * LANES)],
        own_part,
        *near,
        *weights,
        terms,
        cand,
    )
    same_core = [list(range(core, devs, 2)) for core in range(2)]
    same_chip = [
        [g * devs + chip + core for g in range(groups) for core in range(2)]
        for chip in range(0, devs, 2)
    ]
    section = exchange(send, "dev", same_core)
    turned = call(
        turn_kernel,
        arr(BLOCK * BLOCKS, LANES, dtype=BF16),
        vectors,
        scratch=[pltpu.VMEM((BLOCK * BLOCKS, LANES), F32)],
    )
    across = call(section_kernel, arr(2 * groups, 1, 9 * LANES), section)
    gathered = exchange(across, ("group", "dev"), same_chip)
    scale = math.sqrt(BLOCK * devs * BLOCKS)
    stress, fluctuation = call(
        lambda *refs: final_kernel(scale, *refs),
        [arr(6, points), arr(BLOCK * BLOCKS, POINTS)],
        gathered,
        strain,
        assign,
        elastic,
        terms,
        turned,
    )
    return stress, fluctuation.reshape(1, BLOCK, BLOCKS, POINTS)


def solution(mesh):
    in_specs = (
        P(None, ("group", "dev")),
        P(None, ("group", "dev")),
        P(("group", "dev"), None, None),
        P(None, None, ("group", "dev")),
        P(("group", "dev")),
        P("group", None, "dev"),
        P(None, None, "dev"),
        P(),
        P(),
        P(),
        P(),
    )
    out_specs = (P(None, ("group", "dev")), P("group", None, "dev", None))
    return jax.shard_map(local, mesh=mesh, in_specs=in_specs, out_specs=out_specs, check_vma=False)
```

```python
import math

import jax
import jax.numpy as jnp
from jax import lax
from jax.experimental import pallas as pl
from jax.experimental.pallas import tpu as pltpu
from jax.sharding import PartitionSpec as P

BLOCK = 64
IFACE = 16
BLOCKS = 48
POINTS = 128
PLASTIC_CAP = 8
NODES = 256
HALF = BLOCKS // 2
ROWS = HALF * 8
LANES = 128

ridge = 0.5
F32 = jnp.float32
BF16 = jnp.bfloat16
HIGHEST = lax.Precision.HIGHEST


def iota(shape, dim):
    return lax.broadcasted_iota(jnp.int32, shape, dim)


def dot(a, b):
    return jnp.dot(a, b, precision=HIGHEST, preferred_element_type=F32)


def dot_nt(a, b):
    return lax.dot_general(
        a, b, (((1,), (1,)), ((), ())), precision=HIGHEST, preferred_element_type=F32
    )


def dot_tn(a, b):
    return lax.dot_general(
        a, b, (((0,), (0,)), ((), ())), precision=HIGHEST, preferred_element_type=F32
    )


def bdot(a, b):
    return jnp.dot(a, b, preferred_element_type=F32)


def bdot_nt(a, b):
    return lax.dot_general(a, b, (((1,), (1,)), ((), ())), preferred_element_type=F32)


def split2(x):
    high = x.astype(BF16)
    return high, (x - high.astype(F32)).astype(BF16)


def split3(x):
    high = x.astype(BF16).astype(F32)
    rest = x - high
    middle = rest.astype(BF16).astype(F32)
    return high, middle, rest - middle


def spread_rows(values):
    n = values.shape[1]
    rows = []
    for part in split3(values):
        for c in range(3):
            rows.append(jnp.broadcast_to(part[c : c + 1], (16, n)))
        rows.append(jnp.zeros((16, n), F32))
    return jnp.concatenate(rows, axis=0)


def stacked(ref, m):
    high, low = split2(m)
    rows = m.shape[0]
    ref[:rows] = high
    ref[rows : 2 * rows] = high
    ref[2 * rows :] = low


def rough(a, b):
    return bdot(a.astype(BF16), b.astype(BF16))


def pack(load, phase, out_ref):
    for c in range(6):
        out_ref[pl.ds(c, HALF, stride=8), :] = jnp.concatenate(
            [load[pl.ds(c, 1), pl.ds(par, HALF, stride=2), :][0] for par in range(2)], axis=1
        )
    labels = [phase[pl.ds(0, 1), pl.ds(par, HALF, stride=2), :][0] for par in range(2)]
    weights = 1.0 + 2.0 * jnp.concatenate(labels, axis=1).astype(F32)
    out_ref[pl.ds(6, HALF, stride=8), :] = weights
    out_ref[pl.ds(7, HALF, stride=8), :] = jnp.zeros((HALF, LANES), F32)


def faces(disp, listed, out_ref):
    devs = listed.shape[2]
    nodes = disp.shape[1]
    names = jnp.concatenate([listed[0].astype(F32), jnp.zeros((16, LANES - devs), F32)], axis=1)
    names = jnp.concatenate([names, jnp.zeros((LANES - 16, LANES), F32)], axis=0)
    names = jnp.transpose(names)[:devs]
    spread = spread_rows(disp[...])
    spread = jnp.concatenate([spread, jnp.zeros((64, nodes), F32)], axis=0).astype(BF16)
    place = iota((devs, nodes), 1).astype(F32)
    hot = jnp.concatenate(
        [jnp.where(names[:, j : j + 1] == place, 1.0, 0.0) for j in range(16)], axis=0
    ).astype(BF16)
    found = bdot_nt(hot, spread)
    lane = iota((devs, 256), 1) % 16
    total = jnp.zeros((devs, 256), F32)
    for j in range(16):
        total = total + jnp.where(lane == j, found[j * devs : (j + 1) * devs], 0.0)
    near = total[:, :LANES]
    out_ref[:, 0, :] = (near + pltpu.roll(near, 64, 1)) + total[:, LANES:]


def fetch(sources, targets, sems):
    copies = [
        pltpu.make_async_copy(a, b, sems.at[n]) for n, (a, b) in enumerate(zip(sources, targets))
    ]
    for copy in copies:
        copy.start()
    return copies


QUARTER = ROWS // 4


def edge_rows(x):
    lane = iota((QUARTER, LANES), 1) // IFACE
    out = jnp.zeros((QUARTER, LANES), F32)
    for q in range(4):
        rows = x[QUARTER * q : QUARTER * (q + 1)]
        out = jnp.where(lane == 2 * q, pltpu.roll(rows, (32 * q - 48) % LANES, 1), out)
        out = jnp.where(lane == 2 * q + 1, pltpu.roll(rows, (32 * q - 96) % LANES, 1), out)
    return out


def spread_edge(x):
    lane = iota((QUARTER, LANES), 1) // IFACE
    out = []
    for q in range(4):
        first = pltpu.roll(x, (48 - 32 * q) % LANES, 1)
        second = pltpu.roll(x, (96 - 32 * q) % LANES, 1)
        out.append(jnp.where(lane == 3, first, jnp.where(lane == 7, second, 0.0)))
    return jnp.concatenate(out, axis=0)


def own_nodes(disp, conn):
    nodes, points = disp.shape[1], conn.shape[1]
    index = side_by_side(conn[...])
    hot = jnp.where(iota((nodes, 8 * points), 0) == index, 1.0, 0.0).astype(BF16)
    parts = jnp.concatenate(split3(disp[...]) + (jnp.zeros((7, nodes), F32),), axis=0)
    found = bdot(parts.astype(BF16), hot)
    return by_node((found[0:3] + found[3:6]) + found[6:9], points)


def side_by_side(rows):
    return jnp.concatenate([rows[a : a + 1] for a in range(rows.shape[0])], axis=1)


def by_node(sums, points):
    return jnp.concatenate(
        [sums[:, a * points : (a + 1) * points] for a in range(8)],
        axis=0,
    )


def first_kernel(*refs):
    face_ref, pack_ref, edge_ref, rest_ref, *held, sems = refs[10:]
    copies = fetch(refs[:10], held, sems)
    disp, listed, load, phase, conn, maps, assign, root, chain, bridge = held
    for copy in copies[:2]:
        copy.wait()
    faces(disp, listed, face_ref)
    for copy in copies[2:]:
        copy.wait()
    pack(load, phase, pack_ref)
    edge_ref[...] = edge_rows(pack_ref[...])
    points = conn.shape[1]
    blank = jnp.zeros((7, points), F32)
    for c in range(6):
        rest_ref[24 * c : 24 * c + 24, :points] = maps[c]
    rest_ref[144:152, :points] = conn[...].astype(F32)
    rest_ref[152:160, :points] = jnp.concatenate([assign[...].astype(F32), blank], axis=0)
    rest_ref[160:184, :points] = own_nodes(disp, conn)
    rest_ref[:184, points:] = jnp.zeros((184, LANES - points), F32)
    rest_ref[184:248, :] = jnp.concatenate([root[...], chain[...]], axis=1)
    wide = jnp.concatenate([bridge[...], jnp.zeros((IFACE, LANES - IFACE), F32)], axis=1)
    rest_ref[248:264, :] = wide
    rest_ref[264:, :] = pack_ref[...]


def tables(rest_ref, w1, wb, w2, basis_ref, strain_part, own_part):
    strain_part[...] = rest_ref[:184]
    own_part[...] = rest_ref[264:]
    root, chain = rest_ref[184:248, :BLOCK], rest_ref[184:248, BLOCK:]
    bridge = rest_ref[248:264, :IFACE]
    zero = jnp.zeros((BLOCK, BLOCK), F32)

    def straight(m):
        return jnp.concatenate(
            [jnp.concatenate([m, zero], axis=1), jnp.concatenate([zero, m], axis=1)], axis=0
        )

    def crossed(m):
        return jnp.concatenate(
            [jnp.concatenate([zero, m], axis=1), jnp.concatenate([m, zero], axis=1)], axis=0
        )

    gap = BLOCK - IFACE
    wide = jnp.concatenate([bridge, jnp.zeros((IFACE, gap), F32)], axis=1)
    upper = jnp.concatenate([jnp.zeros((gap, BLOCK), F32), wide], axis=0)
    roots, chains, bridges = straight(root), crossed(chain), straight(upper)
    stacked(w1, jnp.concatenate([jnp.transpose(roots), jnp.transpose(chains)], axis=1))
    stacked(wb, jnp.transpose(bridges))
    stacked(w2, jnp.concatenate([roots, -chains, -bridges], axis=0))

    size = 2 * BLOCK
    diagonal = iota((size, size), 0) == iota((size, size), 1)
    edge = jnp.where(diagonal, 1.0, 0.0) - chains
    face = jnp.where(diagonal & (iota((size, size), 0) % BLOCK >= gap), 1.0, 0.0) - bridges
    tall = jnp.concatenate([2.0**0.5 * roots, edge, face], axis=0)
    model = rough(jnp.transpose(tall), tall)
    model = model + jnp.where(diagonal, ridge, 0.0)

    def inner(p, q):
        return jnp.sum(jnp.sum(p * q, axis=1, keepdims=True), axis=0, keepdims=True)

    now = jnp.where(diagonal, size**-0.5, 0.0)
    past, image = None, size**-0.5 * model
    centres, steps = [], []
    for n in range(3):
        if n:
            image = rough(model, now)
        centre = inner(now, image)
        rest = image - centre * now
        if n:
            rest = rest - steps[-1] * past
        step = jnp.maximum(jnp.sqrt(inner(rest, rest)), 0.01 * centres[0] if n else 0.01 * centre)
        centres.append(centre)
        steps.append(step)
        past, now = now, rest / step
    row = iota((8, LANES), 0)
    table = jnp.zeros((8, LANES), F32)
    for n, value in enumerate(centres + steps):
        table = jnp.where(row == n, value, table)
    basis_ref[...] = table


def krylov_kernel(
    own_ref, m1_ref, m2_ref, p1_ref, p2_ref, w1, wb, w2, basis_ref, cand_ref, u_ref, send_ref
):
    centre = [basis_ref[n : n + 1, :] for n in range(3)]
    step = [basis_ref[n + 3 : n + 4, :] for n in range(3)]
    inverse = [1.0 / v for v in step]

    def lanes(x):
        return iota(x.shape, 1)

    def weights_of(x):
        w = x.reshape(HALF, 8, LANES)[:, 6:7, :]
        return jnp.broadcast_to(w, (HALF, 8, LANES)).reshape(ROWS, LANES)

    def parts(x):
        high, low = split2(x)
        return jnp.concatenate([high, low, high], axis=1)

    def stage(x, w):
        return bdot(parts(x), w[...])

    def blocks(x):
        return [x[n : n + ROWS] for n in range(0, x.shape[0], ROWS)]

    def up(x):
        parts = [p for v in blocks(x) for p in (v[8:], v[:8])]
        return jnp.concatenate(parts, axis=0)

    def down(x):
        parts = [p for v in blocks(x) for p in (v[ROWS - 8 :], v[: ROWS - 8])]
        return jnp.concatenate(parts, axis=0)

    def halves(x, w, split):
        both = bdot(split, w1[...])
        lifted = both[:, :LANES]
        mixed = both[:, LANES:]
        edge = x - jnp.where(lanes(x) < BLOCK, mixed, up(mixed))
        return lifted, w * lifted, edge

    def face(x, following):
        return jnp.where(lanes(x) % BLOCK >= BLOCK - IFACE, x, 0.0) - following

    def apply(x, w, split, f, f_before):
        _, weighted, edge = halves(x, w, split)
        shifted = jnp.where(lanes(x) < BLOCK, edge, down(edge))
        left = jnp.concatenate([weighted, shifted, f_before], axis=1)
        return ridge * x + edge + f + stage(left, w2)

    zero = jnp.zeros((ROWS, LANES), F32)
    near = [m1_ref[...], own_ref[...], p1_ref[...], p2_ref[...]]
    w = jnp.concatenate([weights_of(x) for x in near], axis=0)

    x0 = jnp.concatenate(near, axis=0)
    known = jnp.concatenate([spread_edge(m2_ref[...]), x0[: 3 * ROWS]], axis=0)
    split = parts(x0)
    f = jnp.concatenate([face(known, bdot(split, wb[...])), zero], axis=0)
    image = apply(x0, w, split, f[ROWS:], f[: 4 * ROWS])
    x1 = inverse[0] * (image - centre[0] * x0)

    split = parts(x1)
    f = jnp.concatenate([zero, face(x1[: 3 * ROWS], bdot(split[ROWS:], wb[...]))], axis=0)
    now, past = x1[: 3 * ROWS], x0[: 3 * ROWS]
    image = apply(now, w[: 3 * ROWS], split[: 3 * ROWS], f[ROWS:], f[: 3 * ROWS])
    x2 = inverse[1] * (image - centre[1] * now - step[0] * past)

    split = parts(x2[ROWS:])
    f = jnp.concatenate([face(x2[: 2 * ROWS], bdot(split, wb[...])), zero], axis=0)
    now, past = x2[ROWS:], x1[ROWS : 3 * ROWS]
    image = apply(now, w[ROWS : 3 * ROWS], split, f[ROWS:], f[: 2 * ROWS])
    x3 = inverse[2] * (image - centre[2] * now - step[1] * past)

    own = x3[:ROWS]
    lifted, weighted, edge = halves(own, w[ROWS : 2 * ROWS], parts(own))
    f3 = face(own, stage(x3[ROWS:], wb))

    basis = [near[1], x1[ROWS : 2 * ROWS], x2[ROWS : 2 * ROWS], own]
    for n in range(4):
        u_ref[n] = basis[n]

    def long(x):
        return jnp.concatenate([x[8 * k : 8 * k + 8] for k in range(HALF)], axis=1)

    tall = jnp.concatenate([long(x) for x in basis + [lifted, weighted, edge, f3]], axis=0)
    high = tall.astype(BF16).astype(F32)
    both = jnp.concatenate([high, tall - high], axis=0).astype(BF16)
    product = bdot_nt(both, both)
    product = product[:64] + product[64:]
    product = product + pltpu.roll(product, 64, 1)

    def pair(a, b, to):
        return pltpu.roll(product[8 * a : 8 * a + 8], (8 * (to - b)) % LANES, 1)

    at = iota((8, LANES), 1) // 8
    energy = 0.5 * pair(3, 3, 7) + (pair(4, 5, 7) + pair(6, 6, 7) + pair(7, 7, 7))
    moments = jnp.where(at < 4, product[:8], 0.0)
    moments = jnp.where(at == 4, pair(2, 2, 4), moments)
    moments = jnp.where(at == 5, pair(2, 3, 5), moments)
    moments = jnp.where(at == 6, pair(3, 3, 6), moments)
    moments = jnp.where(at == 7, energy, moments)
    line = [
        moments[2 * t : 2 * t + 1] + pltpu.roll(moments[2 * t + 1 : 2 * t + 2], 64, 1)
        for t in range(3)
    ]
    line = jnp.concatenate(line + [cand_ref[...]], axis=1)
    send_ref[:, 0, :] = jnp.broadcast_to(line, (send_ref.shape[0], 4 * LANES))


def turn_kernel(u_ref, out_ref, wide):
    for k in range(HALF):
        rows = jnp.concatenate([u_ref[n, 8 * k : 8 * k + 8, :] for n in range(4)], axis=0)
        high = rows.astype(BF16).astype(F32)
        stack = jnp.concatenate([high, rows - high, high, jnp.zeros_like(high)], axis=0)
        turned = jnp.transpose(stack)
        wide[pl.ds(2 * k, BLOCK, stride=BLOCKS), :] = turned[:BLOCK]
        wide[pl.ds(2 * k + 1, BLOCK, stride=BLOCKS), :] = turned[BLOCK:]
    out_ref[...] = wide[...].astype(BF16)


def strain_kernel(rest_ref, arrived_ref, cand_ref, strain_ref):
    devs = arrived_ref.shape[0]
    points = strain_ref.shape[1]
    index = side_by_side(rest_ref[144:152, :points].astype(jnp.int32))
    refs = 8 * points
    partner = (index - NODES) >> 4
    other = jnp.where(iota((devs, refs), 0) == partner, 1.0, 0.0).astype(BF16)
    ghost = jnp.transpose(arrived_ref[:, 0, :])[:64]
    ghost = jnp.concatenate(split3(ghost), axis=0).astype(BF16)
    found = bdot(ghost, other)
    found = (found[:64] + found[64:128]) + found[128:]
    found = jnp.where(iota((64, refs), 0) % 16 == index % 16, found, 0.0)
    sums = [jnp.sum(found[16 * c : 16 * c + 16], axis=0, keepdims=True) for c in range(3)]
    nodal = by_node(jnp.concatenate(sums, axis=0), points) + rest_ref[160:184, :points]
    strain = jnp.concatenate(
        [
            jnp.sum(rest_ref[24 * c : 24 * c + 24, :points] * nodal, axis=0, keepdims=True)
            for c in range(6)
        ],
        axis=0,
    )
    strain_ref[...] = jnp.concatenate([strain, jnp.zeros((2, points), F32)], axis=0)

    assign = rest_ref[152:153, :points]
    plastic = assign >= 0.0
    flags = jnp.where(plastic, 1.0, 0.0)
    before = jnp.where(iota((points, points), 0) < iota((points, points), 1), 1.0, 0.0)
    rank = bdot(jnp.broadcast_to(flags, (8, points)).astype(BF16), before.astype(BF16))
    pick = jnp.where(plastic & (rank == iota((8, points), 0).astype(F32)), 1.0, 0.0)
    values = jnp.concatenate(
        [
            strain,
            assign + 1.0,
            jnp.zeros((LANES - 7, points), F32),
        ],
        axis=0,
    )
    chosen = dot_nt(pick, values)
    line = chosen[0:1]
    for slot in range(1, PLASTIC_CAP):
        line = line + pltpu.roll(chosen[slot : slot + 1], 8 * slot, 1)
    cand_ref[...] = line


def section_kernel(arrived_ref, turned_ref, send_ref):
    del turned_ref
    devs = arrived_ref.shape[0]
    groups = send_ref.shape[0] // 2
    total = jnp.sum(arrived_ref[:, 0, : 3 * LANES], axis=0, keepdims=True)
    cand = arrived_ref[:, 0, 3 * LANES :]
    turned = jnp.transpose(jnp.concatenate([cand] * (LANES // devs), axis=0))
    line = jnp.concatenate([turned[8 * n : 8 * n + 8, :devs] for n in range(PLASTIC_CAP)], axis=1)
    width = PLASTIC_CAP * devs
    target = line[6:7].astype(jnp.int32) - 1
    row = iota((64, width), 0)
    keep = ((target >> 7) == row // 8) & (row % 8 < 6)
    left = [
        jnp.where(keep, jnp.concatenate([part] * 8, axis=0), 0.0).astype(BF16)
        for part in split3(line)
    ]
    hot = jnp.where(iota((POINTS, width), 0) == (target & (POINTS - 1)), 1.0, 0.0).astype(BF16)
    dense = bdot_nt(jnp.concatenate(left, axis=0), hot)
    dense = (dense[:64] + dense[64:128]) + dense[128:]
    for h in range(groups):
        for core in range(2):
            for c in range(6):
                lanes = slice(c * LANES, (c + 1) * LANES)
                send_ref[2 * h + core, :, lanes] = dense[8 * h + c : 8 * h + c + 1]
            send_ref[2 * h + core, :, 6 * LANES :] = total


def coefficients(m, centre, step):
    m00, m01, m02, m03, m22, m23, m33, energy = m
    m11 = m00 + (step[1] * m02 + (centre[1] - centre[0]) * m01) / step[0]
    m12 = (step[2] * m03 + (centre[2] - centre[0]) * m02 + step[1] * m01) / step[0]
    m13 = (step[1] * (m22 - m11) + (centre[1] - centre[2]) * m12 + step[0] * m02) / step[2]
    products = [
        [m00, m01, m02, m03],
        [m01, m11, m12, m13],
        [m02, m12, m22, m23],
        [m03, m13, m23, m33],
    ]

    def gram(a, b):
        return products[a][b]

    def image(a, b):
        a, b = max(a, b), min(a, b)
        if b == 3:
            return energy
        value = step[b] * products[a][b + 1] + centre[b] * products[a][b]
        return value + step[b - 1] * products[a][b - 1] if b else value

    def inner(p, form):
        total = None
        for a in range(len(p)):
            for b in range(a, len(p)):
                term = p[a] * p[b] * form(a, b)
                if a != b:
                    term = 2.0 * term
                total = term if total is None else total + term
        return total

    def times(p):
        out = [jnp.zeros_like(p[0]) for _ in range(len(p) + 1)]
        for b, v in enumerate(p):
            out[b + 1] = out[b + 1] + step[b] * v
            out[b] = out[b] + centre[b] * v
            if b:
                out[b - 1] = out[b - 1] + step[b - 1] * v
        return out

    one = jnp.ones_like(m00)
    answer = []
    residual = [one]
    direction = [one]
    norm = m00
    for turn in range(4):
        alpha = norm / inner(direction, image)
        answer = answer + [jnp.zeros_like(one)]
        answer = [x + alpha * p for x, p in zip(answer, direction)]
        if turn < 3:
            stepped = times(direction)
            residual = residual + [jnp.zeros_like(one)]
            residual = [r - alpha * v for r, v in zip(residual, stepped)]
            later = inner(residual, gram)
            beta = later / norm
            direction = direction + [jnp.zeros_like(one)]
            direction = [r + beta * p for r, p in zip(residual, direction)]
            norm = later
    return answer


def final_kernel(
    scale,
    arrived_ref,
    strain_ref,
    assign_ref,
    elastic_ref,
    basis_ref,
    u_ref,
    stress_ref,
    out_ref,
):
    groups = arrived_ref.shape[0] // 2
    points = strain_ref.shape[1]
    mine = lax.axis_index("group")
    centre = [basis_ref[n : n + 1, :] for n in range(3)]
    step = [basis_ref[n + 3 : n + 4, :] for n in range(3)]
    both = jnp.sum(arrived_ref[:, 0, : 6 * LANES], axis=0, keepdims=True)
    field = [both[:, c * LANES : (c + 1) * LANES] for c in range(6)]
    field = jnp.concatenate(field + [jnp.zeros((2, LANES), F32)], axis=0)

    def unfold(lines):
        tiles = []
        for t in range(3):
            tile = lines[:, t * LANES : (t + 1) * LANES]
            low = iota(tile.shape, 1) < 64
            tiles.append(jnp.where(low, tile, 0.0))
            tiles.append(jnp.where(low, pltpu.roll(tile, 64, 1), 0.0))
        blank = jnp.zeros((2, LANES), F32)
        return [
            jnp.concatenate([v[h : h + 1] for v in tiles] + [blank], axis=0)
            for h in range(lines.shape[0])
        ]

    lane = iota((8, LANES), 1)
    diagonal = (iota((64, LANES), 0) // 8) == (iota((64, LANES), 1) % 64) // 8

    def tall(x):
        return jnp.concatenate([x] * 8, axis=0)

    def opened(moments):
        high, middle, low = split3(moments + pltpu.roll(moments, 64, 1))
        first = jnp.where(diagonal, tall(jnp.where(lane < 64, high, middle)), 0.0).astype(BF16)
        second = jnp.where(diagonal, tall(jnp.where(lane < 64, high, low)), 0.0).astype(BF16)
        return jnp.concatenate([first, first, second], axis=1)

    def meeting(x):
        high, middle, low = (tall(part) for part in split3(x))
        parts = [high, high, middle, middle, low, high]
        return jnp.concatenate(parts, axis=0).astype(BF16)

    strain = strain_ref[...]
    padded = jnp.concatenate([strain, jnp.zeros((8, LANES - points), F32)], axis=1)
    assign = jnp.concatenate(
        [assign_ref[...], jnp.full((1, LANES - points), -1, jnp.int32)], axis=1
    )
    halves = arrived_ref[:, 0, 6 * LANES :]
    whole = [halves[2 * h : 2 * h + 1] + halves[2 * h + 1 : 2 * h + 2] for h in range(groups)]
    every = unfold(jnp.concatenate(whole, axis=0))
    own = jnp.zeros((8, LANES), F32)
    for h in range(groups):
        own = own + jnp.where(mine == h, every[h], 0.0)
    forces = bdot(opened(own), meeting(field))
    every = jnp.concatenate([opened(v) for v in every], axis=0)
    products = bdot(every, meeting(padded))
    group_of = assign >> 7
    local = jnp.zeros((64, LANES), F32)
    for h in range(groups):
        local = local + jnp.where(group_of == h, products[64 * h : 64 * h + 64], 0.0)

    m = []
    for n in range(8):
        first = jnp.sum(forces[8 * n : 8 * n + 8] * field, axis=0, keepdims=True)
        second = jnp.sum(local[8 * n : 8 * n + 8] * padded, axis=0, keepdims=True)
        m.append(jnp.concatenate([first, second], axis=0))
    answer = coefficients(m, centre, step)

    extra = jnp.zeros((8, LANES), F32)
    for n in range(4):
        extra = extra + answer[n][1:2] * local[8 * n : 8 * n + 8]
    elastic_stress = dot(elastic_ref[...], strain[:6])
    plastic = assign_ref[...] >= 0
    stress_ref[...] = elastic_stress + jnp.where(plastic, extra[:6, :points], 0.0)

    right = jnp.concatenate([(scale * answer[n][0:1]) * field for n in range(4)], axis=0)
    high = right.astype(BF16).astype(F32)
    right = jnp.concatenate([high, high, right - high, jnp.zeros_like(high)], axis=0).astype(BF16)
    for part in range(6):
        rows = slice(512 * part, 512 * part + 512)
        out_ref[rows, :] = bdot(u_ref[rows, :], right)


def call(kernel, outs, *args, scratch=(), own_copies=0, cost=None):
    vmem = pl.BlockSpec(memory_space=pltpu.VMEM)
    many = isinstance(outs, list)
    out_specs = [vmem] * len(outs) if many else vmem
    scratch = list(scratch)
    if own_copies:
        scratch += [pltpu.VMEM(x.shape, x.dtype) for x in args[:own_copies]]
        scratch += [pltpu.SemaphoreType.DMA((own_copies,))]
    spaces = [pl.BlockSpec(memory_space=pltpu.HBM)] * own_copies + [vmem] * len(args)
    limit = 60 if own_copies else 32
    return pl.pallas_call(
        kernel,
        out_shape=outs,
        in_specs=spaces[: len(args)],
        out_specs=out_specs,
        scratch_shapes=scratch,
        cost_estimate=cost,
        compiler_params=pltpu.CompilerParams(vmem_limit_bytes=limit * 1024 * 1024),
    )(*args)


def arr(*shape, dtype=F32):
    return jax.ShapeDtypeStruct(shape, dtype)


def shifted(x, by):
    devices = lax.axis_size("dev")
    return lax.ppermute(x, "dev", [(i, (i + by) % devices) for i in range(devices)])


def exchange(x, axis, members=None):
    return lax.all_to_all(
        x, axis, split_axis=0, concat_axis=0, tiled=True, axis_index_groups=members
    )


def local(
    displacement,
    connectivity,
    face_nodes,
    strain_map,
    assignment,
    phases,
    load_map,
    stiff_root,
    chain_map,
    bridge_map,
    elastic,
):
    groups = lax.axis_size("group")
    devs = lax.axis_size("dev")
    points = connectivity.shape[1]
    assign = assignment.reshape(1, -1)

    listed = jnp.transpose(face_nodes, (0, 2, 1))
    load = jnp.transpose(load_map, (0, 2, 1))
    labels = jnp.transpose(phases, (0, 2, 1))
    sources = [displacement, listed, load, labels, connectivity, strain_map, assign]
    sources += [stiff_root, chain_map, bridge_map]
    outgoing, packed, edge, rest = call(
        first_kernel,
        [arr(devs, 1, LANES), arr(ROWS, LANES), arr(QUARTER, LANES), arr(264 + ROWS, LANES)],
        *sources,
        own_copies=len(sources),
    )
    arrived = exchange(outgoing, "dev")
    near = [shifted(packed, 1), shifted(edge, 2), shifted(packed, -1), shifted(packed, -2)]
    *weights, terms, strain_part, own_part = call(
        tables,
        [
            arr(3 * LANES, 2 * LANES, dtype=BF16),
            arr(3 * LANES, LANES, dtype=BF16),
            arr(9 * LANES, LANES, dtype=BF16),
            arr(8, LANES),
            arr(184, LANES),
            arr(ROWS, LANES),
        ],
        rest,
    )
    cand, strain = call(
        strain_kernel,
        [arr(1, LANES), arr(8, points)],
        strain_part,
        arrived,
        cost=pl.CostEstimate(flops=2 * 10**10, bytes_accessed=0, transcendentals=0),
    )
    vectors, send = call(
        krylov_kernel,
        [arr(4, ROWS, LANES), arr(devs // 2, 1, 4 * LANES)],
        own_part,
        *near,
        *weights,
        terms,
        cand,
    )
    same_core = [list(range(core, devs, 2)) for core in range(2)]
    same_chip = [
        [g * devs + chip + core for g in range(groups) for core in range(2)]
        for chip in range(0, devs, 2)
    ]
    section = exchange(send, "dev", same_core)
    turned = call(
        turn_kernel,
        arr(BLOCK * BLOCKS, LANES, dtype=BF16),
        vectors,
        scratch=[pltpu.VMEM((BLOCK * BLOCKS, LANES), F32)],
    )
    across = call(section_kernel, arr(2 * groups, 1, 9 * LANES), section, turned)
    gathered = exchange(across, ("group", "dev"), same_chip)
    scale = math.sqrt(BLOCK * devs * BLOCKS)
    stress, fluctuation = call(
        lambda *refs: final_kernel(scale, *refs),
        [arr(6, points), arr(BLOCK * BLOCKS, POINTS)],
        gathered,
        strain,
        assign,
        elastic,
        terms,
        turned,
    )
    return stress, fluctuation.reshape(1, BLOCK, BLOCKS, POINTS)


def solution(mesh):
    in_specs = (
        P(None, ("group", "dev")),
        P(None, ("group", "dev")),
        P(("group", "dev"), None, None),
        P(None, None, ("group", "dev")),
        P(("group", "dev")),
        P("group", None, "dev"),
        P(None, None, "dev"),
        P(),
        P(),
        P(),
        P(),
    )
    out_specs = (P(None, ("group", "dev")), P("group", None, "dev", None))
    return jax.shard_map(local, mesh=mesh, in_specs=in_specs, out_specs=out_specs, check_vma=False)
```

```python
import math

import jax
import jax.numpy as jnp
from jax import lax
from jax.experimental import pallas as pl
from jax.experimental.pallas import tpu as pltpu
from jax.sharding import PartitionSpec as P

BLOCK = 64
IFACE = 16
BLOCKS = 48
POINTS = 128
PLASTIC_CAP = 8
NODES = 256
HALF = BLOCKS // 2
ROWS = HALF * 8
LANES = 128

ridge = 0.5
F32 = jnp.float32
BF16 = jnp.bfloat16
HIGHEST = lax.Precision.HIGHEST


def iota(shape, dim):
    return lax.broadcasted_iota(jnp.int32, shape, dim)


def dot(a, b):
    return jnp.dot(a, b, precision=HIGHEST, preferred_element_type=F32)


def dot_nt(a, b):
    return lax.dot_general(
        a, b, (((1,), (1,)), ((), ())), precision=HIGHEST, preferred_element_type=F32
    )


def dot_tn(a, b):
    return lax.dot_general(
        a, b, (((0,), (0,)), ((), ())), precision=HIGHEST, preferred_element_type=F32
    )


def bdot(a, b):
    return jnp.dot(a, b, preferred_element_type=F32)


def bdot_nt(a, b):
    return lax.dot_general(a, b, (((1,), (1,)), ((), ())), preferred_element_type=F32)


def split2(x):
    high = x.astype(BF16)
    return high, (x - high.astype(F32)).astype(BF16)


def split3(x):
    high = x.astype(BF16).astype(F32)
    rest = x - high
    middle = rest.astype(BF16).astype(F32)
    return high, middle, rest - middle


def spread_rows(values):
    n = values.shape[1]
    rows = []
    for part in split3(values):
        for c in range(3):
            rows.append(jnp.broadcast_to(part[c : c + 1], (16, n)))
        rows.append(jnp.zeros((16, n), F32))
    return jnp.concatenate(rows, axis=0)


def stacked(ref, m):
    high, low = split2(m)
    rows = m.shape[0]
    ref[:rows] = high
    ref[rows : 2 * rows] = high
    ref[2 * rows :] = low


def rough(a, b):
    return bdot(a.astype(BF16), b.astype(BF16))


def pack(load, phase, out_ref, base):
    for c in range(6):
        out_ref[pl.ds(base + c, HALF, stride=8), :] = jnp.concatenate(
            [load[pl.ds(c, 1), pl.ds(par, HALF, stride=2), :][0] for par in range(2)], axis=1
        )
    labels = [phase[pl.ds(0, 1), pl.ds(par, HALF, stride=2), :][0] for par in range(2)]
    weights = 1.0 + 2.0 * jnp.concatenate(labels, axis=1).astype(F32)
    out_ref[pl.ds(base + 6, HALF, stride=8), :] = weights
    out_ref[pl.ds(base + 7, HALF, stride=8), :] = jnp.zeros((HALF, LANES), F32)


def faces(disp, listed, out_ref):
    devs = listed.shape[2]
    nodes = disp.shape[1]
    names = jnp.concatenate([listed[0].astype(F32), jnp.zeros((16, LANES - devs), F32)], axis=1)
    names = jnp.concatenate([names, jnp.zeros((LANES - 16, LANES), F32)], axis=0)
    names = jnp.transpose(names)[:devs]
    spread = spread_rows(disp[...])
    spread = jnp.concatenate([spread, jnp.zeros((64, nodes), F32)], axis=0).astype(BF16)
    place = iota((devs, nodes), 1).astype(F32)
    hot = jnp.concatenate(
        [jnp.where(names[:, j : j + 1] == place, 1.0, 0.0) for j in range(16)], axis=0
    ).astype(BF16)
    found = bdot_nt(hot, spread)
    lane = iota((devs, 256), 1) % 16
    total = jnp.zeros((devs, 256), F32)
    for j in range(16):
        total = total + jnp.where(lane == j, found[j * devs : (j + 1) * devs], 0.0)
    near = total[:, :LANES]
    out_ref[:, 0, :] = (near + pltpu.roll(near, 64, 1)) + total[:, LANES:]


def fetch(sources, targets, sems):
    copies = [
        pltpu.make_async_copy(a, b, sems.at[n]) for n, (a, b) in enumerate(zip(sources, targets))
    ]
    for copy in copies:
        copy.start()
    for copy in copies:
        copy.wait()


QUARTER = ROWS // 4


def edge_rows(x):
    lane = iota((QUARTER, LANES), 1) // IFACE
    out = jnp.zeros((QUARTER, LANES), F32)
    for q in range(4):
        rows = x[QUARTER * q : QUARTER * (q + 1)]
        out = jnp.where(lane == 2 * q, pltpu.roll(rows, (32 * q - 48) % LANES, 1), out)
        out = jnp.where(lane == 2 * q + 1, pltpu.roll(rows, (32 * q - 96) % LANES, 1), out)
    return out


def spread_edge(x):
    lane = iota((QUARTER, LANES), 1) // IFACE
    out = []
    for q in range(4):
        first = pltpu.roll(x, (48 - 32 * q) % LANES, 1)
        second = pltpu.roll(x, (96 - 32 * q) % LANES, 1)
        out.append(jnp.where(lane == 3, first, jnp.where(lane == 7, second, 0.0)))
    return jnp.concatenate(out, axis=0)


def own_nodes(disp, conn):
    nodes, points = disp.shape[1], conn.shape[1]
    index = side_by_side(conn[...])
    hot = jnp.where(iota((nodes, 8 * points), 0) == index, 1.0, 0.0).astype(BF16)
    parts = jnp.concatenate(split3(disp[...]) + (jnp.zeros((7, nodes), F32),), axis=0)
    found = bdot(parts.astype(BF16), hot)
    return by_node((found[0:3] + found[3:6]) + found[6:9], points)


def side_by_side(rows):
    return jnp.concatenate([rows[a : a + 1] for a in range(rows.shape[0])], axis=1)


def by_node(sums, points):
    return jnp.concatenate(
        [sums[:, a * points : (a + 1) * points] for a in range(8)],
        axis=0,
    )


def first_kernel(*refs):
    face_ref, rest_ref, *held, sems = refs[10:]
    fetch(refs[:10], held, sems)
    disp, listed, load, phase, conn, maps, assign, root, chain, bridge = held
    faces(disp, listed, face_ref)
    pack(load, phase, rest_ref, 264)
    points = conn.shape[1]
    blank = jnp.zeros((7, points), F32)
    for c in range(6):
        rest_ref[24 * c : 24 * c + 24, :points] = maps[c]
    rest_ref[144:152, :points] = conn[...].astype(F32)
    rest_ref[152:160, :points] = jnp.concatenate([assign[...].astype(F32), blank], axis=0)
    rest_ref[160:184, :points] = own_nodes(disp, conn)
    rest_ref[:184, points:] = jnp.zeros((184, LANES - points), F32)
    rest_ref[184:248, :] = jnp.concatenate([root[...], chain[...]], axis=1)
    wide = jnp.concatenate([bridge[...], jnp.zeros((IFACE, LANES - IFACE), F32)], axis=1)
    rest_ref[248:264, :] = wide


def tables(rest_ref, w1, wb, w2, basis_ref, strain_part, own_part, edge_ref):
    strain_part[...] = rest_ref[:184]
    own_part[...] = rest_ref[264:]
    edge_ref[...] = edge_rows(rest_ref[264:])
    root, chain = rest_ref[184:248, :BLOCK], rest_ref[184:248, BLOCK:]
    bridge = rest_ref[248:264, :IFACE]
    zero = jnp.zeros((BLOCK, BLOCK), F32)

    def straight(m):
        return jnp.concatenate(
            [jnp.concatenate([m, zero], axis=1), jnp.concatenate([zero, m], axis=1)], axis=0
        )

    def crossed(m):
        return jnp.concatenate(
            [jnp.concatenate([zero, m], axis=1), jnp.concatenate([m, zero], axis=1)], axis=0
        )

    gap = BLOCK - IFACE
    wide = jnp.concatenate([bridge, jnp.zeros((IFACE, gap), F32)], axis=1)
    upper = jnp.concatenate([jnp.zeros((gap, BLOCK), F32), wide], axis=0)
    roots, chains, bridges = straight(root), crossed(chain), straight(upper)
    stacked(w1, jnp.concatenate([jnp.transpose(roots), jnp.transpose(chains)], axis=1))
    stacked(wb, jnp.transpose(bridges))
    stacked(w2, jnp.concatenate([roots, -chains, -bridges], axis=0))

    size = 2 * BLOCK
    diagonal = iota((size, size), 0) == iota((size, size), 1)
    edge = jnp.where(diagonal, 1.0, 0.0) - chains
    face = jnp.where(diagonal & (iota((size, size), 0) % BLOCK >= gap), 1.0, 0.0) - bridges
    tall = jnp.concatenate([2.0**0.5 * roots, edge, face], axis=0)
    model = rough(jnp.transpose(tall), tall)
    model = model + jnp.where(diagonal, ridge, 0.0)

    def inner(p, q):
        return jnp.sum(jnp.sum(p * q, axis=1, keepdims=True), axis=0, keepdims=True)

    now = jnp.where(diagonal, size**-0.5, 0.0)
    past, image = None, size**-0.5 * model
    centres, steps = [], []
    for n in range(3):
        if n:
            image = rough(model, now)
        centre = inner(now, image)
        rest = image - centre * now
        if n:
            rest = rest - steps[-1] * past
        step = jnp.maximum(jnp.sqrt(inner(rest, rest)), 0.01 * centres[0] if n else 0.01 * centre)
        centres.append(centre)
        steps.append(step)
        past, now = now, rest / step
    row = iota((8, LANES), 0)
    table = jnp.zeros((8, LANES), F32)
    for n, value in enumerate(centres + steps):
        table = jnp.where(row == n, value, table)
    basis_ref[...] = table


def krylov_kernel(
    own_ref, m1_ref, m2_ref, p1_ref, p2_ref, w1, wb, w2, basis_ref, cand_ref, u_ref, send_ref
):
    centre = [basis_ref[n : n + 1, :] for n in range(3)]
    step = [basis_ref[n + 3 : n + 4, :] for n in range(3)]
    inverse = [1.0 / v for v in step]

    def lanes(x):
        return iota(x.shape, 1)

    def weights_of(x):
        w = x.reshape(HALF, 8, LANES)[:, 6:7, :]
        return jnp.broadcast_to(w, (HALF, 8, LANES)).reshape(ROWS, LANES)

    def parts(x):
        high, low = split2(x)
        return jnp.concatenate([high, low, high], axis=1)

    def stage(x, w):
        return bdot(parts(x), w[...])

    def blocks(x):
        return [x[n : n + ROWS] for n in range(0, x.shape[0], ROWS)]

    def up(x):
        parts = [p for v in blocks(x) for p in (v[8:], v[:8])]
        return jnp.concatenate(parts, axis=0)

    def down(x):
        parts = [p for v in blocks(x) for p in (v[ROWS - 8 :], v[: ROWS - 8])]
        return jnp.concatenate(parts, axis=0)

    def halves(x, w, split):
        both = bdot(split, w1[...])
        lifted = both[:, :LANES]
        mixed = both[:, LANES:]
        edge = x - jnp.where(lanes(x) < BLOCK, mixed, up(mixed))
        return lifted, w * lifted, edge

    def face(x, following):
        return jnp.where(lanes(x) % BLOCK >= BLOCK - IFACE, x, 0.0) - following

    def apply(x, w, split, f, f_before):
        _, weighted, edge = halves(x, w, split)
        shifted = jnp.where(lanes(x) < BLOCK, edge, down(edge))
        left = jnp.concatenate([weighted, shifted, f_before], axis=1)
        return ridge * x + edge + f + stage(left, w2)

    zero = jnp.zeros((ROWS, LANES), F32)
    near = [m1_ref[...], own_ref[...], p1_ref[...], p2_ref[...]]
    w = jnp.concatenate([weights_of(x) for x in near], axis=0)

    x0 = jnp.concatenate(near, axis=0)
    known = jnp.concatenate([spread_edge(m2_ref[...]), x0[: 3 * ROWS]], axis=0)
    split = parts(x0)
    f = jnp.concatenate([face(known, bdot(split, wb[...])), zero], axis=0)
    image = apply(x0, w, split, f[ROWS:], f[: 4 * ROWS])
    x1 = inverse[0] * (image - centre[0] * x0)

    split = parts(x1)
    f = jnp.concatenate([zero, face(x1[: 3 * ROWS], bdot(split[ROWS:], wb[...]))], axis=0)
    now, past = x1[: 3 * ROWS], x0[: 3 * ROWS]
    image = apply(now, w[: 3 * ROWS], split[: 3 * ROWS], f[ROWS:], f[: 3 * ROWS])
    x2 = inverse[1] * (image - centre[1] * now - step[0] * past)

    split = parts(x2[ROWS:])
    f = jnp.concatenate([face(x2[: 2 * ROWS], bdot(split, wb[...])), zero], axis=0)
    now, past = x2[ROWS:], x1[ROWS : 3 * ROWS]
    image = apply(now, w[ROWS : 3 * ROWS], split, f[ROWS:], f[: 2 * ROWS])
    x3 = inverse[2] * (image - centre[2] * now - step[1] * past)

    own = x3[:ROWS]
    lifted, weighted, edge = halves(own, w[ROWS : 2 * ROWS], parts(own))
    f3 = face(own, stage(x3[ROWS:], wb))

    basis = [near[1], x1[ROWS : 2 * ROWS], x2[ROWS : 2 * ROWS], own]
    for n in range(4):
        u_ref[n] = basis[n]

    def long(x):
        return jnp.concatenate([x[8 * k : 8 * k + 8] for k in range(HALF)], axis=1)

    tall = jnp.concatenate([long(x) for x in basis + [lifted, weighted, edge, f3]], axis=0)
    high = tall.astype(BF16).astype(F32)
    both = jnp.concatenate([high, tall - high], axis=0).astype(BF16)
    product = bdot_nt(both, both)
    product = product[:64] + product[64:]
    product = product + pltpu.roll(product, 64, 1)

    def pair(a, b, to):
        return pltpu.roll(product[8 * a : 8 * a + 8], (8 * (to - b)) % LANES, 1)

    at = iota((8, LANES), 1) // 8
    energy = 0.5 * pair(3, 3, 7) + (pair(4, 5, 7) + pair(6, 6, 7) + pair(7, 7, 7))
    moments = jnp.where(at < 4, product[:8], 0.0)
    moments = jnp.where(at == 4, pair(2, 2, 4), moments)
    moments = jnp.where(at == 5, pair(2, 3, 5), moments)
    moments = jnp.where(at == 6, pair(3, 3, 6), moments)
    moments = jnp.where(at == 7, energy, moments)
    line = [
        moments[2 * t : 2 * t + 1] + pltpu.roll(moments[2 * t + 1 : 2 * t + 2], 64, 1)
        for t in range(3)
    ]
    line = jnp.concatenate(line + [cand_ref[...]], axis=1)
    send_ref[:, 0, :] = jnp.broadcast_to(line, (send_ref.shape[0], 4 * LANES))


def turn_kernel(u_ref, out_ref, wide):
    for k in range(HALF):
        rows = jnp.concatenate([u_ref[n, 8 * k : 8 * k + 8, :] for n in range(4)], axis=0)
        high = rows.astype(BF16).astype(F32)
        stack = jnp.concatenate([high, rows - high, high, jnp.zeros_like(high)], axis=0)
        turned = jnp.transpose(stack)
        wide[pl.ds(2 * k, BLOCK, stride=BLOCKS), :] = turned[:BLOCK]
        wide[pl.ds(2 * k + 1, BLOCK, stride=BLOCKS), :] = turned[BLOCK:]
    out_ref[...] = wide[...].astype(BF16)


def strain_kernel(rest_ref, arrived_ref, cand_ref, strain_ref):
    devs = arrived_ref.shape[0]
    points = strain_ref.shape[1]
    index = side_by_side(rest_ref[144:152, :points].astype(jnp.int32))
    refs = 8 * points
    partner = (index - NODES) >> 4
    other = jnp.where(iota((devs, refs), 0) == partner, 1.0, 0.0).astype(BF16)
    ghost = jnp.transpose(arrived_ref[:, 0, :])[:64]
    ghost = jnp.concatenate(split3(ghost), axis=0).astype(BF16)
    found = bdot(ghost, other)
    found = (found[:64] + found[64:128]) + found[128:]
    found = jnp.where(iota((64, refs), 0) % 16 == index % 16, found, 0.0)
    sums = [jnp.sum(found[16 * c : 16 * c + 16], axis=0, keepdims=True) for c in range(3)]
    nodal = by_node(jnp.concatenate(sums, axis=0), points) + rest_ref[160:184, :points]
    strain = jnp.concatenate(
        [
            jnp.sum(rest_ref[24 * c : 24 * c + 24, :points] * nodal, axis=0, keepdims=True)
            for c in range(6)
        ],
        axis=0,
    )
    strain_ref[...] = jnp.concatenate([strain, jnp.zeros((2, points), F32)], axis=0)

    assign = rest_ref[152:153, :points]
    plastic = assign >= 0.0
    flags = jnp.where(plastic, 1.0, 0.0)
    before = jnp.where(iota((points, points), 0) < iota((points, points), 1), 1.0, 0.0)
    rank = bdot(jnp.broadcast_to(flags, (8, points)).astype(BF16), before.astype(BF16))
    pick = jnp.where(plastic & (rank == iota((8, points), 0).astype(F32)), 1.0, 0.0)
    values = jnp.concatenate(
        [
            strain,
            assign + 1.0,
            jnp.zeros((LANES - 7, points), F32),
        ],
        axis=0,
    )
    chosen = dot_nt(pick, values)
    line = chosen[0:1]
    for slot in range(1, PLASTIC_CAP):
        line = line + pltpu.roll(chosen[slot : slot + 1], 8 * slot, 1)
    cand_ref[...] = line


def section_kernel(arrived_ref, send_ref):
    devs = arrived_ref.shape[0]
    groups = send_ref.shape[0] // 2
    total = jnp.sum(arrived_ref[:, 0, : 3 * LANES], axis=0, keepdims=True)
    cand = arrived_ref[:, 0, 3 * LANES :]
    turned = jnp.transpose(jnp.concatenate([cand] * (LANES // devs), axis=0))
    line = jnp.concatenate([turned[8 * n : 8 * n + 8, :devs] for n in range(PLASTIC_CAP)], axis=1)
    width = PLASTIC_CAP * devs
    target = line[6:7].astype(jnp.int32) - 1
    row = iota((64, width), 0)
    keep = ((target >> 7) == row // 8) & (row % 8 < 6)
    left = [
        jnp.where(keep, jnp.concatenate([part] * 8, axis=0), 0.0).astype(BF16)
        for part in split3(line)
    ]
    hot = jnp.where(iota((POINTS, width), 0) == (target & (POINTS - 1)), 1.0, 0.0).astype(BF16)
    dense = bdot_nt(jnp.concatenate(left, axis=0), hot)
    dense = (dense[:64] + dense[64:128]) + dense[128:]
    for h in range(groups):
        for core in range(2):
            for c in range(6):
                lanes = slice(c * LANES, (c + 1) * LANES)
                send_ref[2 * h + core, :, lanes] = dense[8 * h + c : 8 * h + c + 1]
            send_ref[2 * h + core, :, 6 * LANES :] = total


def coefficients(m, centre, step):
    m00, m01, m02, m03, m22, m23, m33, energy = m
    m11 = m00 + (step[1] * m02 + (centre[1] - centre[0]) * m01) / step[0]
    m12 = (step[2] * m03 + (centre[2] - centre[0]) * m02 + step[1] * m01) / step[0]
    m13 = (step[1] * (m22 - m11) + (centre[1] - centre[2]) * m12 + step[0] * m02) / step[2]
    products = [
        [m00, m01, m02, m03],
        [m01, m11, m12, m13],
        [m02, m12, m22, m23],
        [m03, m13, m23, m33],
    ]

    def gram(a, b):
        return products[a][b]

    def image(a, b):
        a, b = max(a, b), min(a, b)
        if b == 3:
            return energy
        value = step[b] * products[a][b + 1] + centre[b] * products[a][b]
        return value + step[b - 1] * products[a][b - 1] if b else value

    def inner(p, form):
        total = None
        for a in range(len(p)):
            for b in range(a, len(p)):
                term = p[a] * p[b] * form(a, b)
                if a != b:
                    term = 2.0 * term
                total = term if total is None else total + term
        return total

    def times(p):
        out = [jnp.zeros_like(p[0]) for _ in range(len(p) + 1)]
        for b, v in enumerate(p):
            out[b + 1] = out[b + 1] + step[b] * v
            out[b] = out[b] + centre[b] * v
            if b:
                out[b - 1] = out[b - 1] + step[b - 1] * v
        return out

    one = jnp.ones_like(m00)
    answer = []
    residual = [one]
    direction = [one]
    norm = m00
    for turn in range(4):
        alpha = norm / inner(direction, image)
        answer = answer + [jnp.zeros_like(one)]
        answer = [x + alpha * p for x, p in zip(answer, direction)]
        if turn < 3:
            stepped = times(direction)
            residual = residual + [jnp.zeros_like(one)]
            residual = [r - alpha * v for r, v in zip(residual, stepped)]
            later = inner(residual, gram)
            beta = later / norm
            direction = direction + [jnp.zeros_like(one)]
            direction = [r + beta * p for r, p in zip(residual, direction)]
            norm = later
    return answer


def final_kernel(
    scale,
    arrived_ref,
    strain_ref,
    assign_ref,
    elastic_ref,
    basis_ref,
    u_ref,
    stress_ref,
    out_ref,
):
    groups = arrived_ref.shape[0] // 2
    points = strain_ref.shape[1]
    mine = lax.axis_index("group")
    centre = [basis_ref[n : n + 1, :] for n in range(3)]
    step = [basis_ref[n + 3 : n + 4, :] for n in range(3)]
    both = jnp.sum(arrived_ref[:, 0, : 6 * LANES], axis=0, keepdims=True)
    field = [both[:, c * LANES : (c + 1) * LANES] for c in range(6)]
    field = jnp.concatenate(field + [jnp.zeros((2, LANES), F32)], axis=0)

    def unfold(lines):
        tiles = []
        for t in range(3):
            tile = lines[:, t * LANES : (t + 1) * LANES]
            low = iota(tile.shape, 1) < 64
            tiles.append(jnp.where(low, tile, 0.0))
            tiles.append(jnp.where(low, pltpu.roll(tile, 64, 1), 0.0))
        blank = jnp.zeros((2, LANES), F32)
        return [
            jnp.concatenate([v[h : h + 1] for v in tiles] + [blank], axis=0)
            for h in range(lines.shape[0])
        ]

    lane = iota((8, LANES), 1)
    diagonal = (iota((64, LANES), 0) // 8) == (iota((64, LANES), 1) % 64) // 8

    def tall(x):
        return jnp.concatenate([x] * 8, axis=0)

    def opened(moments):
        high, middle, low = split3(moments + pltpu.roll(moments, 64, 1))
        first = jnp.where(diagonal, tall(jnp.where(lane < 64, high, middle)), 0.0).astype(BF16)
        second = jnp.where(diagonal, tall(jnp.where(lane < 64, high, low)), 0.0).astype(BF16)
        return jnp.concatenate([first, first, second], axis=1)

    def meeting(x):
        high, middle, low = (tall(part) for part in split3(x))
        parts = [high, high, middle, middle, low, high]
        return jnp.concatenate(parts, axis=0).astype(BF16)

    strain = strain_ref[...]
    padded = jnp.concatenate([strain, jnp.zeros((8, LANES - points), F32)], axis=1)
    assign = jnp.concatenate(
        [assign_ref[...], jnp.full((1, LANES - points), -1, jnp.int32)], axis=1
    )
    halves = arrived_ref[:, 0, 6 * LANES :]
    whole = [halves[2 * h : 2 * h + 1] + halves[2 * h + 1 : 2 * h + 2] for h in range(groups)]
    every = unfold(jnp.concatenate(whole, axis=0))
    own = jnp.zeros((8, LANES), F32)
    for h in range(groups):
        own = own + jnp.where(mine == h, every[h], 0.0)
    forces = bdot(opened(own), meeting(field))
    every = jnp.concatenate([opened(v) for v in every], axis=0)
    products = bdot(every, meeting(padded))
    group_of = assign >> 7
    local = jnp.zeros((64, LANES), F32)
    for h in range(groups):
        local = local + jnp.where(group_of == h, products[64 * h : 64 * h + 64], 0.0)

    m = []
    for n in range(8):
        first = jnp.sum(forces[8 * n : 8 * n + 8] * field, axis=0, keepdims=True)
        second = jnp.sum(local[8 * n : 8 * n + 8] * padded, axis=0, keepdims=True)
        m.append(jnp.concatenate([first, second], axis=0))
    answer = coefficients(m, centre, step)

    extra = jnp.zeros((8, LANES), F32)
    for n in range(4):
        extra = extra + answer[n][1:2] * local[8 * n : 8 * n + 8]
    elastic_stress = dot(elastic_ref[...], strain[:6])
    plastic = assign_ref[...] >= 0
    stress_ref[...] = elastic_stress + jnp.where(plastic, extra[:6, :points], 0.0)

    right = jnp.concatenate([(scale * answer[n][0:1]) * field for n in range(4)], axis=0)
    high = right.astype(BF16).astype(F32)
    right = jnp.concatenate([high, high, right - high, jnp.zeros_like(high)], axis=0).astype(BF16)
    for part in range(6):
        rows = slice(512 * part, 512 * part + 512)
        out_ref[rows, :] = bdot(u_ref[rows, :], right)


def call(kernel, outs, *args, scratch=(), own_copies=0, cost=None):
    vmem = pl.BlockSpec(memory_space=pltpu.VMEM)
    many = isinstance(outs, list)
    out_specs = [vmem] * len(outs) if many else vmem
    scratch = list(scratch)
    if own_copies:
        scratch += [pltpu.VMEM(x.shape, x.dtype) for x in args[:own_copies]]
        scratch += [pltpu.SemaphoreType.DMA((own_copies,))]
    spaces = [pl.BlockSpec(memory_space=pltpu.HBM)] * own_copies + [vmem] * len(args)
    limit = 60 if own_copies else 32
    return pl.pallas_call(
        kernel,
        out_shape=outs,
        in_specs=spaces[: len(args)],
        out_specs=out_specs,
        scratch_shapes=scratch,
        cost_estimate=cost,
        compiler_params=pltpu.CompilerParams(vmem_limit_bytes=limit * 1024 * 1024),
    )(*args)


def arr(*shape, dtype=F32):
    return jax.ShapeDtypeStruct(shape, dtype)


def shifted(x, by):
    devices = lax.axis_size("dev")
    return lax.ppermute(x, "dev", [(i, (i + by) % devices) for i in range(devices)])


def exchange(x, axis, members=None):
    return lax.all_to_all(
        x, axis, split_axis=0, concat_axis=0, tiled=True, axis_index_groups=members
    )


def local(
    displacement,
    connectivity,
    face_nodes,
    strain_map,
    assignment,
    phases,
    load_map,
    stiff_root,
    chain_map,
    bridge_map,
    elastic,
):
    groups = lax.axis_size("group")
    devs = lax.axis_size("dev")
    points = connectivity.shape[1]
    assign = assignment.reshape(1, -1)

    listed = jnp.transpose(face_nodes, (0, 2, 1))
    load = jnp.transpose(load_map, (0, 2, 1))
    labels = jnp.transpose(phases, (0, 2, 1))
    sources = [displacement, listed, load, labels, connectivity, strain_map, assign]
    sources += [stiff_root, chain_map, bridge_map]
    outgoing, rest = call(
        first_kernel,
        [arr(devs, 1, LANES), arr(264 + ROWS, LANES)],
        *sources,
        own_copies=len(sources),
    )
    arrived = exchange(outgoing, "dev")
    *weights, terms, strain_part, packed, edge = call(
        tables,
        [
            arr(3 * LANES, 2 * LANES, dtype=BF16),
            arr(3 * LANES, LANES, dtype=BF16),
            arr(9 * LANES, LANES, dtype=BF16),
            arr(8, LANES),
            arr(184, LANES),
            arr(ROWS, LANES),
            arr(QUARTER, LANES),
        ],
        rest,
    )
    near = [shifted(packed, 1), shifted(edge, 2), shifted(packed, -1), shifted(packed, -2)]
    cand, strain = call(
        strain_kernel,
        [arr(1, LANES), arr(8, points)],
        strain_part,
        arrived,
        cost=pl.CostEstimate(flops=2 * 10**10, bytes_accessed=0, transcendentals=0),
    )
    vectors, send = call(
        krylov_kernel,
        [arr(4, ROWS, LANES), arr(devs // 2, 1, 4 * LANES)],
        packed,
        *near,
        *weights,
        terms,
        cand,
    )
    same_core = [list(range(core, devs, 2)) for core in range(2)]
    same_chip = [
        [g * devs + chip + core for g in range(groups) for core in range(2)]
        for chip in range(0, devs, 2)
    ]
    section = exchange(send, "dev", same_core)
    turned = call(
        turn_kernel,
        arr(BLOCK * BLOCKS, LANES, dtype=BF16),
        vectors,
        scratch=[pltpu.VMEM((BLOCK * BLOCKS, LANES), F32)],
    )
    across = call(section_kernel, arr(2 * groups, 1, 9 * LANES), section)
    gathered = exchange(across, ("group", "dev"), same_chip)
    scale = math.sqrt(BLOCK * devs * BLOCKS)
    stress, fluctuation = call(
        lambda *refs: final_kernel(scale, *refs),
        [arr(6, points), arr(BLOCK * BLOCKS, POINTS)],
        gathered,
        strain,
        assign,
        elastic,
        terms,
        turned,
    )
    return stress, fluctuation.reshape(1, BLOCK, BLOCKS, POINTS)


def solution(mesh):
    in_specs = (
        P(None, ("group", "dev")),
        P(None, ("group", "dev")),
        P(("group", "dev"), None, None),
        P(None, None, ("group", "dev")),
        P(("group", "dev")),
        P("group", None, "dev"),
        P(None, None, "dev"),
        P(),
        P(),
        P(),
        P(),
    )
    out_specs = (P(None, ("group", "dev")), P("group", None, "dev", None))
    return jax.shard_map(local, mesh=mesh, in_specs=in_specs, out_specs=out_specs, check_vma=False)
```
